32 devices in a mesh: fsdp: 16 (over z, x, core), tp: 2 (over y).
Axes of the slice: x: 2, y: 2, z: 4, core: 2. Of those that a mesh axis runs over, the one named last changes fastest.
Arguments:
- block_input: bfloat16 [8192, 1024], P(('fsdp', 'tp')), may hold values from -6 to 6
- segment_ids: int32 [8192], P('fsdp'), may hold values from 0 to 2, as said below
- output_cotangent: bfloat16 [8192, 1024], P(('fsdp', 'tp')), may hold values from -6 to 6
- input_gain: float32 [1024], replicated, may hold values from 0.5 to 1.5
- inner_weight: bfloat16 [1024, 2, 1536], P('fsdp', None, 'tp'), may hold values from -0.1875 to 0.1875
- timestep_weight: bfloat16 [1024, 24], P('fsdp', 'tp'), may hold values from -0.09375 to 0.09375
- state_weight: bfloat16 [1024, 256], P('fsdp'), may hold values from -0.1875 to 0.1875
- query_weight: bfloat16 [1024, 512], P('fsdp', 'tp'), may hold values from -0.1875 to 0.1875
- keyvalue_matrix: bfloat16 [1024, 256], P('fsdp'), may hold values from -0.1875 to 0.1875
- conv_kernel: float32 [4, 1792], replicated, may hold values from -3 to 3
- conv_offset: float32 [1792], replicated, may hold values from -1.5 to 1.5
- timestep_bias: float32 [24], replicated, may hold values from -7 to -2.5
- decay_log: float32 [24], replicated, may hold values from 0 to 1.5
- skip_scale: float32 [24], replicated, may hold values from 0.5 to 1.5
- gated_gain: float32 [1536], replicated, may hold values from 0.5 to 1.5
- mamba_down: bfloat16 [1536, 1024], P('tp', 'fsdp'), may hold values from -0.15625 to 0.15625
- attention_down: bfloat16 [512, 1024], P('tp', 'fsdp'), may hold values from -1 to 1
- middle_gain: float32 [1024], replicated, may hold values from 0.5 to 1.5
- gateup_weight: bfloat16 [1024, 2, 2048], P('fsdp', None, 'tp'), may hold values from -0.1875 to 0.1875
- down_weight: bfloat16 [2048, 1024], P('tp', 'fsdp'), may hold values from -0.125 to 0.125
Outputs:
- block_output: float32 [8192, 1024], P(('fsdp', 'tp'))
- input_grad: float32 [8192, 1024], P(('fsdp', 'tp'))
- input_gain_grad: float32 [1024], replicated
- inner_weight_grad: float32 [1024, 2, 1536], P('fsdp', None, 'tp')
- timestep_weight_grad: float32 [1024, 24], P('fsdp', 'tp')
- state_weight_grad: float32 [1024, 256], P('fsdp')
- query_weight_grad: float32 [1024, 512], P('fsdp', 'tp')
- keyvalue_weight_grad: float32 [1024, 256], P('fsdp')
- conv_kernel_grad: float32 [4, 1792], replicated
- conv_offset_grad: float32 [1792], replicated
- timestep_bias_grad: float32 [24], replicated
- decay_log_grad: float32 [24], replicated
- skip_scale_grad: float32 [24], replicated
- gated_gain_grad: float32 [1536], replicated
- mamba_down_grad: float32 [1536, 1024], P('tp', 'fsdp')
- attention_down_grad: float32 [512, 1024], P('tp', 'fsdp')
- middle_gain_grad: float32 [1024], replicated
- gateup_weight_grad: float32 [1024, 2, 2048], P('fsdp', None, 'tp')
- down_weight_grad: float32 [2048, 1024], P('tp', 'fsdp')
The draws below stay inside these ranges and needn't reach their ends.
Inputs may be any that keep to these rules, and one draw needn't show every extreme that they name: `segment_ids`: in each aligned block of 512 tokens the ids never fall, start at 0 and end at 2; the run of id 1 begins within the block's first 256 tokens and ends within its last 256.
All inputs are finite; a program needn't handle non-finite values.
Results may differ from the reference program's by a relative error of at most 0.019.
Values may be sent and summed in bfloat16 or wider, within the bound.
No kernel may reach another device: no remote copies, remote signals or barrier semaphores. Data moves between devices by JAX's collectives and lax.ppermute only.
A program may use at most 192 MiB of HBM per device.

```python
import math
import jax
import jax.numpy as jnp
from jax import lax

MODEL_WIDTH = 1024
HM = 24
NS = 128
KERNEL = 4
QUERY_HEADS = 8
KEYVALUE_HEADS = 2
HEAD_SIZE = 64
FF = 2048
SCAN_BLOCK = 256
QUERY_BLOCK = 512
TOK_DEV = 256
DS = 1536
GROUP = 512
TOKENS = 8192


def draw_segment_ids(key, part):
    key = jax.random.fold_in(key, 11)
    group_count = TOKENS // GROUP
    first_key, second_key = jax.random.split(key)
    opening = jax.random.randint(first_key, (group_count, 1), 1, TOK_DEV)
    closing = jax.random.randint(second_key, (group_count, 1), GROUP - TOK_DEV + 1, GROUP)
    places = jnp.arange(GROUP, dtype=jnp.int32)[None, :]
    labels = (places >= opening).astype(jnp.int32) + (places >= closing).astype(jnp.int32)
    return labels.reshape(TOKENS)


def shard_levels(rng, extent, cuts, low, top_value):
    def one(axis_at, blocks):
        heights = jax.random.uniform(jax.random.fold_in(jax.random.fold_in(rng, 6), axis_at), (blocks,), jnp.float32, low / len(cuts), top_value / len(cuts))
        return jnp.repeat(jnp.exp(heights), extent[axis_at] // blocks).reshape((-1,) + (1,) * (len(extent) - axis_at - 1))

    loudness = one(*cuts[0])
    for cut in cuts[1:]:
        loudness = loudness * one(*cut)
    return loudness


def noise(own_key, extent, scale, limit, cuts=(), kind=jnp.bfloat16):
    factor_of = shard_levels(own_key, extent, cuts, -0.22, 0.18) if cuts else 1.0
    values = jax.random.normal(own_key, extent, jnp.float32) * scale * factor_of
    return jnp.minimum(jnp.maximum(values, -limit), limit).astype(kind)


def setup_inputs(seed: int = 0) -> dict:
    arg_keys = jax.random.split(jax.random.key(seed), 21)
    block_input = noise(arg_keys[0], (TOKENS, MODEL_WIDTH), 1.0, 6.0, ((0, 32),))
    segment_ids = draw_segment_ids(jax.random.fold_in(arg_keys[20], 71), 0)
    output_cotangent = noise(arg_keys[2], (TOKENS, MODEL_WIDTH), 1.0, 6.0, ((0, 32),))
    input_gain = jnp.clip(1.0 + 0.1 * jax.random.normal(arg_keys[3], (MODEL_WIDTH,), jnp.float32), 0.5, 1.5)
    inner_weight = noise(arg_keys[4], (MODEL_WIDTH, 2, DS), MODEL_WIDTH ** -0.5, 0.1875, ((0, 16), (2, 2)))
    timestep_weight = noise(arg_keys[5], (MODEL_WIDTH, HM), (4 * MODEL_WIDTH) ** -0.5, 0.09375, ((0, 16), (1, 2)))
    state_weight = noise(arg_keys[6], (MODEL_WIDTH, 2 * NS), MODEL_WIDTH ** -0.5, 0.1875, ((0, 16),))
    query_weight = noise(arg_keys[7], (MODEL_WIDTH, QUERY_HEADS * HEAD_SIZE), MODEL_WIDTH ** -0.5, 0.1875, ((0, 16), (1, 2)))
    keyvalue_matrix = noise(arg_keys[8], (MODEL_WIDTH, 2 * KEYVALUE_HEADS * HEAD_SIZE), MODEL_WIDTH ** -0.5, 0.1875, ((0, 16),))
    conv_kernel = noise(arg_keys[9], (KERNEL, DS + 2 * NS), KERNEL ** -0.5, 3.0, (), jnp.float32)
    conv_offset = noise(arg_keys[10], (DS + 2 * NS,), 0.3, 1.5, (), jnp.float32)
    timestep_bias = jnp.clip(jax.random.uniform(arg_keys[11], (HM,), jnp.float32, -7.0, -2.5), -7.0, -2.5)
    decay_log = jnp.clip(jax.random.uniform(arg_keys[12], (HM,), jnp.float32, 0.0, 1.5), 0.0, 1.5)
    skip_scale = jnp.clip(jax.random.uniform(arg_keys[13], (HM,), jnp.float32, 0.5, 1.5), 0.5, 1.5)
    gated_gain = jnp.clip(1.0 + 0.1 * jax.random.normal(arg_keys[14], (DS,), jnp.float32), 0.5, 1.5)
    mamba_down = noise(arg_keys[15], (DS, MODEL_WIDTH), DS ** -0.5, 0.15625, ((0, 2), (1, 16)))
    attention_down = noise(arg_keys[16], (QUERY_HEADS * HEAD_SIZE, MODEL_WIDTH), (QUERY_HEADS * HEAD_SIZE // 16) ** -0.5, 1.0, ((0, 2), (1, 16)))
    middle_gain = jnp.clip(1.0 + 0.1 * jax.random.normal(arg_keys[17], (MODEL_WIDTH,), jnp.float32), 0.5, 1.5)
    gateup_weight = noise(arg_keys[18], (MODEL_WIDTH, 2, FF), MODEL_WIDTH ** -0.5, 0.1875, ((0, 16), (2, 2)))
    down_weight = noise(arg_keys[19], (FF, MODEL_WIDTH), FF ** -0.5, 0.125, ((0, 2), (1, 16)))
    return {"block_input": block_input, "segment_ids": segment_ids, "output_cotangent": output_cotangent, "input_gain": input_gain, "inner_weight": inner_weight, "timestep_weight": timestep_weight, "state_weight": state_weight, "query_weight": query_weight, "keyvalue_matrix": keyvalue_matrix, "conv_kernel": conv_kernel, "conv_offset": conv_offset, "timestep_bias": timestep_bias, "decay_log": decay_log, "skip_scale": skip_scale, "gated_gain": gated_gain, "mamba_down": mamba_down, "attention_down": attention_down, "middle_gain": middle_gain, "gateup_weight": gateup_weight, "down_weight": down_weight}


EPSILON = 1e-05
MASKED_SCORE = -1e+30
ROPE_BASE = 100000000000.0
PRECISE = lax.Precision.HIGHEST

@jax.custom_vjp
def lowered_part(v):
    return lax.optimization_barrier(v.astype(jnp.bfloat16)).astype(jnp.float32)

@jax.custom_vjp
def low_back(v):
    return v

def low_keep(v):
    return (lowered_part(v), None)

def low_pass(kept, grad):
    return (grad,)

def back_keep(v):
    return (v, None)

def back_low(kept, grad):
    return (lowered_part(grad),)
lowered_part.defvjp(low_keep, low_pass)
low_back.defvjp(back_keep, back_low)

def inverse_rms(values):
    return lax.rsqrt(lax.optimization_barrier(jnp.mean(values * values, -1, keepdims=True)) + EPSILON)

def causal_conv(signal, kernel, offset, segment):
    length_tokens = signal.shape[0]
    result = offset[None, :] + kernel[0][None, :] * signal
    for distance in range(1, kernel.shape[0]):
        shifted = jnp.concatenate([jnp.zeros((distance, signal.shape[1]), signal.dtype), signal[:length_tokens - distance]], 0)
        earlier = jnp.concatenate([jnp.full((distance,), -1, jnp.int32), segment[:length_tokens - distance]], 0)
        retained = (earlier == segment).astype(signal.dtype)
        result = result + kernel[distance][None, :] * shifted * retained[:, None]
    return result

def state_scan(values, timesteps, decays, key_row_block, query_rows, segment, block):
    total, head_count, channels = values.shape
    count = total // block
    states = key_row_block.shape[1]
    lower = jnp.arange(block)[:, None] >= jnp.arange(block)[None, :]

    def advance(carry, pieces):
        memory, previous = carry
        value_block, step_block, key_block, query_block, labels = pieces
        rates = step_block * decays[None, :]
        cumulative = jnp.cumsum(rates, 0)
        linked = jnp.logical_and(labels[:, None] == labels[None, :], lower)
        gaps = cumulative[:, None, :] - cumulative[None, :, :]
        weights = jnp.exp(jnp.where(linked[:, :, None], gaps, 0.0)) * linked[:, :, None].astype(jnp.float32)
        intersections = jnp.dot(query_block, key_block.T, precision=PRECISE)
        scaled = value_block * step_block[:, :, None]
        within = jnp.einsum('tsh,shp->thp', intersections[:, :, None] * weights, scaled, precision=PRECISE)
        carried = jnp.exp(cumulative) * (labels == previous).astype(jnp.float32)[:, None]
        across = jnp.einsum('tn,hpn->thp', query_block, memory, precision=PRECISE) * carried[:, :, None]
        final = cumulative[block - 1]
        ending = labels[block - 1]
        toward = jnp.exp(final[None, :] - cumulative) * (labels == ending).astype(jnp.float32)[:, None]
        fresh = jnp.einsum('sh,shp,sn->hpn', toward, scaled, key_block, precision=PRECISE)
        kept = jnp.exp(final) * (ending == previous).astype(jnp.float32)
        memory = memory * kept[:, None, None] + fresh
        return ((memory, ending), within + across)
    start = (jnp.zeros((head_count, channels, states), jnp.float32), jnp.array(-1, jnp.int32))
    pieces = (values.reshape(count, block, head_count, channels), timesteps.reshape(count, block, head_count), key_row_block.reshape(count, block, states), query_rows.reshape(count, block, states), segment.reshape(count, block))
    folded, outputs = lax.scan(jax.checkpoint(advance), start, pieces)
    return outputs.reshape(total, head_count, channels)

def mixer_core(values, raw_steps, step_bias, decay_log, skip_scale, key_row_block, query_rows, segment, block):
    timesteps = jax.nn.softplus(raw_steps + step_bias[None, :])
    decays = -jnp.exp(decay_log)
    head_count = timesteps.shape[1]
    shaped = values.reshape(values.shape[0], head_count, -1)
    output = state_scan(shaped, timesteps, decays, key_row_block, query_rows, segment, block)
    return (output + skip_scale[None, :, None] * shaped).reshape(values.shape)

def rotary_apply(vectors, direction):
    length_tokens, head_count, columns = vectors.shape
    halfway = columns // 2
    frequency = jnp.exp(jnp.arange(halfway, dtype=jnp.float32) * (-2.0 * math.log(ROPE_BASE) / columns))
    angles = jnp.arange(length_tokens, dtype=jnp.float32)[:, None] * frequency[None, :] * direction
    cosine = jnp.cos(angles)[:, None, :]
    sinusoid = jnp.sin(angles)[:, None, :]
    former = vectors[..., :halfway]
    latter = vectors[..., halfway:]
    return jnp.concatenate([former * cosine - latter * sinusoid, latter * cosine + former * sinusoid], -1)

def attention_mask(segment, start, rowcount):
    positions = start + jnp.arange(rowcount, dtype=jnp.int32)
    columns = jnp.arange(segment.shape[0], dtype=jnp.int32)
    labels = lax.dynamic_slice_in_dim(segment, start, rowcount)
    return jnp.logical_and(columns[None, :] <= positions[:, None], segment[None, :] == labels[:, None])

def attention(queries, key_row_block, value_row_block, segment):
    length_tokens, head_count, columns = queries.shape
    block_count = length_tokens // QUERY_BLOCK
    scaling = 1.0 / math.sqrt(columns)
    query_blocks = queries.reshape(block_count, QUERY_BLOCK, head_count, columns)
    block_starts = jnp.arange(block_count, dtype=jnp.int32) * QUERY_BLOCK

    def one_block(pieces):
        query_block, start = pieces
        scores = low_back(jnp.einsum('qhd,khd->hqk', query_block, key_row_block, precision=PRECISE) * scaling)
        allowed = attention_mask(segment, start, QUERY_BLOCK)
        masked = jnp.where(allowed[None], scores, MASKED_SCORE)
        highest = lax.optimization_barrier(jnp.max(masked, -1, keepdims=True))
        weights = jnp.exp(masked - highest)
        probs = weights / lax.optimization_barrier(jnp.sum(weights, -1, keepdims=True))
        return jnp.einsum('hqk,khd->qhd', lowered_part(probs), value_row_block, precision=PRECISE)
    result = lax.map(jax.checkpoint(one_block), (query_blocks, block_starts))
    return result.reshape(length_tokens, head_count, columns)

def layer(params, residual, segment):
    input_gain, inner_weight, timestep_weight, state_weight, query_weight, keyvalue_matrix, conv_kernel, conv_offset, timestep_bias, decay_log, skip_scale, gated_gain, mamba_down, attention_down, middle_gain, gateup_weight, down_weight = params
    length_tokens = residual.shape[0]
    normed = lowered_part(residual * inverse_rms(residual) * input_gain)
    inner = low_back(jnp.einsum('gd,dkc->gkc', normed, inner_weight, precision=PRECISE))
    raw_steps = low_back(jnp.dot(normed, timestep_weight, precision=PRECISE))
    state_proj = low_back(jnp.dot(normed, state_weight, precision=PRECISE))
    query_proj = low_back(jnp.dot(normed, query_weight, precision=PRECISE))
    keyvalue_projected = low_back(jnp.dot(normed, keyvalue_matrix, precision=PRECISE))
    gate_half = inner[:, 0]
    ssm_width = gate_half.shape[1]
    convolved = jax.nn.silu(causal_conv(jnp.concatenate([inner[:, 1], state_proj], 1), conv_kernel, conv_offset, segment))
    conv_values = lowered_part(convolved[:, :ssm_width])
    conv_states = lowered_part(convolved[:, ssm_width:])
    state_dim = conv_states.shape[1] // 2
    scanned = mixer_core(conv_values, raw_steps, timestep_bias, decay_log, skip_scale, conv_states[:, :state_dim], conv_states[:, state_dim:], segment, SCAN_BLOCK)
    gated = scanned * jax.nn.silu(gate_half)
    squares = low_back(lax.optimization_barrier(jnp.sum(gated * gated, -1)))
    factor = lowered_part(lax.rsqrt(squares / ssm_width + EPSILON))
    mamba_part = low_back(jnp.dot(lowered_part(gated * gated_gain), mamba_down, precision=PRECISE))
    queries = lowered_part(rotary_apply(query_proj.reshape(length_tokens, QUERY_HEADS, HEAD_SIZE), 1.0))
    key_row_block = lowered_part(rotary_apply(keyvalue_projected[:, :KEYVALUE_HEADS * HEAD_SIZE].reshape(length_tokens, KEYVALUE_HEADS, HEAD_SIZE), 1.0))
    value_row_block = lowered_part(keyvalue_projected[:, KEYVALUE_HEADS * HEAD_SIZE:].reshape(length_tokens, KEYVALUE_HEADS, HEAD_SIZE))
    key_row_block = jnp.repeat(key_row_block, QUERY_HEADS // KEYVALUE_HEADS, axis=1)
    value_row_block = jnp.repeat(value_row_block, QUERY_HEADS // KEYVALUE_HEADS, axis=1)
    attended = attention(queries, key_row_block, value_row_block, segment)
    attended = lowered_part(low_back(attended)).reshape(length_tokens, QUERY_HEADS * HEAD_SIZE)
    attention_part = jnp.dot(attended, attention_down, precision=PRECISE)
    mixed = low_back(factor[:, None] * mamba_part + attention_part)
    middle = residual + mixed
    hidden_in = lowered_part(middle * inverse_rms(middle) * middle_gain)
    gateup = low_back(jnp.einsum('gd,dkf->gkf', hidden_in, gateup_weight, precision=PRECISE))
    activated = lowered_part(jax.nn.silu(gateup[:, 0]) * gateup[:, 1])
    feedforward = low_back(jnp.dot(activated, down_weight, precision=PRECISE))
    return middle + feedforward

def reference(block_input, segment_ids, output_cotangent, input_gain, inner_weight, timestep_weight, state_weight, query_weight, keyvalue_matrix, conv_kernel, conv_offset, timestep_bias, decay_log, skip_scale, gated_gain, mamba_down, attention_down, middle_gain, gateup_weight, down_weight):
    params = tuple((parameter.astype(jnp.float32) for parameter in (input_gain, inner_weight, timestep_weight, state_weight, query_weight, keyvalue_matrix, conv_kernel, conv_offset, timestep_bias, decay_log, skip_scale, gated_gain, mamba_down, attention_down, middle_gain, gateup_weight, down_weight)))
    group_count = TOKENS // GROUP
    inputs = block_input.astype(jnp.float32).reshape(group_count, GROUP, MODEL_WIDTH)
    labels = segment_ids.reshape(group_count, GROUP)
    cotangents = output_cotangent.astype(jnp.float32).reshape(group_count, GROUP, MODEL_WIDTH)

    def one_group(totals, pieces):
        residual_group, label_group, cotangent_group = pieces

        def forward(weights, residual):
            return layer(weights, residual, label_group)
        output, pullback = jax.vjp(forward, params, residual_group)
        weight_grads, input_grads = pullback(cotangent_group)
        totals = jax.tree.map(jnp.add, totals, weight_grads)
        return (totals, (output, input_grads))
    zeros = jax.tree.map(jnp.zeros_like, params)
    totals, (outputs, input_grads) = lax.scan(one_group, zeros, (inputs, labels, cotangents))
    return (outputs.reshape(TOKENS, MODEL_WIDTH), input_grads.reshape(TOKENS, MODEL_WIDTH), totals[0], totals[1], totals[2], totals[3], totals[4], totals[5], totals[6], totals[7], totals[8], totals[9], totals[10], totals[11], totals[12], totals[13], totals[14], totals[15], totals[16])
```

```python
import math

import jax
import jax.numpy as jnp
from jax import lax
from jax.experimental import pallas as pl
from jax.experimental.pallas import tpu as pltpu
from jax.sharding import PartitionSpec as P

QUERY_HEADS = 8
KEYVALUE_HEADS = 2
HEAD_SIZE = 64
SCAN_BLOCK = 256
QUERY_BLOCK = 512


EPSILON = 1e-05
MASKED_SCORE = -1e30
ROPE_BASE = 100000000000.0
PRECISE = lax.Precision.HIGHEST


def inverse_rms(values):
    return lax.rsqrt(jnp.mean(values * values, -1, keepdims=True) + EPSILON)


def contract_rows(left, right):
    return lax.dot_general(
        left, right, (((0,), (0,)), ((), ())), preferred_element_type=jnp.float32
    )


def contract_cols(left, right):
    return lax.dot_general(
        left, right, (((1,), (1,)), ((), ())), preferred_element_type=jnp.float32
    )


def causal_conv(signal, kernel, offset, segment):
    length_tokens = signal.shape[0]
    result = offset[None, :] + kernel[0][None, :] * signal
    for distance in range(1, kernel.shape[0]):
        shifted = jnp.concatenate(
            [
                jnp.zeros((distance, signal.shape[1]), signal.dtype),
                signal[: length_tokens - distance],
            ],
            0,
        )
        earlier = jnp.concatenate(
            [jnp.full((distance,), -1, jnp.int32), segment[: length_tokens - distance]], 0
        )
        retained = (earlier == segment).astype(signal.dtype)
        result = result + kernel[distance][None, :] * shifted * retained[:, None]
    return result


def state_scan(values, timesteps, decays, key_row_block, query_rows, segment, block):
    total, head_count, channels = values.shape
    count = total // block
    states = key_row_block.shape[1]
    lower = jnp.arange(block)[:, None] >= jnp.arange(block)[None, :]

    def advance(carry, pieces):
        memory, previous = carry
        value_block, step_block, key_block, query_block, labels = pieces
        rates = step_block * decays[None, :]
        cumulative = jnp.cumsum(rates, 0)
        linked = jnp.logical_and(labels[:, None] == labels[None, :], lower)
        gaps = cumulative[:, None, :] - cumulative[None, :, :]
        weights = jnp.exp(jnp.where(linked[:, :, None], gaps, 0.0)) * linked[:, :, None].astype(
            jnp.float32
        )
        intersections = jnp.dot(query_block, key_block.T, precision=PRECISE)
        scaled = value_block * step_block[:, :, None]
        within = jnp.einsum(
            "tsh,shp->thp", intersections[:, :, None] * weights, scaled, precision=PRECISE
        )
        carried = jnp.exp(cumulative) * (labels == previous).astype(jnp.float32)[:, None]
        across = (
            jnp.einsum("tn,hpn->thp", query_block, memory, precision=PRECISE) * carried[:, :, None]
        )
        final = cumulative[block - 1]
        ending = labels[block - 1]
        toward = (
            jnp.exp(final[None, :] - cumulative) * (labels == ending).astype(jnp.float32)[:, None]
        )
        fresh = jnp.einsum("sh,shp,sn->hpn", toward, scaled, key_block, precision=PRECISE)
        kept = jnp.exp(final) * (ending == previous).astype(jnp.float32)
        memory = memory * kept[:, None, None] + fresh
        return ((memory, ending), within + across)

    start = (jnp.zeros((head_count, channels, states), jnp.float32), jnp.array(-1, jnp.int32))
    pieces = (
        values.reshape(count, block, head_count, channels),
        timesteps.reshape(count, block, head_count),
        key_row_block.reshape(count, block, states),
        query_rows.reshape(count, block, states),
        segment.reshape(count, block),
    )
    folded, outputs = lax.scan(jax.checkpoint(advance), start, pieces)
    return outputs.reshape(total, head_count, channels)


def mixer_core(
    values, raw_steps, step_bias, decay_log, skip_scale, key_row_block, query_rows, segment, block
):
    timesteps = jax.nn.softplus(raw_steps + step_bias[None, :])
    decays = -jnp.exp(decay_log)
    head_count = timesteps.shape[1]
    shaped = values.reshape(values.shape[0], head_count, -1)
    output = state_scan(shaped, timesteps, decays, key_row_block, query_rows, segment, block)
    return (output + skip_scale[None, :, None] * shaped).reshape(values.shape)


def rotary_apply(vectors, direction):
    length_tokens, head_count, columns = vectors.shape
    halfway = columns // 2
    frequency = jnp.exp(
        jnp.arange(halfway, dtype=jnp.float32) * (-2.0 * math.log(ROPE_BASE) / columns)
    )
    angles = jnp.arange(length_tokens, dtype=jnp.float32)[:, None] * frequency[None, :] * direction
    cosine = jnp.cos(angles)[:, None, :]
    sinusoid = jnp.sin(angles)[:, None, :]
    former = vectors[..., :halfway]
    latter = vectors[..., halfway:]
    return jnp.concatenate(
        [former * cosine - latter * sinusoid, latter * cosine + former * sinusoid], -1
    )


def attention_mask(segment, start, rowcount):
    positions = start + jnp.arange(rowcount, dtype=jnp.int32)
    columns = jnp.arange(segment.shape[0], dtype=jnp.int32)
    labels = lax.dynamic_slice_in_dim(segment, start, rowcount)
    return jnp.logical_and(
        columns[None, :] <= positions[:, None], segment[None, :] == labels[:, None]
    )


def general_body(
    block_input,
    segment_ids,
    output_cotangent,
    input_gain,
    inner_weight,
    timestep_weight,
    state_weight,
    query_weight,
    keyvalue_matrix,
    conv_kernel,
    conv_offset,
    timestep_bias,
    decay_log,
    skip_scale,
    gated_gain,
    mamba_down,
    attention_down,
    middle_gain,
    gateup_weight,
    down_weight,
):
    tensor_parallel_rank = lax.axis_index("tp")
    residual = block_input.astype(jnp.float32)
    first_rms = inverse_rms(residual)
    normed = lax.all_gather(
        (residual * first_rms * input_gain).astype(jnp.bfloat16), "tp", axis=0, tiled=True
    )
    (
        inner_full,
        timestep_full,
        state_full,
        query_full,
        keyvalue_full,
        mamba_full,
        attention_full,
        gateup_full,
        down_full,
    ) = (
        lax.all_gather(inner_weight, "fsdp", axis=0, tiled=True),
        lax.all_gather(timestep_weight, "fsdp", axis=0, tiled=True),
        lax.all_gather(state_weight, "fsdp", axis=0, tiled=True),
        lax.all_gather(query_weight, "fsdp", axis=0, tiled=True),
        lax.all_gather(keyvalue_matrix, "fsdp", axis=0, tiled=True),
        lax.all_gather(mamba_down, "fsdp", axis=1, tiled=True),
        lax.all_gather(attention_down, "fsdp", axis=1, tiled=True),
        lax.all_gather(gateup_weight, "fsdp", axis=0, tiled=True),
        lax.all_gather(down_weight, "fsdp", axis=1, tiled=True),
    )
    length_tokens = normed.shape[0]
    local_heads = timestep_full.shape[1]
    local_width = inner_full.shape[2]
    ssm_width = gated_gain.shape[0]
    state_dim = state_full.shape[1] // 2
    query_head_count = query_full.shape[1] // HEAD_SIZE
    head_start = tensor_parallel_rank * local_heads
    width_start = tensor_parallel_rank * local_width
    inner = jnp.einsum("gd,dkc->gkc", normed, inner_full, preferred_element_type=jnp.float32)
    raw_steps = jnp.dot(normed, timestep_full, preferred_element_type=jnp.float32)
    state_proj = jnp.dot(normed, state_full, preferred_element_type=jnp.float32)
    query_proj = jnp.dot(normed, query_full, preferred_element_type=jnp.float32)
    keyvalue_projected = jnp.dot(normed, keyvalue_full, preferred_element_type=jnp.float32)
    gate_half = inner[:, 0]
    local_kernel = jnp.concatenate(
        [
            lax.dynamic_slice_in_dim(conv_kernel, width_start, local_width, 1),
            conv_kernel[:, ssm_width:],
        ],
        1,
    )
    local_offset = jnp.concatenate(
        [
            lax.dynamic_slice_in_dim(conv_offset, width_start, local_width, 0),
            conv_offset[ssm_width:],
        ],
        0,
    )
    local_bias = lax.dynamic_slice_in_dim(timestep_bias, head_start, local_heads, 0)
    local_decay = lax.dynamic_slice_in_dim(decay_log, head_start, local_heads, 0)
    local_skip = lax.dynamic_slice_in_dim(skip_scale, head_start, local_heads, 0)
    local_gain = lax.dynamic_slice_in_dim(gated_gain, width_start, local_width, 0)

    def convolve(signal, kernel, offset):
        return jax.nn.silu(causal_conv(signal, kernel, offset, segment_ids))

    convolved, conv_pullback = jax.vjp(
        convolve, jnp.concatenate([inner[:, 1], state_proj], 1), local_kernel, local_offset
    )
    conv_values = convolved[:, :local_width].astype(jnp.bfloat16)
    conv_states = convolved[:, local_width:].astype(jnp.bfloat16).astype(jnp.float32)

    def scan_heads(values, steps_in, bias_in, decay_in, skip_in, key_rows_in, query_rows_in):
        return mixer_core(
            values,
            steps_in,
            bias_in,
            decay_in,
            skip_in,
            key_rows_in,
            query_rows_in,
            segment_ids,
            SCAN_BLOCK,
        )

    scanned, scan_pullback = jax.vjp(
        scan_heads,
        conv_values.astype(jnp.float32),
        raw_steps,
        local_bias,
        local_decay,
        local_skip,
        conv_states[:, :state_dim],
        conv_states[:, state_dim:],
    )
    silu_gate = jax.nn.silu(gate_half)
    gated = scanned * silu_gate
    gated_low = (gated * local_gain).astype(jnp.bfloat16)
    mamba_partial = jnp.dot(gated_low, mamba_full, preferred_element_type=jnp.float32)
    queries = rotary_apply(
        query_proj.reshape(length_tokens, query_head_count, HEAD_SIZE), 1.0
    ).astype(jnp.bfloat16)
    key_gathered = rotary_apply(
        keyvalue_projected[:, : KEYVALUE_HEADS * HEAD_SIZE].reshape(
            length_tokens, KEYVALUE_HEADS, HEAD_SIZE
        ),
        1.0,
    ).astype(jnp.bfloat16)
    value_gathered = (
        keyvalue_projected[:, KEYVALUE_HEADS * HEAD_SIZE :]
        .reshape(length_tokens, KEYVALUE_HEADS, HEAD_SIZE)
        .astype(jnp.bfloat16)
    )
    owner_ranks = (
        tensor_parallel_rank * query_head_count + jnp.arange(query_head_count, dtype=jnp.int32)
    ) // (QUERY_HEADS // KEYVALUE_HEADS)
    choice_picker = (
        owner_ranks[:, None] == jnp.arange(KEYVALUE_HEADS, dtype=jnp.int32)[None, :]
    ).astype(jnp.bfloat16)
    key_row_block = jnp.einsum(
        "jh,ghd->gjd", choice_picker, key_gathered, preferred_element_type=jnp.float32
    ).astype(jnp.bfloat16)
    value_row_block = jnp.einsum(
        "jh,ghd->gjd", choice_picker, value_gathered, preferred_element_type=jnp.float32
    ).astype(jnp.bfloat16)
    scaling = 1.0 / math.sqrt(HEAD_SIZE)
    block_count = length_tokens // QUERY_BLOCK
    query_blocks = queries.reshape(block_count, QUERY_BLOCK, query_head_count, HEAD_SIZE)
    block_starts = jnp.arange(block_count, dtype=jnp.int32) * QUERY_BLOCK

    def block_scores(query_block, start):
        scores = (
            jnp.einsum(
                "qjd,kjd->jqk", query_block, key_row_block, preferred_element_type=jnp.float32
            )
            * scaling
        )
        allowed = attention_mask(segment_ids, start, QUERY_BLOCK)
        return jnp.where(allowed[None], scores, MASKED_SCORE)

    def forward_block(pieces):
        query_block, start = pieces
        masked = block_scores(query_block, start)
        highest = jnp.max(masked, -1, keepdims=True)
        weights = jnp.exp(masked - highest)
        totals = jnp.sum(weights, -1, keepdims=True)
        probs_low = (weights / totals).astype(jnp.bfloat16)
        result = jnp.einsum(
            "jqk,kjd->qjd", probs_low, value_row_block, preferred_element_type=jnp.float32
        )
        return (result, (highest + jnp.log(totals))[..., 0])

    attended, logsums = lax.map(forward_block, (query_blocks, block_starts))
    attended_low = attended.reshape(length_tokens, query_head_count * HEAD_SIZE).astype(
        jnp.bfloat16
    )
    attention_partial = jnp.dot(attended_low, attention_full, preferred_element_type=jnp.float32)
    square_local = jnp.sum(gated * gated, -1)
    mamba_rows, attention_rows, square_rows = (
        lax.psum_scatter(mamba_partial, "tp", scatter_dimension=0, tiled=True),
        lax.psum_scatter(attention_partial, "tp", scatter_dimension=0, tiled=True),
        lax.psum_scatter(square_local, "tp", scatter_dimension=0, tiled=True),
    )
    norm_factor = lax.rsqrt(square_rows / ssm_width + EPSILON)
    factor_low = norm_factor.astype(jnp.bfloat16)
    factor_own = lax.optimization_barrier(factor_low).astype(jnp.float32)
    middle = residual + (factor_own[:, None] * mamba_rows + attention_rows)
    middle_rms = inverse_rms(middle)
    hidden_in = lax.all_gather(
        (middle * middle_rms * middle_gain).astype(jnp.bfloat16), "tp", axis=0, tiled=True
    )
    gateup = jnp.einsum("gd,dkf->gkf", hidden_in, gateup_full, preferred_element_type=jnp.float32)
    gate_part = gateup[:, 0]
    up_part = gateup[:, 1]
    activated = (jax.nn.silu(gate_part) * up_part).astype(jnp.bfloat16)
    feedforward = lax.psum_scatter(
        jnp.dot(activated, down_full, preferred_element_type=jnp.float32).astype(jnp.bfloat16),
        "tp",
        scatter_dimension=0,
        tiled=True,
    ).astype(jnp.float32)
    block_output = middle + feedforward
    cotangent_all = lax.all_gather(output_cotangent, "tp", axis=0, tiled=True)
    grad_activated = contract_cols(cotangent_all, down_full)
    down_wgrad = contract_rows(activated, cotangent_all)
    gate_sigmoid = jax.nn.sigmoid(gate_part)
    grad_gate_part = (
        grad_activated * up_part * gate_sigmoid * (1.0 + gate_part * (1.0 - gate_sigmoid))
    )
    grad_up_part = grad_activated * jax.nn.silu(gate_part)
    grad_gateup = jnp.stack([grad_gate_part, grad_up_part], 1).astype(jnp.bfloat16)
    gateup_wgrad = jnp.einsum(
        "gd,gkf->dkf", hidden_in, grad_gateup, preferred_element_type=jnp.float32
    )
    grad_hidden = lax.psum_scatter(
        jnp.einsum("gkf,dkf->gd", grad_gateup, gateup_full, preferred_element_type=jnp.float32),
        "tp",
        scatter_dimension=0,
        tiled=True,
    )
    middle_normal = middle * middle_rms
    middle_gain_part = jnp.sum(grad_hidden * middle_normal, 0)
    middle_scaled = grad_hidden * middle_gain
    grad_middle = output_cotangent.astype(jnp.float32) + middle_rms * (
        middle_scaled - middle_normal * jnp.mean(middle_scaled * middle_normal, -1, keepdims=True)
    )
    mix_low = grad_middle.astype(jnp.bfloat16)
    mix_own = mix_low.astype(jnp.float32)
    grad_factor = jnp.sum(mix_own * mamba_rows, -1)
    grad_square = (grad_factor * -0.5 * norm_factor * norm_factor * norm_factor / ssm_width).astype(
        jnp.bfloat16
    )
    mix_all, factor_rows, square_rows_grad = (
        lax.all_gather(mix_low, "tp", axis=0, tiled=True),
        lax.all_gather(factor_low, "tp", axis=0, tiled=True),
        lax.all_gather(grad_square, "tp", axis=0, tiled=True),
    )
    grad_mamba = (factor_rows.astype(jnp.float32)[:, None] * mix_all.astype(jnp.float32)).astype(
        jnp.bfloat16
    )
    mamba_wgrad = contract_rows(gated_low, grad_mamba)
    grad_gated_low = contract_cols(grad_mamba, mamba_full)
    gain_grad = jnp.sum(grad_gated_low * gated, 0)
    grad_gated = (
        grad_gated_low * local_gain + 2.0 * gated * square_rows_grad.astype(jnp.float32)[:, None]
    )
    zsigmoid = jax.nn.sigmoid(gate_half)
    grad_scanned = grad_gated * silu_gate
    grad_gate = grad_gated * scanned * zsigmoid * (1.0 + gate_half * (1.0 - zsigmoid))
    grad_values, grad_steps, grad_bias, grad_decay, grad_skip, grad_keys_in, grad_queries_in = (
        scan_pullback(grad_scanned)
    )
    grad_signal, kernel_local, offset_local = conv_pullback(
        jnp.concatenate([grad_values, grad_keys_in, grad_queries_in], 1)
    )
    attention_wgrad = contract_rows(attended_low, mix_all)
    grad_attended = (
        contract_cols(mix_all, attention_full)
        .astype(jnp.bfloat16)
        .reshape(block_count, QUERY_BLOCK, query_head_count, HEAD_SIZE)
    )

    def backward_block(carry, pieces):
        key_grad, value_grad = carry
        query_block, grad_block, logsum_block, start = pieces
        masked = block_scores(query_block, start)
        probs = jnp.exp(masked - logsum_block[..., None])
        grad_probs = jnp.einsum(
            "qjd,kjd->jqk", grad_block, value_row_block, preferred_element_type=jnp.float32
        )
        inner_sum = jnp.sum(grad_probs * probs, -1, keepdims=True)
        grad_scores = (probs * (grad_probs - inner_sum)).astype(jnp.bfloat16)
        query_grad = (
            jnp.einsum(
                "jqk,kjd->qjd", grad_scores, key_row_block, preferred_element_type=jnp.float32
            )
            * scaling
        )
        key_grad = (
            key_grad
            + jnp.einsum(
                "jqk,qjd->kjd", grad_scores, query_block, preferred_element_type=jnp.float32
            )
            * scaling
        )
        value_grad = value_grad + jnp.einsum(
            "jqk,qjd->kjd",
            probs.astype(jnp.bfloat16),
            grad_block,
            preferred_element_type=jnp.float32,
        )
        return ((key_grad, value_grad), query_grad)

    empty_rows = jnp.zeros((length_tokens, query_head_count, HEAD_SIZE), jnp.float32)
    (key_grad, value_grad), query_grads = lax.scan(
        backward_block,
        (empty_rows, empty_rows),
        (query_blocks, grad_attended, logsums, block_starts),
    )
    query_back = rotary_apply(
        query_grads.reshape(length_tokens, query_head_count, HEAD_SIZE), -1.0
    ).reshape(length_tokens, query_head_count * HEAD_SIZE)
    selector_float = choice_picker.astype(jnp.float32)
    key_returned = rotary_apply(
        jnp.einsum("jh,gjd->ghd", selector_float, key_grad, precision=PRECISE), -1.0
    )
    value_returned = jnp.einsum("jh,gjd->ghd", selector_float, value_grad, precision=PRECISE)
    keyvalue_partial = jnp.concatenate(
        [
            key_returned.reshape(length_tokens, KEYVALUE_HEADS * HEAD_SIZE),
            value_returned.reshape(length_tokens, KEYVALUE_HEADS * HEAD_SIZE),
        ],
        1,
    )
    state_total, keyvalue_total = (
        lax.psum(grad_signal[:, local_width:].astype(jnp.bfloat16), "tp").astype(jnp.float32),
        lax.psum(keyvalue_partial.astype(jnp.bfloat16), "tp").astype(jnp.float32),
    )
    inner_low = jnp.stack([grad_gate, grad_signal[:, :local_width]], 1).astype(jnp.bfloat16)
    steps_low = grad_steps.astype(jnp.bfloat16)
    query_low = query_back.astype(jnp.bfloat16)
    state_low = state_total.astype(jnp.bfloat16)
    keyvalue_low = keyvalue_total.astype(jnp.bfloat16)
    inner_wgrad = jnp.einsum("gd,gkc->dkc", normed, inner_low, preferred_element_type=jnp.float32)
    timestep_wgrad = contract_rows(normed, steps_low)
    state_wgrad = contract_rows(normed, state_low)
    query_wgrad = contract_rows(normed, query_low)
    keyvalue_wgrad = contract_rows(normed, keyvalue_low)
    normed_partial = (
        jnp.einsum("gkc,dkc->gd", inner_low, inner_full, preferred_element_type=jnp.float32)
        + contract_cols(steps_low, timestep_full)
        + contract_cols(query_low, query_full)
    )
    leader = (tensor_parallel_rank == 0).astype(jnp.float32)
    normed_partial = normed_partial + leader * (
        contract_cols(state_low, state_full) + contract_cols(keyvalue_low, keyvalue_full)
    )
    normed_grad = lax.psum_scatter(
        normed_partial.astype(jnp.bfloat16), "tp", scatter_dimension=0, tiled=True
    ).astype(jnp.float32)
    first_normal = residual * first_rms
    input_gain_part = jnp.sum(normed_grad * first_normal, 0)
    first_scaled = normed_grad * input_gain
    input_grad = grad_middle + first_rms * (
        first_scaled - first_normal * jnp.mean(first_scaled * first_normal, -1, keepdims=True)
    )
    gated_part = lax.dynamic_update_slice_in_dim(
        jnp.zeros((ssm_width,), jnp.float32), gain_grad, width_start, 0
    )
    kernel_part = jnp.concatenate(
        [
            lax.dynamic_update_slice_in_dim(
                jnp.zeros((conv_kernel.shape[0], ssm_width), jnp.float32),
                kernel_local[:, :local_width],
                width_start,
                1,
            ),
            kernel_local[:, local_width:],
        ],
        1,
    )
    offset_part = jnp.concatenate(
        [
            lax.dynamic_update_slice_in_dim(
                jnp.zeros((ssm_width,), jnp.float32), offset_local[:local_width], width_start, 0
            ),
            offset_local[local_width:],
        ],
        0,
    )
    head_zeros = jnp.zeros((timestep_bias.shape[0],), jnp.float32)
    bias_part = lax.dynamic_update_slice_in_dim(head_zeros, grad_bias, head_start, 0)
    decay_part = lax.dynamic_update_slice_in_dim(head_zeros, grad_decay, head_start, 0)
    skip_part = lax.dynamic_update_slice_in_dim(head_zeros, grad_skip, head_start, 0)
    summed = lax.psum(
        (
            input_gain_part,
            middle_gain_part,
            kernel_part,
            offset_part,
            bias_part,
            decay_part,
            skip_part,
            gated_part,
        ),
        ("fsdp", "tp"),
    )
    (
        inner_out,
        timestep_out,
        state_out,
        query_out,
        keyvalue_out,
        mamba_out,
        attention_out,
        gateup_out,
        down_out,
    ) = (
        lax.psum_scatter(
            inner_wgrad.astype(jnp.bfloat16), "fsdp", scatter_dimension=0, tiled=True
        ).astype(jnp.float32),
        lax.psum_scatter(
            timestep_wgrad.astype(jnp.bfloat16), "fsdp", scatter_dimension=0, tiled=True
        ).astype(jnp.float32),
        lax.psum_scatter(
            state_wgrad.astype(jnp.bfloat16), "fsdp", scatter_dimension=0, tiled=True
        ).astype(jnp.float32),
        lax.psum_scatter(
            query_wgrad.astype(jnp.bfloat16), "fsdp", scatter_dimension=0, tiled=True
        ).astype(jnp.float32),
        lax.psum_scatter(
            keyvalue_wgrad.astype(jnp.bfloat16), "fsdp", scatter_dimension=0, tiled=True
        ).astype(jnp.float32),
        lax.psum_scatter(
            mamba_wgrad.astype(jnp.bfloat16), "fsdp", scatter_dimension=1, tiled=True
        ).astype(jnp.float32),
        lax.psum_scatter(
            attention_wgrad.astype(jnp.bfloat16), "fsdp", scatter_dimension=1, tiled=True
        ).astype(jnp.float32),
        lax.psum_scatter(
            gateup_wgrad.astype(jnp.bfloat16), "fsdp", scatter_dimension=0, tiled=True
        ).astype(jnp.float32),
        lax.psum_scatter(
            down_wgrad.astype(jnp.bfloat16), "fsdp", scatter_dimension=1, tiled=True
        ).astype(jnp.float32),
    )
    return (
        block_output,
        input_grad,
        summed[0],
        inner_out,
        timestep_out,
        state_out,
        query_out,
        keyvalue_out,
        summed[2],
        summed[3],
        summed[4],
        summed[5],
        summed[6],
        summed[7],
        mamba_out,
        attention_out,
        summed[1],
        gateup_out,
        down_out,
    )


BLOCK = 256
LOG2E = 1.4426950408889634
HIDDEN_BIAS = -1e30


def narrow(values):
    return values.astype(jnp.bfloat16)


def wide(values):
    return values.astype(jnp.float32)


def mm(left, right):
    return jnp.dot(left, right, preferred_element_type=jnp.float32)


def sigmoid(values):
    return 1.0 / (1.0 + jnp.exp(-values))


def dot_wide(ones, values):
    first = narrow(values)
    rest = values - wide(first)
    second = narrow(rest)
    third = narrow(rest - wide(second))
    return mm(ones, first) + mm(ones, second) + mm(ones, third)


def triangle(rows, upper):
    down = lax.broadcasted_iota(jnp.int32, (rows, rows), 0)
    across = lax.broadcasted_iota(jnp.int32, (rows, rows), 1)
    keep = (across >= down) if upper else (down >= across)
    return jnp.where(keep, 1.0, 0.0).astype(jnp.bfloat16)


def pair_bias(label_column, label_row):
    rows = label_column.shape[0]
    down = lax.broadcasted_iota(jnp.int32, (rows, rows), 0)
    across = lax.broadcasted_iota(jnp.int32, (rows, rows), 1)
    keep = jnp.logical_and(label_column == label_row, down >= across)
    return jnp.where(keep, 0.0, HIDDEN_BIAS)


def conv_taps(signal, info):
    taps = [signal]
    for distance in range(1, 4):
        taps.append(pltpu.roll(signal, distance, 0) * info[:, distance : distance + 1])
    return taps


def conv_pre(taps, channel):
    result = channel[4:5, :]
    for distance in range(4):
        result = result + channel[distance : distance + 1, :] * taps[distance]
    return result


def conv_back(grad_pre, channel, info):
    rows = grad_pre.shape[0]
    result = channel[0:1, :] * grad_pre
    for distance in range(1, 4):
        masked = grad_pre * info[:, distance : distance + 1]
        result = result + channel[distance : distance + 1, :] * pltpu.roll(masked, rows - distance, 0)
    return result


def column_of(values, lane):
    lanes = lax.broadcasted_iota(jnp.int32, values.shape, 1)
    return jnp.sum(jnp.where(lanes == lane, values, 0.0), 1, keepdims=True)


def half_lanes(values, which):
    lanes = lax.broadcasted_iota(jnp.int32, values.shape, 1)
    keep = (lanes < HEAD_SIZE) if which == 0 else (lanes >= HEAD_SIZE)
    return jnp.where(keep, values, jnp.zeros_like(values))


def spans(rows):
    return [slice(at, at + BLOCK) for at in range(0, rows, BLOCK)]


def mixer_forward_kernel(
    gate_ref,
    value_ref,
    state_ref,
    steps_ref,
    info_ref,
    label_ref,
    channel_ref,
    state_channel_ref,
    head_ref,
    low_ref,
    scanned_ref,
    square_ref,
    dt_ref,
    cum_ref,
    crossed,
    bias,
    source_rows,
):
    pair = pl.program_id(0)
    info = info_ref[...]
    rows = info.shape[0]

    @pl.when(pair == 0)
    def _():
        taps = conv_taps(state_ref[...], info)
        pre = conv_pre(taps, state_channel_ref[...])
        states = narrow(pre * sigmoid(pre))
        half = states.shape[1] // 2
        crossed[...] = contract_cols(states[:, half:], states[:, :half])
        bias[...] = pair_bias(info[:, 4:5], label_ref[0:1, :])
        raw = steps_ref[...] + head_ref[0:1, :]
        dt = jnp.maximum(raw, 0.0) + jnp.log1p(jnp.exp(-jnp.abs(raw)))
        cum = dot_wide(triangle(rows, False), dt * (head_ref[1:2, :] * LOG2E))
        dt_ref[...] = dt
        cum_ref[...] = cum
        source_rows[...] = (cum - jnp.log(dt) * LOG2E).T
        square_ref[...] = jnp.zeros_like(square_ref)

    channel = channel_ref[...]
    pre = conv_pre(conv_taps(value_ref[...], info), channel)
    values = narrow(pre * sigmoid(pre))
    outputs = [channel[5:6, :] * wide(values[span]) for span in spans(rows)]
    for which in range(2):
        head = 2 * pair + which
        target = column_of(cum_ref[...], head)
        source = source_rows[pl.ds(head, 1), :]
        chosen = half_lanes(values, which)
        for i, down in enumerate(spans(rows)):
            for across in spans(rows)[: i + 1]:
                weights = jnp.exp2((target[down] - source[:, across]) + bias[down, across])
                outputs[i] += mm(narrow(weights * crossed[down, across]), chosen[across])
    scanned = jnp.concatenate(outputs, 0)
    scanned_ref[...] = scanned
    gate = gate_ref[...]
    gated = scanned * (gate * sigmoid(gate))
    low_ref[...] = narrow(gated * channel[6:7, :])
    square_ref[...] += gated * gated


def mixer_backward_kernel(
    gate_ref,
    value_ref,
    state_ref,
    steps_ref,
    info_ref,
    label_ref,
    channel_ref,
    state_channel_ref,
    head_ref,
    scanned_ref,
    incoming_ref,
    dt_ref,
    cum_ref,
    grad_gate_ref,
    grad_value_ref,
    grad_state_ref,
    grad_steps_ref,
    channel_grad_ref,
    state_grad_ref,
    head_grad_ref,
    crossed,
    bias,
    summed,
    states_low,
    source_rows,
    dt_rows,
    target_sums,
    source_sums,
):
    pair = pl.program_id(0)
    info = info_ref[...]
    rows = info.shape[0]
    half = state_ref.shape[1] // 2

    @pl.when(pair == 0)
    def _():
        pre = conv_pre(conv_taps(state_ref[...], info), state_channel_ref[...])
        states = narrow(pre * sigmoid(pre))
        states_low[...] = states
        crossed[...] = contract_cols(states[:, half:], states[:, :half])
        bias[...] = pair_bias(info[:, 4:5], label_ref[0:1, :])
        source_rows[...] = cum_ref[...].T
        dt_rows[...] = dt_ref[...].T
        summed[...] = jnp.zeros_like(summed)
        target_sums[...] = jnp.zeros_like(target_sums)
        source_sums[...] = jnp.zeros_like(source_sums)

    channel = channel_ref[...]
    taps = conv_taps(value_ref[...], info)
    pre = conv_pre(taps, channel)
    opened = sigmoid(pre)
    values = narrow(pre * opened)
    gate = gate_ref[...]
    gate_open = sigmoid(gate)
    silu_gate = gate * gate_open
    scanned = scanned_ref[...]
    gated = scanned * silu_gate
    incoming = incoming_ref[...]
    gain_grad = jnp.sum(incoming * gated, 0, keepdims=True)
    grad_gated = incoming * channel[6:7, :] + 2.0 * gated * info[:, 5:6]
    grad_gate_ref[...] = narrow(
        grad_gated * scanned * gate_open * (1.0 + gate * (1.0 - gate_open))
    )
    grad_scanned = grad_gated * silu_gate
    skip_grad = jnp.sum(grad_scanned * wide(values), 0, keepdims=True)
    low_grad = narrow(grad_scanned)
    value_grads = [channel[5:6, :] * grad_scanned[span] for span in spans(rows)]
    lanes = lax.broadcasted_iota(jnp.int32, (BLOCK, 128), 1)
    for which in range(2):
        head = 2 * pair + which
        target = column_of(cum_ref[...], head)
        dt_column = column_of(dt_ref[...], head)
        source = source_rows[pl.ds(head, 1), :]
        dt_row = dt_rows[pl.ds(head, 1), :]
        chosen = half_lanes(low_grad, which)
        returned = [jnp.zeros((BLOCK, 128), jnp.float32) for _ in spans(rows)]
        column_sums = [jnp.zeros((1, BLOCK), jnp.float32) for _ in spans(rows)]
        for i, down in enumerate(spans(rows)):
            row_sum = jnp.zeros((BLOCK, 1), jnp.float32)
            for j, across in enumerate(spans(rows)[: i + 1]):
                decay = jnp.exp2((target[down] - source[:, across]) + bias[down, across])
                linked = crossed[down, across]
                returned[j] += contract_rows(narrow(decay * linked), chosen[down])
                reach = decay * contract_cols(chosen[down], values[across])
                scaled = reach * dt_row[:, across]
                summed[down, across] += scaled
                column_sums[j] += jnp.sum(reach * linked, 0, keepdims=True)
                row_sum += jnp.sum(scaled * linked, 1, keepdims=True)
            target_sums[down, :] += jnp.where(lanes == head, row_sum, 0.0)
        for j, across in enumerate(spans(rows)):
            value_grads[j] += dt_column[across] * returned[j]
            source_sums[pl.ds(head, 1), across] = column_sums[j]
    grad_pre = jnp.concatenate(value_grads, 0) * (opened * (1.0 + pre * (1.0 - opened)))
    grad_value_ref[...] = narrow(conv_back(grad_pre, channel, info))
    channel_grad_ref[...] = jnp.concatenate(
        [jnp.sum(grad_pre * tap, 0, keepdims=True) for tap in taps]
        + [jnp.sum(grad_pre, 0, keepdims=True), skip_grad, gain_grad, jnp.zeros_like(gain_grad)],
        0,
    )

    @pl.when(pair == pl.num_programs(0) - 1)
    def _():
        low = narrow(summed[...])
        states = states_low[...]
        grad_keys = contract_rows(low, states[:, half:])
        grad_queries = mm(low, states[:, :half])
        state_channel = state_channel_ref[...]
        state_taps = conv_taps(state_ref[...], info)
        state_pre = conv_pre(state_taps, state_channel)
        state_open = sigmoid(state_pre)
        grad_state_pre = jnp.concatenate([grad_keys, grad_queries], 1) * (
            state_open * (1.0 + state_pre * (1.0 - state_open))
        )
        grad_state_ref[...] = narrow(conv_back(grad_state_pre, state_channel, info))
        state_grad_ref[...] = jnp.concatenate(
            [jnp.sum(grad_state_pre * tap, 0, keepdims=True) for tap in state_taps]
            + [jnp.sum(grad_state_pre, 0, keepdims=True)]
            + [jnp.zeros((3, 2 * half), jnp.float32)],
            0,
        )
        dt = dt_ref[...]
        rate = head_ref[1:2, :]
        source_columns = source_sums[...].T
        grad_rate = dot_wide(triangle(rows, True), target_sums[...] - dt * source_columns)
        grad_dt = source_columns + rate * grad_rate
        grad_steps = grad_dt * sigmoid(steps_ref[...] + head_ref[0:1, :])
        grad_steps_ref[...] = narrow(grad_steps)
        head_grad_ref[...] = jnp.concatenate(
            [
                jnp.sum(grad_steps, 0, keepdims=True),
                jnp.sum(grad_rate * dt * rate, 0, keepdims=True),
                jnp.zeros((6, 128), jnp.float32),
            ],
            0,
        )


def rotated(values, cosine, sinusoid):
    lanes = lax.broadcasted_iota(jnp.int32, values.shape, 1)
    quarter = HEAD_SIZE // 2
    swapped = jnp.where(
        lanes % HEAD_SIZE < quarter,
        pltpu.roll(values, values.shape[1] - quarter, 1),
        pltpu.roll(values, quarter, 1),
    )
    return values * cosine + swapped * sinusoid


def attention_forward_kernel(
    rank_ref,
    query_ref,
    keyvalue_ref,
    info_ref,
    label_ref,
    cosine_ref,
    sinusoid_ref,
    attended_ref,
    turned_ref,
    key_ref,
    value_ref,
    logsum_ref,
    bias,
):
    rows = query_ref.shape[0]
    cosine, sinusoid = cosine_ref[...], sinusoid_ref[...]
    bias[...] = pair_bias(info_ref[:, 4:5], label_ref[0:1, :])
    lanes = lax.broadcasted_iota(jnp.int32, (rows, 128), 1)
    own = (lanes < HEAD_SIZE) == (rank_ref[0] == 0)

    def doubled(values):
        return jnp.where(own, values, pltpu.roll(values, HEAD_SIZE, 1))

    keys = narrow(doubled(rotated(keyvalue_ref[:, :128], cosine, sinusoid)))
    values = narrow(doubled(keyvalue_ref[:, 128:]))
    key_ref[...] = keys
    value_ref[...] = values
    scaling = 1.0 / math.sqrt(HEAD_SIZE)
    logsums = [jnp.zeros((BLOCK, 128), jnp.float32) for _ in spans(rows)]
    block_lanes = lax.broadcasted_iota(jnp.int32, (BLOCK, 128), 1)
    for pair in range(query_ref.shape[1] // 128):
        columns = slice(128 * pair, 128 * pair + 128)
        queries = narrow(rotated(query_ref[:, columns], cosine, sinusoid))
        turned_ref[:, columns] = queries
        results = [jnp.zeros((BLOCK, 128), jnp.float32) for _ in spans(rows)]
        for which in range(2):
            chosen = half_lanes(queries, which)
            reading = half_lanes(values, which)
            for i, down in enumerate(spans(rows)):
                width = BLOCK * (i + 1)
                scores = contract_cols(chosen[down], keys[:width]) * scaling + bias[down, :width]
                highest = jnp.max(scores, 1, keepdims=True)
                weights = jnp.exp(scores - highest)
                total = jnp.sum(weights, 1, keepdims=True)
                results[i] += mm(narrow(weights * (1.0 / total)), reading[:width])
                logsums[i] = jnp.where(
                    block_lanes == 2 * pair + which, highest + jnp.log(total), logsums[i]
                )
        for i, down in enumerate(spans(rows)):
            attended_ref[down, columns] = narrow(results[i])
    for i, down in enumerate(spans(rows)):
        logsum_ref[down, :] = logsums[i]


def attention_backward_kernel(
    rank_ref,
    incoming_ref,
    turned_ref,
    key_ref,
    value_ref,
    logsum_ref,
    info_ref,
    label_ref,
    cosine_ref,
    sinusoid_ref,
    grad_query_ref,
    grad_keyvalue_ref,
    bias,
):
    rows = turned_ref.shape[0]
    cosine, sinusoid = cosine_ref[...], sinusoid_ref[...]
    bias[...] = pair_bias(info_ref[:, 4:5], label_ref[0:1, :])
    keys, values = key_ref[...], value_ref[...]
    scaling = 1.0 / math.sqrt(HEAD_SIZE)
    zero = jnp.zeros((BLOCK, 128), jnp.float32)
    key_grads = [zero for _ in spans(rows)]
    value_grads = [zero for _ in spans(rows)]
    for pair in range(turned_ref.shape[1] // 128):
        columns = slice(128 * pair, 128 * pair + 128)
        query_grads = [zero for _ in spans(rows)]
        for which in range(2):
            queries = half_lanes(turned_ref[:, columns], which)
            incoming = half_lanes(incoming_ref[:, columns], which)
            reading = half_lanes(keys, which)
            head = 2 * pair + which
            for i, down in enumerate(spans(rows)):
                width = BLOCK * (i + 1)
                scores = contract_cols(queries[down], keys[:width]) * scaling + bias[down, :width]
                probs = jnp.exp(scores - logsum_ref[down, head : head + 1])
                grad_probs = contract_cols(incoming[down], values[:width])
                inner_sum = jnp.sum(grad_probs * probs, 1, keepdims=True)
                grad_scores = narrow(probs * (grad_probs - inner_sum))
                probs_low = narrow(probs)
                query_grads[i] += mm(grad_scores, reading[:width])
                for j, across in enumerate(spans(rows)[: i + 1]):
                    key_grads[j] += contract_rows(grad_scores[:, across], queries[down])
                    value_grads[j] += contract_rows(probs_low[:, across], incoming[down])
        grad_query_ref[:, columns] = narrow(
            rotated(jnp.concatenate(query_grads, 0) * scaling, cosine, -sinusoid)
        )
    lanes = lax.broadcasted_iota(jnp.int32, (rows, 128), 1)
    own = (lanes < HEAD_SIZE) == (rank_ref[0] == 0)

    def placed(values):
        return jnp.where(own, values + pltpu.roll(values, HEAD_SIZE, 1), 0.0)

    key_grad = rotated(placed(jnp.concatenate(key_grads, 0) * scaling), cosine, -sinusoid)
    grad_keyvalue_ref[:, :128] = narrow(key_grad)
    grad_keyvalue_ref[:, 128:] = narrow(placed(jnp.concatenate(value_grads, 0)))


def block_spec(shape, index):
    return pl.BlockSpec(shape, index)


def fixed(array):
    return pl.BlockSpec(array.shape, lambda p: (0, 0))


def params():
    return pltpu.CompilerParams(vmem_limit_bytes=48 * 1024 * 1024)


def mixer_forward(projected, widths, info, labels, channel, state_channel, heads):
    rows = info.shape[0]
    width, state_at, steps_at = widths
    pairs = width // 128
    state_width = state_channel.shape[1]
    column = lambda p: (0, p)
    return pl.pallas_call(
        mixer_forward_kernel,
        grid=(pairs,),
        in_specs=[
            block_spec((rows, 128), column),
            block_spec((rows, 128), lambda p: (0, pairs + p)),
            block_spec((rows, state_width), lambda p: (0, state_at // state_width)),
            block_spec((rows, 128), lambda p: (0, steps_at // 128)),
            fixed(info),
            fixed(labels),
            block_spec((8, 128), column),
            fixed(state_channel),
            fixed(heads),
        ],
        out_specs=[
            block_spec((rows, 128), column),
            block_spec((rows, 128), column),
            block_spec((rows, 128), lambda p: (0, 0)),
            block_spec((rows, 128), lambda p: (0, 0)),
            block_spec((rows, 128), lambda p: (0, 0)),
        ],
        out_shape=[
            jax.ShapeDtypeStruct((rows, width), jnp.bfloat16),
            jax.ShapeDtypeStruct((rows, width), jnp.float32),
            jax.ShapeDtypeStruct((rows, 128), jnp.float32),
            jax.ShapeDtypeStruct((rows, 128), jnp.float32),
            jax.ShapeDtypeStruct((rows, 128), jnp.float32),
        ],
        scratch_shapes=[
            pltpu.VMEM((rows, rows), jnp.float32),
            pltpu.VMEM((rows, rows), jnp.float32),
            pltpu.VMEM((128, rows), jnp.float32),
        ],
        compiler_params=params(),
        cost_estimate=pl.CostEstimate(
            flops=24 * rows * rows * width, bytes_accessed=rows * width * 14, transcendentals=0
        ),
        name="mixer_forward",
    )(projected, projected, projected, projected, info, labels, channel, state_channel, heads)


def mixer_backward(
    projected, widths, info, labels, channel, state_channel, heads, scanned, incoming, dt, cum
):
    rows = info.shape[0]
    width, state_at, steps_at = widths
    pairs = width // 128
    state_width = state_channel.shape[1]
    column = lambda p: (0, p)
    still = lambda p: (0, 0)
    return pl.pallas_call(
        mixer_backward_kernel,
        grid=(pairs,),
        in_specs=[
            block_spec((rows, 128), column),
            block_spec((rows, 128), lambda p: (0, pairs + p)),
            block_spec((rows, state_width), lambda p: (0, state_at // state_width)),
            block_spec((rows, 128), lambda p: (0, steps_at // 128)),
            fixed(info),
            fixed(labels),
            block_spec((8, 128), column),
            fixed(state_channel),
            fixed(heads),
            block_spec((rows, 128), column),
            block_spec((rows, 128), column),
            fixed(dt),
            fixed(cum),
        ],
        out_specs=[
            block_spec((rows, 128), column),
            block_spec((rows, 128), column),
            block_spec((rows, state_width), still),
            block_spec((rows, 128), still),
            block_spec((8, 128), column),
            block_spec((8, state_width), still),
            block_spec((8, 128), still),
        ],
        out_shape=[
            jax.ShapeDtypeStruct((rows, width), jnp.bfloat16),
            jax.ShapeDtypeStruct((rows, width), jnp.bfloat16),
            jax.ShapeDtypeStruct((rows, state_width), jnp.bfloat16),
            jax.ShapeDtypeStruct((rows, 128), jnp.bfloat16),
            jax.ShapeDtypeStruct((8, width), jnp.float32),
            jax.ShapeDtypeStruct((8, state_width), jnp.float32),
            jax.ShapeDtypeStruct((8, 128), jnp.float32),
        ],
        scratch_shapes=[
            pltpu.VMEM((rows, rows), jnp.float32),
            pltpu.VMEM((rows, rows), jnp.float32),
            pltpu.VMEM((rows, rows), jnp.float32),
            pltpu.VMEM((rows, state_width), jnp.bfloat16),
            pltpu.VMEM((128, rows), jnp.float32),
            pltpu.VMEM((128, rows), jnp.float32),
            pltpu.VMEM((rows, 128), jnp.float32),
            pltpu.VMEM((128, rows), jnp.float32),
        ],
        compiler_params=params(),
        cost_estimate=pl.CostEstimate(
            flops=72 * rows * rows * width, bytes_accessed=rows * width * 22, transcendentals=0
        ),
        name="mixer_backward",
    )(
        projected,
        projected,
        projected,
        projected,
        info,
        labels,
        channel,
        state_channel,
        heads,
        scanned,
        incoming,
        dt,
        cum,
    )


def attention_forward(rank, projected, widths, info, labels, cosine, sinusoid):
    rows = info.shape[0]
    query_at, keyvalue_at, query_width, keyvalue_width = widths
    return pl.pallas_call(
        attention_forward_kernel,
        grid=(1,),
        in_specs=[
            pl.BlockSpec(memory_space=pltpu.SMEM),
            block_spec((rows, query_width), lambda p: (0, query_at // query_width)),
            block_spec((rows, keyvalue_width), lambda p: (0, keyvalue_at // keyvalue_width)),
            fixed(info),
            fixed(labels),
            fixed(cosine),
            fixed(sinusoid),
        ],
        out_specs=[
            block_spec((rows, query_width), lambda p: (0, 0)),
            block_spec((rows, query_width), lambda p: (0, 0)),
            block_spec((rows, 128), lambda p: (0, 0)),
            block_spec((rows, 128), lambda p: (0, 0)),
            block_spec((rows, 128), lambda p: (0, 0)),
        ],
        out_shape=[
            jax.ShapeDtypeStruct((rows, query_width), jnp.bfloat16),
            jax.ShapeDtypeStruct((rows, query_width), jnp.bfloat16),
            jax.ShapeDtypeStruct((rows, 128), jnp.bfloat16),
            jax.ShapeDtypeStruct((rows, 128), jnp.bfloat16),
            jax.ShapeDtypeStruct((rows, 128), jnp.float32),
        ],
        scratch_shapes=[pltpu.VMEM((rows, rows), jnp.float32)],
        compiler_params=params(),
        cost_estimate=pl.CostEstimate(
            flops=24 * rows * rows * query_width, bytes_accessed=rows * 4096, transcendentals=0
        ),
        name="attention_forward",
    )(rank, projected, projected, info, labels, cosine, sinusoid)


def attention_backward(rank, incoming, turned, keys, values, logsum, info, labels, cosine, sinusoid):
    rows, query_width = turned.shape
    arrays = (incoming, turned, keys, values, logsum, info, labels, cosine, sinusoid)
    return pl.pallas_call(
        attention_backward_kernel,
        grid=(1,),
        in_specs=[pl.BlockSpec(memory_space=pltpu.SMEM)] + [fixed(array) for array in arrays],
        out_specs=[
            block_spec((rows, query_width), lambda p: (0, 0)),
            block_spec((rows, 256), lambda p: (0, 0)),
        ],
        out_shape=[
            jax.ShapeDtypeStruct((rows, query_width), jnp.bfloat16),
            jax.ShapeDtypeStruct((rows, 256), jnp.bfloat16),
        ],
        scratch_shapes=[pltpu.VMEM((rows, rows), jnp.float32)],
        compiler_params=params(),
        cost_estimate=pl.CostEstimate(
            flops=72 * rows * rows * query_width, bytes_accessed=rows * 4096, transcendentals=0
        ),
        name="attention_backward",
    )(rank, *arrays)


def place_kernel(count, starts_ref, *refs):
    pieces, whole, done = refs[:count], refs[count], refs[count + 1]
    rows = pieces[0].shape[0]
    copies = []
    for at, piece in enumerate(pieces):
        start = pl.multiple_of(starts_ref[at] * rows, rows)
        copies.append(pltpu.make_async_copy(piece, whole.at[pl.ds(start, rows)], done.at[at]))
    for copy in copies:
        copy.start()
    for copy in copies:
        copy.wait()


def place(starts, pieces):
    count = len(pieces)
    rows, columns = pieces[0].shape
    return pl.pallas_call(
        lambda *refs: place_kernel(count, *refs),
        in_specs=[pl.BlockSpec(memory_space=pltpu.SMEM)]
        + [pl.BlockSpec(memory_space=pl.ANY)] * count,
        out_specs=pl.BlockSpec(memory_space=pltpu.VMEM),
        out_shape=jax.ShapeDtypeStruct((count * rows, columns), pieces[0].dtype),
        scratch_shapes=[pltpu.SemaphoreType.DMA((count,))],
        compiler_params=params(),
        cost_estimate=pl.CostEstimate(
            flops=0, bytes_accessed=4 * count * rows * columns, transcendentals=0
        ),
        name="place",
    )(starts, *pieces)


def swaps(size, bit):
    return [(i, i ^ bit) for i in range(size)]


def ring(size):
    return [(i, (i + 4) % size) for i in range(size)]


def gather_pieces(piece, size):
    held = [piece]
    for _ in range(size // 4 - 1):
        held.append(lax.ppermute(held[-1], "fsdp", ring(size)))
    pieces = []
    for shard in held:
        for line in (shard, lax.ppermute(shard, "fsdp", swaps(size, 2))):
            pieces += [line, lax.ppermute(line, "fsdp", swaps(size, 1))]
    return pieces


def reduce_pieces(grad, size):
    half = grad.shape[0] // 2
    own = narrow(
        wide(grad[:half]) + wide(lax.ppermute(grad[half:], "fsdp", swaps(size, 1)))
    )
    half //= 2
    own = wide(own[:half]) + wide(lax.ppermute(own[half:], "fsdp", swaps(size, 2)))
    parts = own.reshape(size // 4, -1, own.shape[1])
    total = parts[1]
    for step in range(2, size // 4 + 1):
        total = parts[step % (size // 4)] + wide(
            lax.ppermute(narrow(total), "fsdp", ring(size))
        )
    return total


def reduce_all(values, size):
    bit = 1
    while bit < size:
        values = values + lax.ppermute(values, "fsdp", swaps(size, bit))
        bit *= 2
    return values + lax.ppermute(values, "tp", swaps(2, 1))


def packed_body(
    size,
    block_input,
    segment_ids,
    output_cotangent,
    input_gain,
    inner_weight,
    timestep_weight,
    state_weight,
    query_weight,
    keyvalue_matrix,
    conv_kernel,
    conv_offset,
    timestep_bias,
    decay_log,
    skip_scale,
    gated_gain,
    mamba_down,
    attention_down,
    middle_gain,
    gateup_weight,
    down_weight,
):
    rank = lax.axis_index("tp")
    at = lax.axis_index("fsdp")
    depth = size // 4
    rows = segment_ids.shape[0]
    own_rows = rows // 2
    shard, _, width = inner_weight.shape
    model = shard * size
    heads = timestep_weight.shape[1]
    state_width = state_weight.shape[1]
    query_width = query_weight.shape[1]
    keyvalue_width = keyvalue_matrix.shape[1]
    hidden = gateup_weight.shape[2]
    ssm_width = gated_gain.shape[0]
    state_at = 2 * width
    query_at = state_at + state_width
    keyvalue_at = query_at + query_width
    steps_at = keyvalue_at + keyvalue_width

    def other(values):
        return lax.ppermute(values, "tp", swaps(2, 1))

    def joined(own, far):
        first = jnp.where(rank == 0, own, far)
        second = jnp.where(rank == 0, far, own)
        return jnp.concatenate([first, second], 0)

    def own_half(values):
        return lax.dynamic_slice_in_dim(values, rank * own_rows, own_rows, 0)

    def far_half(values):
        return lax.dynamic_slice_in_dim(values, (1 - rank) * own_rows, own_rows, 0)

    first_shard = jnp.concatenate(
        [
            inner_weight.reshape(shard, 2 * width),
            state_weight,
            query_weight,
            keyvalue_matrix,
            jnp.pad(timestep_weight, ((0, 0), (0, 128 - heads))),
        ],
        1,
    )
    second_shard = jnp.concatenate([mamba_down, attention_down], 0).T
    third_shard = jnp.concatenate([gateup_weight.reshape(shard, 2 * hidden), down_weight.T], 1)
    ring_at, x_at, core_at = at // 4, (at // 2) % 2, at % 2

    def block_of(distance, x_flip, core_flip):
        return ((ring_at - distance + depth) % depth) * 4 + (x_at ^ x_flip) * 2 + (
            core_at ^ core_flip
        )

    starts = jnp.stack(
        [block_of(k, i, j) for k in range(depth) for i in range(2) for j in range(2)]
    ).astype(jnp.int32)
    first_pieces = gather_pieces(first_shard, size)
    second_shard, third_shard, _ = lax.optimization_barrier(
        (second_shard, third_shard, first_pieces[-4])
    )
    second_pieces = gather_pieces(second_shard, size)
    third_shard, _ = lax.optimization_barrier((third_shard, second_pieces[-4]))
    third_pieces = gather_pieces(third_shard, size)

    relative = jnp.arange(model, dtype=jnp.int32)
    piece_at = relative // shard
    absolute = (
        block_of(piece_at % depth, (piece_at // depth) % 2, piece_at // (2 * depth)) * shard
        + relative % shard
    )
    permutation = (jnp.arange(model, dtype=jnp.int32)[:, None] == absolute[None, :]).astype(
        jnp.bfloat16
    )

    def permuted(values):
        return narrow(mm(values, permutation))

    residual_low = joined(block_input, other(block_input))
    residual = wide(residual_low)
    first_rms = inverse_rms(residual)
    normed = narrow(residual * first_rms * input_gain)
    cotangent = joined(output_cotangent, other(output_cotangent))
    labels = segment_ids.astype(jnp.float32)
    info = [jnp.zeros((rows, 1), jnp.float32)]
    for distance in range(1, 4):
        earlier = jnp.concatenate([jnp.full((distance,), -1.0), labels[:-distance]], 0)
        info.append((earlier == labels).astype(jnp.float32)[:, None])
    info = jnp.concatenate(info + [labels[:, None], jnp.zeros((rows, 123), jnp.float32)], 1)
    label_rows = jnp.broadcast_to(labels[None, :], (8, rows))
    repeat = width // heads
    local_skip = lax.dynamic_slice_in_dim(skip_scale, rank * heads, heads, 0)
    local = lambda array: lax.dynamic_slice_in_dim(array, rank * width, width, array.ndim - 1)
    channel = jnp.concatenate(
        [
            local(conv_kernel),
            local(conv_offset)[None],
            jnp.repeat(local_skip, repeat)[None],
            local(gated_gain)[None],
            jnp.zeros((1, width), jnp.float32),
        ],
        0,
    )
    state_channel = jnp.concatenate(
        [
            conv_kernel[:, ssm_width:],
            conv_offset[None, ssm_width:],
            jnp.zeros((3, state_width), jnp.float32),
        ],
        0,
    )
    local_head = lambda array: lax.dynamic_slice_in_dim(array, rank * heads, heads, 0)
    head_rows = jnp.pad(
        jnp.stack([local_head(timestep_bias), -jnp.exp(local_head(decay_log))]),
        ((0, 6), (0, 128 - heads)),
    )
    quarter = HEAD_SIZE // 2
    frequency = jnp.exp(
        jnp.arange(quarter, dtype=jnp.float32) * (-2.0 * math.log(ROPE_BASE) / HEAD_SIZE)
    )
    angles = jnp.arange(rows, dtype=jnp.float32)[:, None] * frequency[None, :]
    cosine = jnp.tile(jnp.cos(angles), (1, 4))
    sinusoid = jnp.sin(angles)
    sinusoid = jnp.concatenate([-sinusoid, sinusoid, -sinusoid, sinusoid], 1)
    rank_array = rank.astype(jnp.int32)[None]

    first_weight = place(starts, first_pieces)
    projected = mm(normed, first_weight)
    attended, turned, keys, values, logsum = attention_forward(
        rank_array,
        projected,
        (query_at, keyvalue_at, query_width, keyvalue_width),
        info,
        label_rows,
        cosine,
        sinusoid,
    )
    second_weight = place(starts, second_pieces)
    mamba_weight, attention_weight = second_weight[:, :width], second_weight[:, width:]
    attention_low = narrow(contract_cols(attended, attention_weight))
    attention_part = wide(attention_low) + wide(other(attention_low))
    mixer_widths = (width, state_at, steps_at)
    gated_low, scanned, square_lanes, dt, cum = mixer_forward(
        projected, mixer_widths, info, label_rows, channel, state_channel, head_rows
    )
    squares = jnp.sum(square_lanes, 1)
    squares = squares + other(squares)
    mamba_low = narrow(contract_cols(gated_low, mamba_weight))
    mamba_part = wide(mamba_low) + wide(other(mamba_low))
    norm_factor = lax.rsqrt(squares / ssm_width + EPSILON)
    factor = wide(narrow(norm_factor))[:, None]
    middle = residual + (factor * mamba_part + attention_part)
    middle_rms = inverse_rms(middle)
    hidden_in = narrow(middle * middle_rms * middle_gain)
    third_weight = place(starts, third_pieces)
    gateup_full, down_full = third_weight[:, : 2 * hidden], third_weight[:, 2 * hidden :]
    gateup = mm(hidden_in, gateup_full)
    gate_part, up_part = gateup[:, :hidden], gateup[:, hidden:]
    gate_sigmoid = jax.nn.sigmoid(gate_part)
    activated = narrow(gate_part * gate_sigmoid * up_part)

    grad_activated = mm(cotangent, down_full)
    grad_gateup = narrow(
        jnp.concatenate(
            [
                grad_activated
                * up_part
                * gate_sigmoid
                * (1.0 + gate_part * (1.0 - gate_sigmoid)),
                grad_activated * (gate_part * gate_sigmoid),
            ],
            1,
        )
    )
    hidden_low = narrow(contract_cols(grad_gateup, gateup_full))
    grad_hidden = wide(hidden_low) + wide(other(hidden_low))
    feedforward_low = narrow(contract_cols(activated, down_full))
    block_output = (
        own_half(middle)
        + wide(own_half(feedforward_low))
        + wide(other(far_half(feedforward_low)))
    )
    down_grad = reduce_pieces(narrow(contract_rows(permuted(cotangent), activated)), size)
    gateup_grad = reduce_pieces(narrow(contract_rows(permuted(hidden_in), grad_gateup)), size)
    middle_normal = middle * middle_rms
    middle_gain_part = jnp.sum(grad_hidden * middle_normal, 0)
    middle_scaled = grad_hidden * middle_gain
    grad_middle = wide(cotangent) + middle_rms * (
        middle_scaled - middle_normal * jnp.mean(middle_scaled * middle_normal, -1, keepdims=True)
    )
    mix_low = narrow(grad_middle)
    mix = wide(mix_low)
    grad_square = narrow(
        jnp.sum(mix * mamba_part, -1) * -0.5 * norm_factor * norm_factor * norm_factor / ssm_width
    )
    grad_mamba = narrow(factor * mix)

    second_grad = reduce_pieces(
        narrow(
            jnp.concatenate(
                [
                    contract_rows(permuted(grad_mamba), gated_low),
                    contract_rows(permuted(mix_low), attended),
                ],
                1,
            )
        ),
        size,
    )
    grad_gated_low = mm(grad_mamba, mamba_weight)
    lanes = jnp.arange(128, dtype=jnp.int32)[None, :]
    info = jnp.where(lanes == 5, wide(grad_square)[:, None], info)
    grad_attended = narrow(mm(mix_low, attention_weight))
    grad_query, grad_keyvalue = attention_backward(
        rank_array, grad_attended, turned, keys, values, logsum, info, label_rows, cosine, sinusoid
    )
    grad_gate, grad_value, grad_state, grad_steps, channel_grad, state_grad, head_grad = (
        mixer_backward(
            projected,
            mixer_widths,
            info,
            label_rows,
            channel,
            state_channel,
            head_rows,
            scanned,
            grad_gated_low,
            dt,
            cum,
        )
    )
    grad_projected = jnp.concatenate(
        [grad_gate, grad_value, grad_state, grad_query, grad_keyvalue, grad_steps], 1
    )
    normed_partial = contract_cols(grad_projected, first_weight)
    first_grad = reduce_pieces(
        narrow(contract_rows(permuted(normed), grad_projected)), size
    )
    first_normal = residual * first_rms
    input_gain_part = jnp.sum(normed_partial * first_normal, 0)
    normed_low = narrow(normed_partial)
    normed_grad = wide(own_half(normed_low)) + wide(other(far_half(normed_low)))
    own_normal = own_half(first_normal)
    first_scaled = normed_grad * input_gain
    input_grad = own_half(grad_middle) + own_half(first_rms) * (
        first_scaled - own_normal * jnp.mean(first_scaled * own_normal, -1, keepdims=True)
    )

    spread = lambda part, total, start: lax.dynamic_update_slice_in_dim(
        jnp.zeros(part.shape[:-1] + (total,), jnp.float32), part, start, part.ndim - 1
    )
    channel_parts = jnp.concatenate(
        [spread(channel_grad[:5], ssm_width, rank * width), state_grad[:5]], 1
    )
    skip_grad = jnp.sum(channel_grad[5].reshape(heads, repeat), 1)
    head_parts = spread(
        jnp.concatenate([head_grad[:2, :heads], skip_grad[None]], 0),
        timestep_bias.shape[0],
        rank * heads,
    )
    gain_parts = spread(channel_grad[6], ssm_width, rank * width)
    leader = (rank == 0).astype(jnp.float32)
    parts = [input_gain_part, middle_gain_part * leader, gain_parts, channel_parts, head_parts]
    flat = jnp.concatenate([part.reshape(-1) for part in parts])
    flat = reduce_all(jnp.pad(flat, (0, -flat.shape[0] % 1024)).reshape(-1, 128), size).reshape(-1)
    summed = []
    for part in parts:
        summed.append(flat[: part.size].reshape(part.shape))
        flat = flat[part.size :]
    shared = jnp.concatenate(
        [first_grad[:, state_at:query_at], first_grad[:, keyvalue_at:steps_at]], 1
    )
    shared = shared + other(shared)
    return (
        block_output,
        input_grad,
        summed[0],
        first_grad[:, :state_at].reshape(shard, 2, width),
        first_grad[:, steps_at : steps_at + heads],
        shared[:, :state_width],
        first_grad[:, query_at:keyvalue_at],
        shared[:, state_width:],
        summed[3][:4],
        summed[3][4],
        summed[4][0],
        summed[4][1],
        summed[4][2],
        summed[2],
        second_grad[:, :width].T,
        second_grad[:, width:].T,
        summed[1],
        gateup_grad.reshape(shard, 2, hidden),
        down_grad.T,
    )


def solution(mesh):
    fsdp, tp = mesh.shape["fsdp"], mesh.shape["tp"]

    def body(*operands):
        rows = operands[1].shape[0]
        if tp == 2 and fsdp % 4 == 0 and rows == 2 * BLOCK:
            return packed_body(fsdp, *operands)
        return general_body(*operands)

    return jax.shard_map(
        body,
        mesh=mesh,
        in_specs=(
            P(("fsdp", "tp"), None),
            P("fsdp"),
            P(("fsdp", "tp"), None),
            P(),
            P("fsdp", None, "tp"),
            P("fsdp", "tp"),
            P("fsdp", None),
            P("fsdp", "tp"),
            P("fsdp", None),
            P(),
            P(),
            P(),
            P(),
            P(),
            P(),
            P("tp", "fsdp"),
            P("tp", "fsdp"),
            P(),
            P("fsdp", None, "tp"),
            P("tp", "fsdp"),
        ),
        out_specs=(
            P(("fsdp", "tp"), None),
            P(("fsdp", "tp"), None),
            P(),
            P("fsdp", None, "tp"),
            P("fsdp", "tp"),
            P("fsdp", None),
            P("fsdp", "tp"),
            P("fsdp", None),
            P(),
            P(),
            P(),
            P(),
            P(),
            P(),
            P("tp", "fsdp"),
            P("tp", "fsdp"),
            P(),
            P("fsdp", None, "tp"),
            P("tp", "fsdp"),
        ),
        check_vma=False,
    )
```

```python
import math

import jax
import jax.numpy as jnp
from jax import lax
from jax.experimental import pallas as pl
from jax.experimental.pallas import tpu as pltpu
from jax.sharding import PartitionSpec as P

QUERY_HEADS = 8
KEYVALUE_HEADS = 2
HEAD_SIZE = 64
SCAN_BLOCK = 256
QUERY_BLOCK = 512


EPSILON = 1e-05
MASKED_SCORE = -1e30
ROPE_BASE = 100000000000.0
PRECISE = lax.Precision.HIGHEST


def inverse_rms(values):
    return lax.rsqrt(jnp.mean(values * values, -1, keepdims=True) + EPSILON)


def contract_rows(left, right):
    return lax.dot_general(
        left, right, (((0,), (0,)), ((), ())), preferred_element_type=jnp.float32
    )


def contract_cols(left, right):
    return lax.dot_general(
        left, right, (((1,), (1,)), ((), ())), preferred_element_type=jnp.float32
    )


def causal_conv(signal, kernel, offset, segment):
    length_tokens = signal.shape[0]
    result = offset[None, :] + kernel[0][None, :] * signal
    for distance in range(1, kernel.shape[0]):
        shifted = jnp.concatenate(
            [
                jnp.zeros((distance, signal.shape[1]), signal.dtype),
                signal[: length_tokens - distance],
            ],
            0,
        )
        earlier = jnp.concatenate(
            [jnp.full((distance,), -1, jnp.int32), segment[: length_tokens - distance]], 0
        )
        retained = (earlier == segment).astype(signal.dtype)
        result = result + kernel[distance][None, :] * shifted * retained[:, None]
    return result


def state_scan(values, timesteps, decays, key_row_block, query_rows, segment, block):
    total, head_count, channels = values.shape
    count = total // block
    states = key_row_block.shape[1]
    lower = jnp.arange(block)[:, None] >= jnp.arange(block)[None, :]

    def advance(carry, pieces):
        memory, previous = carry
        value_block, step_block, key_block, query_block, labels = pieces
        rates = step_block * decays[None, :]
        cumulative = jnp.cumsum(rates, 0)
        linked = jnp.logical_and(labels[:, None] == labels[None, :], lower)
        gaps = cumulative[:, None, :] - cumulative[None, :, :]
        weights = jnp.exp(jnp.where(linked[:, :, None], gaps, 0.0)) * linked[:, :, None].astype(
            jnp.float32
        )
        intersections = jnp.dot(query_block, key_block.T, precision=PRECISE)
        scaled = value_block * step_block[:, :, None]
        within = jnp.einsum(
            "tsh,shp->thp", intersections[:, :, None] * weights, scaled, precision=PRECISE
        )
        carried = jnp.exp(cumulative) * (labels == previous).astype(jnp.float32)[:, None]
        across = (
            jnp.einsum("tn,hpn->thp", query_block, memory, precision=PRECISE) * carried[:, :, None]
        )
        final = cumulative[block - 1]
        ending = labels[block - 1]
        toward = (
            jnp.exp(final[None, :] - cumulative) * (labels == ending).astype(jnp.float32)[:, None]
        )
        fresh = jnp.einsum("sh,shp,sn->hpn", toward, scaled, key_block, precision=PRECISE)
        kept = jnp.exp(final) * (ending == previous).astype(jnp.float32)
        memory = memory * kept[:, None, None] + fresh
        return ((memory, ending), within + across)

    start = (jnp.zeros((head_count, channels, states), jnp.float32), jnp.array(-1, jnp.int32))
    pieces = (
        values.reshape(count, block, head_count, channels),
        timesteps.reshape(count, block, head_count),
        key_row_block.reshape(count, block, states),
        query_rows.reshape(count, block, states),
        segment.reshape(count, block),
    )
    folded, outputs = lax.scan(jax.checkpoint(advance), start, pieces)
    return outputs.reshape(total, head_count, channels)


def mixer_core(
    values, raw_steps, step_bias, decay_log, skip_scale, key_row_block, query_rows, segment, block
):
    timesteps = jax.nn.softplus(raw_steps + step_bias[None, :])
    decays = -jnp.exp(decay_log)
    head_count = timesteps.shape[1]
    shaped = values.reshape(values.shape[0], head_count, -1)
    output = state_scan(shaped, timesteps, decays, key_row_block, query_rows, segment, block)
    return (output + skip_scale[None, :, None] * shaped).reshape(values.shape)


def rotary_apply(vectors, direction):
    length_tokens, head_count, columns = vectors.shape
    halfway = columns // 2
    frequency = jnp.exp(
        jnp.arange(halfway, dtype=jnp.float32) * (-2.0 * math.log(ROPE_BASE) / columns)
    )
    angles = jnp.arange(length_tokens, dtype=jnp.float32)[:, None] * frequency[None, :] * direction
    cosine = jnp.cos(angles)[:, None, :]
    sinusoid = jnp.sin(angles)[:, None, :]
    former = vectors[..., :halfway]
    latter = vectors[..., halfway:]
    return jnp.concatenate(
        [former * cosine - latter * sinusoid, latter * cosine + former * sinusoid], -1
    )


def attention_mask(segment, start, rowcount):
    positions = start + jnp.arange(rowcount, dtype=jnp.int32)
    columns = jnp.arange(segment.shape[0], dtype=jnp.int32)
    labels = lax.dynamic_slice_in_dim(segment, start, rowcount)
    return jnp.logical_and(
        columns[None, :] <= positions[:, None], segment[None, :] == labels[:, None]
    )


def general_body(
    block_input,
    segment_ids,
    output_cotangent,
    input_gain,
    inner_weight,
    timestep_weight,
    state_weight,
    query_weight,
    keyvalue_matrix,
    conv_kernel,
    conv_offset,
    timestep_bias,
    decay_log,
    skip_scale,
    gated_gain,
    mamba_down,
    attention_down,
    middle_gain,
    gateup_weight,
    down_weight,
):
    tensor_parallel_rank = lax.axis_index("tp")
    residual = block_input.astype(jnp.float32)
    first_rms = inverse_rms(residual)
    normed = lax.all_gather(
        (residual * first_rms * input_gain).astype(jnp.bfloat16), "tp", axis=0, tiled=True
    )
    (
        inner_full,
        timestep_full,
        state_full,
        query_full,
        keyvalue_full,
        mamba_full,
        attention_full,
        gateup_full,
        down_full,
    ) = (
        lax.all_gather(inner_weight, "fsdp", axis=0, tiled=True),
        lax.all_gather(timestep_weight, "fsdp", axis=0, tiled=True),
        lax.all_gather(state_weight, "fsdp", axis=0, tiled=True),
        lax.all_gather(query_weight, "fsdp", axis=0, tiled=True),
        lax.all_gather(keyvalue_matrix, "fsdp", axis=0, tiled=True),
        lax.all_gather(mamba_down, "fsdp", axis=1, tiled=True),
        lax.all_gather(attention_down, "fsdp", axis=1, tiled=True),
        lax.all_gather(gateup_weight, "fsdp", axis=0, tiled=True),
        lax.all_gather(down_weight, "fsdp", axis=1, tiled=True),
    )
    length_tokens = normed.shape[0]
    local_heads = timestep_full.shape[1]
    local_width = inner_full.shape[2]
    ssm_width = gated_gain.shape[0]
    state_dim = state_full.shape[1] // 2
    query_head_count = query_full.shape[1] // HEAD_SIZE
    head_start = tensor_parallel_rank * local_heads
    width_start = tensor_parallel_rank * local_width
    inner = jnp.einsum("gd,dkc->gkc", normed, inner_full, preferred_element_type=jnp.float32)
    raw_steps = jnp.dot(normed, timestep_full, preferred_element_type=jnp.float32)
    state_proj = jnp.dot(normed, state_full, preferred_element_type=jnp.float32)
    query_proj = jnp.dot(normed, query_full, preferred_element_type=jnp.float32)
    keyvalue_projected = jnp.dot(normed, keyvalue_full, preferred_element_type=jnp.float32)
    gate_half = inner[:, 0]
    local_kernel = jnp.concatenate(
        [
            lax.dynamic_slice_in_dim(conv_kernel, width_start, local_width, 1),
            conv_kernel[:, ssm_width:],
        ],
        1,
    )
    local_offset = jnp.concatenate(
        [
            lax.dynamic_slice_in_dim(conv_offset, width_start, local_width, 0),
            conv_offset[ssm_width:],
        ],
        0,
    )
    local_bias = lax.dynamic_slice_in_dim(timestep_bias, head_start, local_heads, 0)
    local_decay = lax.dynamic_slice_in_dim(decay_log, head_start, local_heads, 0)
    local_skip = lax.dynamic_slice_in_dim(skip_scale, head_start, local_heads, 0)
    local_gain = lax.dynamic_slice_in_dim(gated_gain, width_start, local_width, 0)

    def convolve(signal, kernel, offset):
        return jax.nn.silu(causal_conv(signal, kernel, offset, segment_ids))

    convolved, conv_pullback = jax.vjp(
        convolve, jnp.concatenate([inner[:, 1], state_proj], 1), local_kernel, local_offset
    )
    conv_values = convolved[:, :local_width].astype(jnp.bfloat16)
    conv_states = convolved[:, local_width:].astype(jnp.bfloat16).astype(jnp.float32)

    def scan_heads(values, steps_in, bias_in, decay_in, skip_in, key_rows_in, query_rows_in):
        return mixer_core(
            values,
            steps_in,
            bias_in,
            decay_in,
            skip_in,
            key_rows_in,
            query_rows_in,
            segment_ids,
            SCAN_BLOCK,
        )

    scanned, scan_pullback = jax.vjp(
        scan_heads,
        conv_values.astype(jnp.float32),
        raw_steps,
        local_bias,
        local_decay,
        local_skip,
        conv_states[:, :state_dim],
        conv_states[:, state_dim:],
    )
    silu_gate = jax.nn.silu(gate_half)
    gated = scanned * silu_gate
    gated_low = (gated * local_gain).astype(jnp.bfloat16)
    mamba_partial = jnp.dot(gated_low, mamba_full, preferred_element_type=jnp.float32)
    queries = rotary_apply(
        query_proj.reshape(length_tokens, query_head_count, HEAD_SIZE), 1.0
    ).astype(jnp.bfloat16)
    key_gathered = rotary_apply(
        keyvalue_projected[:, : KEYVALUE_HEADS * HEAD_SIZE].reshape(
            length_tokens, KEYVALUE_HEADS, HEAD_SIZE
        ),
        1.0,
    ).astype(jnp.bfloat16)
    value_gathered = (
        keyvalue_projected[:, KEYVALUE_HEADS * HEAD_SIZE :]
        .reshape(length_tokens, KEYVALUE_HEADS, HEAD_SIZE)
        .astype(jnp.bfloat16)
    )
    owner_ranks = (
        tensor_parallel_rank * query_head_count + jnp.arange(query_head_count, dtype=jnp.int32)
    ) // (QUERY_HEADS // KEYVALUE_HEADS)
    choice_picker = (
        owner_ranks[:, None] == jnp.arange(KEYVALUE_HEADS, dtype=jnp.int32)[None, :]
    ).astype(jnp.bfloat16)
    key_row_block = jnp.einsum(
        "jh,ghd->gjd", choice_picker, key_gathered, preferred_element_type=jnp.float32
    ).astype(jnp.bfloat16)
    value_row_block = jnp.einsum(
        "jh,ghd->gjd", choice_picker, value_gathered, preferred_element_type=jnp.float32
    ).astype(jnp.bfloat16)
    scaling = 1.0 / math.sqrt(HEAD_SIZE)
    block_count = length_tokens // QUERY_BLOCK
    query_blocks = queries.reshape(block_count, QUERY_BLOCK, query_head_count, HEAD_SIZE)
    block_starts = jnp.arange(block_count, dtype=jnp.int32) * QUERY_BLOCK

    def block_scores(query_block, start):
        scores = (
            jnp.einsum(
                "qjd,kjd->jqk", query_block, key_row_block, preferred_element_type=jnp.float32
            )
            * scaling
        )
        allowed = attention_mask(segment_ids, start, QUERY_BLOCK)
        return jnp.where(allowed[None], scores, MASKED_SCORE)

    def forward_block(pieces):
        query_block, start = pieces
        masked = block_scores(query_block, start)
        highest = jnp.max(masked, -1, keepdims=True)
        weights = jnp.exp(masked - highest)
        totals = jnp.sum(weights, -1, keepdims=True)
        probs_low = (weights / totals).astype(jnp.bfloat16)
        result = jnp.einsum(
            "jqk,kjd->qjd", probs_low, value_row_block, preferred_element_type=jnp.float32
        )
        return (result, (highest + jnp.log(totals))[..., 0])

    attended, logsums = lax.map(forward_block, (query_blocks, block_starts))
    attended_low = attended.reshape(length_tokens, query_head_count * HEAD_SIZE).astype(
        jnp.bfloat16
    )
    attention_partial = jnp.dot(attended_low, attention_full, preferred_element_type=jnp.float32)
    square_local = jnp.sum(gated * gated, -1)
    mamba_rows, attention_rows, square_rows = (
        lax.psum_scatter(mamba_partial, "tp", scatter_dimension=0, tiled=True),
        lax.psum_scatter(attention_partial, "tp", scatter_dimension=0, tiled=True),
        lax.psum_scatter(square_local, "tp", scatter_dimension=0, tiled=True),
    )
    norm_factor = lax.rsqrt(square_rows / ssm_width + EPSILON)
    factor_low = norm_factor.astype(jnp.bfloat16)
    factor_own = lax.optimization_barrier(factor_low).astype(jnp.float32)
    middle = residual + (factor_own[:, None] * mamba_rows + attention_rows)
    middle_rms = inverse_rms(middle)
    hidden_in = lax.all_gather(
        (middle * middle_rms * middle_gain).astype(jnp.bfloat16), "tp", axis=0, tiled=True
    )
    gateup = jnp.einsum("gd,dkf->gkf", hidden_in, gateup_full, preferred_element_type=jnp.float32)
    gate_part = gateup[:, 0]
    up_part = gateup[:, 1]
    activated = (jax.nn.silu(gate_part) * up_part).astype(jnp.bfloat16)
    feedforward = lax.psum_scatter(
        jnp.dot(activated, down_full, preferred_element_type=jnp.float32).astype(jnp.bfloat16),
        "tp",
        scatter_dimension=0,
        tiled=True,
    ).astype(jnp.float32)
    block_output = middle + feedforward
    cotangent_all = lax.all_gather(output_cotangent, "tp", axis=0, tiled=True)
    grad_activated = contract_cols(cotangent_all, down_full)
    down_wgrad = contract_rows(activated, cotangent_all)
    gate_sigmoid = jax.nn.sigmoid(gate_part)
    grad_gate_part = (
        grad_activated * up_part * gate_sigmoid * (1.0 + gate_part * (1.0 - gate_sigmoid))
    )
    grad_up_part = grad_activated * jax.nn.silu(gate_part)
    grad_gateup = jnp.stack([grad_gate_part, grad_up_part], 1).astype(jnp.bfloat16)
    gateup_wgrad = jnp.einsum(
        "gd,gkf->dkf", hidden_in, grad_gateup, preferred_element_type=jnp.float32
    )
    grad_hidden = lax.psum_scatter(
        jnp.einsum("gkf,dkf->gd", grad_gateup, gateup_full, preferred_element_type=jnp.float32),
        "tp",
        scatter_dimension=0,
        tiled=True,
    )
    middle_normal = middle * middle_rms
    middle_gain_part = jnp.sum(grad_hidden * middle_normal, 0)
    middle_scaled = grad_hidden * middle_gain
    grad_middle = output_cotangent.astype(jnp.float32) + middle_rms * (
        middle_scaled - middle_normal * jnp.mean(middle_scaled * middle_normal, -1, keepdims=True)
    )
    mix_low = grad_middle.astype(jnp.bfloat16)
    mix_own = mix_low.astype(jnp.float32)
    grad_factor = jnp.sum(mix_own * mamba_rows, -1)
    grad_square = (grad_factor * -0.5 * norm_factor * norm_factor * norm_factor / ssm_width).astype(
        jnp.bfloat16
    )
    mix_all, factor_rows, square_rows_grad = (
        lax.all_gather(mix_low, "tp", axis=0, tiled=True),
        lax.all_gather(factor_low, "tp", axis=0, tiled=True),
        lax.all_gather(grad_square, "tp", axis=0, tiled=True),
    )
    grad_mamba = (factor_rows.astype(jnp.float32)[:, None] * mix_all.astype(jnp.float32)).astype(
        jnp.bfloat16
    )
    mamba_wgrad = contract_rows(gated_low, grad_mamba)
    grad_gated_low = contract_cols(grad_mamba, mamba_full)
    gain_grad = jnp.sum(grad_gated_low * gated, 0)
    grad_gated = (
        grad_gated_low * local_gain + 2.0 * gated * square_rows_grad.astype(jnp.float32)[:, None]
    )
    zsigmoid = jax.nn.sigmoid(gate_half)
    grad_scanned = grad_gated * silu_gate
    grad_gate = grad_gated * scanned * zsigmoid * (1.0 + gate_half * (1.0 - zsigmoid))
    grad_values, grad_steps, grad_bias, grad_decay, grad_skip, grad_keys_in, grad_queries_in = (
        scan_pullback(grad_scanned)
    )
    grad_signal, kernel_local, offset_local = conv_pullback(
        jnp.concatenate([grad_values, grad_keys_in, grad_queries_in], 1)
    )
    attention_wgrad = contract_rows(attended_low, mix_all)
    grad_attended = (
        contract_cols(mix_all, attention_full)
        .astype(jnp.bfloat16)
        .reshape(block_count, QUERY_BLOCK, query_head_count, HEAD_SIZE)
    )

    def backward_block(carry, pieces):
        key_grad, value_grad = carry
        query_block, grad_block, logsum_block, start = pieces
        masked = block_scores(query_block, start)
        probs = jnp.exp(masked - logsum_block[..., None])
        grad_probs = jnp.einsum(
            "qjd,kjd->jqk", grad_block, value_row_block, preferred_element_type=jnp.float32
        )
        inner_sum = jnp.sum(grad_probs * probs, -1, keepdims=True)
        grad_scores = (probs * (grad_probs - inner_sum)).astype(jnp.bfloat16)
        query_grad = (
            jnp.einsum(
                "jqk,kjd->qjd", grad_scores, key_row_block, preferred_element_type=jnp.float32
            )
            * scaling
        )
        key_grad = (
            key_grad
            + jnp.einsum(
                "jqk,qjd->kjd", grad_scores, query_block, preferred_element_type=jnp.float32
            )
            * scaling
        )
        value_grad = value_grad + jnp.einsum(
            "jqk,qjd->kjd",
            probs.astype(jnp.bfloat16),
            grad_block,
            preferred_element_type=jnp.float32,
        )
        return ((key_grad, value_grad), query_grad)

    empty_rows = jnp.zeros((length_tokens, query_head_count, HEAD_SIZE), jnp.float32)
    (key_grad, value_grad), query_grads = lax.scan(
        backward_block,
        (empty_rows, empty_rows),
        (query_blocks, grad_attended, logsums, block_starts),
    )
    query_back = rotary_apply(
        query_grads.reshape(length_tokens, query_head_count, HEAD_SIZE), -1.0
    ).reshape(length_tokens, query_head_count * HEAD_SIZE)
    selector_float = choice_picker.astype(jnp.float32)
    key_returned = rotary_apply(
        jnp.einsum("jh,gjd->ghd", selector_float, key_grad, precision=PRECISE), -1.0
    )
    value_returned = jnp.einsum("jh,gjd->ghd", selector_float, value_grad, precision=PRECISE)
    keyvalue_partial = jnp.concatenate(
        [
            key_returned.reshape(length_tokens, KEYVALUE_HEADS * HEAD_SIZE),
            value_returned.reshape(length_tokens, KEYVALUE_HEADS * HEAD_SIZE),
        ],
        1,
    )
    state_total, keyvalue_total = (
        lax.psum(grad_signal[:, local_width:].astype(jnp.bfloat16), "tp").astype(jnp.float32),
        lax.psum(keyvalue_partial.astype(jnp.bfloat16), "tp").astype(jnp.float32),
    )
    inner_low = jnp.stack([grad_gate, grad_signal[:, :local_width]], 1).astype(jnp.bfloat16)
    steps_low = grad_steps.astype(jnp.bfloat16)
    query_low = query_back.astype(jnp.bfloat16)
    state_low = state_total.astype(jnp.bfloat16)
    keyvalue_low = keyvalue_total.astype(jnp.bfloat16)
    inner_wgrad = jnp.einsum("gd,gkc->dkc", normed, inner_low, preferred_element_type=jnp.float32)
    timestep_wgrad = contract_rows(normed, steps_low)
    state_wgrad = contract_rows(normed, state_low)
    query_wgrad = contract_rows(normed, query_low)
    keyvalue_wgrad = contract_rows(normed, keyvalue_low)
    normed_partial = (
        jnp.einsum("gkc,dkc->gd", inner_low, inner_full, preferred_element_type=jnp.float32)
        + contract_cols(steps_low, timestep_full)
        + contract_cols(query_low, query_full)
    )
    leader = (tensor_parallel_rank == 0).astype(jnp.float32)
    normed_partial = normed_partial + leader * (
        contract_cols(state_low, state_full) + contract_cols(keyvalue_low, keyvalue_full)
    )
    normed_grad = lax.psum_scatter(
        normed_partial.astype(jnp.bfloat16), "tp", scatter_dimension=0, tiled=True
    ).astype(jnp.float32)
    first_normal = residual * first_rms
    input_gain_part = jnp.sum(normed_grad * first_normal, 0)
    first_scaled = normed_grad * input_gain
    input_grad = grad_middle + first_rms * (
        first_scaled - first_normal * jnp.mean(first_scaled * first_normal, -1, keepdims=True)
    )
    gated_part = lax.dynamic_update_slice_in_dim(
        jnp.zeros((ssm_width,), jnp.float32), gain_grad, width_start, 0
    )
    kernel_part = jnp.concatenate(
        [
            lax.dynamic_update_slice_in_dim(
                jnp.zeros((conv_kernel.shape[0], ssm_width), jnp.float32),
                kernel_local[:, :local_width],
                width_start,
                1,
            ),
            kernel_local[:, local_width:],
        ],
        1,
    )
    offset_part = jnp.concatenate(
        [
            lax.dynamic_update_slice_in_dim(
                jnp.zeros((ssm_width,), jnp.float32), offset_local[:local_width], width_start, 0
            ),
            offset_local[local_width:],
        ],
        0,
    )
    head_zeros = jnp.zeros((timestep_bias.shape[0],), jnp.float32)
    bias_part = lax.dynamic_update_slice_in_dim(head_zeros, grad_bias, head_start, 0)
    decay_part = lax.dynamic_update_slice_in_dim(head_zeros, grad_decay, head_start, 0)
    skip_part = lax.dynamic_update_slice_in_dim(head_zeros, grad_skip, head_start, 0)
    summed = lax.psum(
        (
            input_gain_part,
            middle_gain_part,
            kernel_part,
            offset_part,
            bias_part,
            decay_part,
            skip_part,
            gated_part,
        ),
        ("fsdp", "tp"),
    )
    (
        inner_out,
        timestep_out,
        state_out,
        query_out,
        keyvalue_out,
        mamba_out,
        attention_out,
        gateup_out,
        down_out,
    ) = (
        lax.psum_scatter(
            inner_wgrad.astype(jnp.bfloat16), "fsdp", scatter_dimension=0, tiled=True
        ).astype(jnp.float32),
        lax.psum_scatter(
            timestep_wgrad.astype(jnp.bfloat16), "fsdp", scatter_dimension=0, tiled=True
        ).astype(jnp.float32),
        lax.psum_scatter(
            state_wgrad.astype(jnp.bfloat16), "fsdp", scatter_dimension=0, tiled=True
        ).astype(jnp.float32),
        lax.psum_scatter(
            query_wgrad.astype(jnp.bfloat16), "fsdp", scatter_dimension=0, tiled=True
        ).astype(jnp.float32),
        lax.psum_scatter(
            keyvalue_wgrad.astype(jnp.bfloat16), "fsdp", scatter_dimension=0, tiled=True
        ).astype(jnp.float32),
        lax.psum_scatter(
            mamba_wgrad.astype(jnp.bfloat16), "fsdp", scatter_dimension=1, tiled=True
        ).astype(jnp.float32),
        lax.psum_scatter(
            attention_wgrad.astype(jnp.bfloat16), "fsdp", scatter_dimension=1, tiled=True
        ).astype(jnp.float32),
        lax.psum_scatter(
            gateup_wgrad.astype(jnp.bfloat16), "fsdp", scatter_dimension=0, tiled=True
        ).astype(jnp.float32),
        lax.psum_scatter(
            down_wgrad.astype(jnp.bfloat16), "fsdp", scatter_dimension=1, tiled=True
        ).astype(jnp.float32),
    )
    return (
        block_output,
        input_grad,
        summed[0],
        inner_out,
        timestep_out,
        state_out,
        query_out,
        keyvalue_out,
        summed[2],
        summed[3],
        summed[4],
        summed[5],
        summed[6],
        summed[7],
        mamba_out,
        attention_out,
        summed[1],
        gateup_out,
        down_out,
    )


BLOCK = 256
LOG2E = 1.4426950408889634
HIDDEN_BIAS = -1e30


def narrow(values):
    return values.astype(jnp.bfloat16)


def wide(values):
    return values.astype(jnp.float32)


def mm(left, right):
    return jnp.dot(left, right, preferred_element_type=jnp.float32)


def sigmoid(values):
    return 1.0 / (1.0 + jnp.exp(-values))


def dot_wide(ones, values):
    first = narrow(values)
    rest = values - wide(first)
    second = narrow(rest)
    third = narrow(rest - wide(second))
    return mm(ones, first) + mm(ones, second) + mm(ones, third)


def triangle(rows, upper):
    down = lax.broadcasted_iota(jnp.int32, (rows, rows), 0)
    across = lax.broadcasted_iota(jnp.int32, (rows, rows), 1)
    keep = (across >= down) if upper else (down >= across)
    return jnp.where(keep, 1.0, 0.0).astype(jnp.bfloat16)


def pair_bias(label_column, label_row):
    rows = label_column.shape[0]
    down = lax.broadcasted_iota(jnp.int32, (rows, rows), 0)
    across = lax.broadcasted_iota(jnp.int32, (rows, rows), 1)
    keep = jnp.logical_and(label_column == label_row, down >= across)
    return jnp.where(keep, 0.0, HIDDEN_BIAS)


def conv_taps(signal, info):
    taps = [signal]
    for distance in range(1, 4):
        taps.append(pltpu.roll(signal, distance, 0) * info[:, distance : distance + 1])
    return taps


def conv_pre(taps, channel):
    result = channel[4:5, :]
    for distance in range(4):
        result = result + channel[distance : distance + 1, :] * taps[distance]
    return result


def conv_back(grad_pre, channel, info):
    rows = grad_pre.shape[0]
    result = channel[0:1, :] * grad_pre
    for distance in range(1, 4):
        masked = grad_pre * info[:, distance : distance + 1]
        result = result + channel[distance : distance + 1, :] * pltpu.roll(masked, rows - distance, 0)
    return result


def column_of(values, lane):
    lanes = lax.broadcasted_iota(jnp.int32, values.shape, 1)
    return jnp.sum(jnp.where(lanes == lane, values, 0.0), 1, keepdims=True)


def half_lanes(values, which):
    lanes = lax.broadcasted_iota(jnp.int32, values.shape, 1)
    keep = (lanes < HEAD_SIZE) if which == 0 else (lanes >= HEAD_SIZE)
    return jnp.where(keep, values, jnp.zeros_like(values))


def spans(rows):
    return [slice(at, at + BLOCK) for at in range(0, rows, BLOCK)]


def mixer_forward_kernel(
    gate_ref,
    value_ref,
    state_ref,
    steps_ref,
    info_ref,
    label_ref,
    channel_ref,
    state_channel_ref,
    head_ref,
    low_ref,
    scanned_ref,
    square_ref,
    dt_ref,
    cum_ref,
    crossed,
    bias,
    source_rows,
):
    pair = pl.program_id(0)
    info = info_ref[...]
    rows = info.shape[0]

    @pl.when(pair == 0)
    def _():
        taps = conv_taps(state_ref[...], info)
        pre = conv_pre(taps, state_channel_ref[...])
        states = narrow(pre * sigmoid(pre))
        half = states.shape[1] // 2
        crossed[...] = contract_cols(states[:, half:], states[:, :half])
        bias[...] = pair_bias(info[:, 4:5], label_ref[0:1, :])
        raw = steps_ref[...] + head_ref[0:1, :]
        dt = jnp.maximum(raw, 0.0) + jnp.log1p(jnp.exp(-jnp.abs(raw)))
        cum = dot_wide(triangle(rows, False), dt * (head_ref[1:2, :] * LOG2E))
        dt_ref[...] = dt
        cum_ref[...] = cum
        source_rows[...] = (cum - jnp.log(dt) * LOG2E).T
        square_ref[...] = jnp.zeros_like(square_ref)

    channel = channel_ref[...]
    pre = conv_pre(conv_taps(value_ref[...], info), channel)
    values = narrow(pre * sigmoid(pre))
    outputs = [channel[5:6, :] * wide(values[span]) for span in spans(rows)]
    for which in range(2):
        head = 2 * pair + which
        target = column_of(cum_ref[...], head)
        source = source_rows[pl.ds(head, 1), :]
        chosen = half_lanes(values, which)
        for i, down in enumerate(spans(rows)):
            for across in spans(rows)[: i + 1]:
                weights = jnp.exp2((target[down] - source[:, across]) + bias[down, across])
                outputs[i] += mm(narrow(weights * crossed[down, across]), chosen[across])
    scanned = jnp.concatenate(outputs, 0)
    scanned_ref[...] = scanned
    gate = gate_ref[...]
    gated = scanned * (gate * sigmoid(gate))
    low_ref[...] = narrow(gated * channel[6:7, :])
    square_ref[...] += gated * gated


def mixer_backward_kernel(
    gate_ref,
    value_ref,
    state_ref,
    steps_ref,
    info_ref,
    label_ref,
    channel_ref,
    state_channel_ref,
    head_ref,
    scanned_ref,
    incoming_ref,
    dt_ref,
    cum_ref,
    grad_value_ref,
    grad_state_ref,
    grad_steps_ref,
    channel_grad_ref,
    state_grad_ref,
    head_grad_ref,
    crossed,
    bias,
    summed,
    states_low,
    source_rows,
    dt_rows,
    target_sums,
    source_sums,
):
    pair = pl.program_id(0)
    info = info_ref[...]
    rows = info.shape[0]
    half = state_ref.shape[1] // 2

    @pl.when(pair == 0)
    def _():
        pre = conv_pre(conv_taps(state_ref[...], info), state_channel_ref[...])
        states = narrow(pre * sigmoid(pre))
        states_low[...] = states
        crossed[...] = contract_cols(states[:, half:], states[:, :half])
        bias[...] = pair_bias(info[:, 4:5], label_ref[0:1, :])
        source_rows[...] = cum_ref[...].T
        dt_rows[...] = dt_ref[...].T
        summed[...] = jnp.zeros_like(summed)
        target_sums[...] = jnp.zeros_like(target_sums)
        source_sums[...] = jnp.zeros_like(source_sums)

    channel = channel_ref[...]
    taps = conv_taps(value_ref[...], info)
    pre = conv_pre(taps, channel)
    opened = sigmoid(pre)
    values = narrow(pre * opened)
    gate = gate_ref[...]
    gate_open = sigmoid(gate)
    silu_gate = gate * gate_open
    scanned = scanned_ref[...]
    gated = scanned * silu_gate
    incoming = incoming_ref[...]
    gain_grad = jnp.sum(incoming * gated, 0, keepdims=True)
    grad_gated = incoming * channel[6:7, :] + 2.0 * gated * info[:, 5:6]
    grad_scanned = grad_gated * silu_gate
    skip_grad = jnp.sum(grad_scanned * wide(values), 0, keepdims=True)
    low_grad = narrow(grad_scanned)
    value_grads = [channel[5:6, :] * grad_scanned[span] for span in spans(rows)]
    lanes = lax.broadcasted_iota(jnp.int32, (BLOCK, 128), 1)
    for which in range(2):
        head = 2 * pair + which
        target = column_of(cum_ref[...], head)
        dt_column = column_of(dt_ref[...], head)
        source = source_rows[pl.ds(head, 1), :]
        dt_row = dt_rows[pl.ds(head, 1), :]
        chosen = half_lanes(low_grad, which)
        returned = [jnp.zeros((BLOCK, 128), jnp.float32) for _ in spans(rows)]
        column_sums = [jnp.zeros((1, BLOCK), jnp.float32) for _ in spans(rows)]
        for i, down in enumerate(spans(rows)):
            row_sum = jnp.zeros((BLOCK, 1), jnp.float32)
            for j, across in enumerate(spans(rows)[: i + 1]):
                decay = jnp.exp2((target[down] - source[:, across]) + bias[down, across])
                linked = crossed[down, across]
                returned[j] += contract_rows(narrow(decay * linked), chosen[down])
                reach = decay * contract_cols(chosen[down], values[across])
                scaled = reach * dt_row[:, across]
                summed[down, across] += scaled
                column_sums[j] += jnp.sum(reach * linked, 0, keepdims=True)
                row_sum += jnp.sum(scaled * linked, 1, keepdims=True)
            target_sums[down, :] += jnp.where(lanes == head, row_sum, 0.0)
        for j, across in enumerate(spans(rows)):
            value_grads[j] += dt_column[across] * returned[j]
            source_sums[pl.ds(head, 1), across] = column_sums[j]
    grad_pre = jnp.concatenate(value_grads, 0) * (opened * (1.0 + pre * (1.0 - opened)))
    grad_value_ref[...] = narrow(conv_back(grad_pre, channel, info))
    channel_grad_ref[...] = jnp.concatenate(
        [jnp.sum(grad_pre * tap, 0, keepdims=True) for tap in taps]
        + [jnp.sum(grad_pre, 0, keepdims=True), skip_grad, gain_grad, jnp.zeros_like(gain_grad)],
        0,
    )

    @pl.when(pair == pl.num_programs(0) - 1)
    def _():
        low = narrow(summed[...])
        states = states_low[...]
        grad_keys = contract_rows(low, states[:, half:])
        grad_queries = mm(low, states[:, :half])
        state_channel = state_channel_ref[...]
        state_taps = conv_taps(state_ref[...], info)
        state_pre = conv_pre(state_taps, state_channel)
        state_open = sigmoid(state_pre)
        grad_state_pre = jnp.concatenate([grad_keys, grad_queries], 1) * (
            state_open * (1.0 + state_pre * (1.0 - state_open))
        )
        grad_state_ref[...] = narrow(conv_back(grad_state_pre, state_channel, info))
        state_grad_ref[...] = jnp.concatenate(
            [jnp.sum(grad_state_pre * tap, 0, keepdims=True) for tap in state_taps]
            + [jnp.sum(grad_state_pre, 0, keepdims=True)]
            + [jnp.zeros((3, 2 * half), jnp.float32)],
            0,
        )
        dt = dt_ref[...]
        rate = head_ref[1:2, :]
        source_columns = source_sums[...].T
        grad_rate = dot_wide(triangle(rows, True), target_sums[...] - dt * source_columns)
        grad_dt = source_columns + rate * grad_rate
        grad_steps = grad_dt * sigmoid(steps_ref[...] + head_ref[0:1, :])
        grad_steps_ref[...] = narrow(grad_steps)
        head_grad_ref[...] = jnp.concatenate(
            [
                jnp.sum(grad_steps, 0, keepdims=True),
                jnp.sum(grad_rate * dt * rate, 0, keepdims=True),
                jnp.zeros((6, 128), jnp.float32),
            ],
            0,
        )


def copies_of(starts_ref, pieces, whole, done, column=0):
    rows = pieces[0].shape[0]
    width = whole.shape[1]
    copies = []
    for at, piece in enumerate(pieces):
        start = pl.multiple_of(starts_ref[at] * rows, rows)
        copies.append(
            pltpu.make_async_copy(
                piece.at[:, column : column + width], whole.at[pl.ds(start, rows)], done.at[at]
            )
        )
    for copy in copies:
        copy.start()
    return copies


def wait_all(copies):
    for copy in copies:
        copy.wait()


def smem():
    return pl.BlockSpec(memory_space=pltpu.SMEM)


def vmem():
    return pl.BlockSpec(memory_space=pltpu.VMEM)


def hbm():
    return pl.BlockSpec(memory_space=pltpu.HBM)


def rotated(values, cosine, sinusoid):
    lanes = lax.broadcasted_iota(jnp.int32, values.shape, 1)
    quarter = HEAD_SIZE // 2
    swapped = jnp.where(
        lanes % HEAD_SIZE < quarter,
        pltpu.roll(values, values.shape[1] - quarter, 1),
        pltpu.roll(values, quarter, 1),
    )
    return values * cosine + swapped * sinusoid


def attention_forward_kernel(
    count,
    query_width,
    rank_ref,
    starts_ref,
    normed_ref,
    info_ref,
    label_ref,
    cosine_ref,
    sinusoid_ref,
    gated_ref,
    factor_ref,
    *refs,
):
    pieces = refs[:count]
    attended_ref, turned_ref, key_ref, value_ref, logsum_ref, mamba_ref, mixed_ref = refs[count:-4]
    bias, projected, whole, done = refs[-4:]
    copies = copies_of(starts_ref, pieces, whole, done)
    rows = normed_ref.shape[0]
    cosine, sinusoid = cosine_ref[...], sinusoid_ref[...]
    bias[...] = pair_bias(info_ref[:, 4:5], label_ref[0:1, :])
    wait_all(copies)
    end = projected.shape[1]
    for at in range(0, end, 256):
        projected[:, at : at + 256] = mm(normed_ref[...], whole[:, at : at + 256])
    lanes = lax.broadcasted_iota(jnp.int32, (rows, 128), 1)
    own = (lanes < HEAD_SIZE) == (rank_ref[0] == 0)

    def doubled(values):
        return jnp.where(own, values, pltpu.roll(values, HEAD_SIZE, 1))

    middle = query_width + 128
    keys = narrow(doubled(rotated(projected[:, query_width:middle], cosine, sinusoid)))
    values = narrow(doubled(projected[:, middle : middle + 128]))
    key_ref[...] = keys
    value_ref[...] = values
    scaling = 1.0 / math.sqrt(HEAD_SIZE)
    logsums = [jnp.zeros((BLOCK, 128), jnp.float32) for _ in spans(rows)]
    block_lanes = lax.broadcasted_iota(jnp.int32, (BLOCK, 128), 1)
    for pair in range(query_width // 128):
        columns = slice(128 * pair, 128 * pair + 128)
        queries = narrow(rotated(projected[:, columns], cosine, sinusoid))
        turned_ref[:, columns] = queries
        results = [jnp.zeros((BLOCK, 128), jnp.float32) for _ in spans(rows)]
        for which in range(2):
            chosen = half_lanes(queries, which)
            reading = half_lanes(values, which)
            for i, down in enumerate(spans(rows)):
                width = BLOCK * (i + 1)
                scores = contract_cols(chosen[down], keys[:width]) * scaling + bias[down, :width]
                highest = jnp.max(scores, 1, keepdims=True)
                weights = jnp.exp(scores - highest)
                total = jnp.sum(weights, 1, keepdims=True)
                results[i] += mm(narrow(weights * (1.0 / total)), reading[:width])
                logsums[i] = jnp.where(
                    block_lanes == 2 * pair + which, highest + jnp.log(total), logsums[i]
                )
        for i, down in enumerate(spans(rows)):
            attended_ref[down, columns] = narrow(results[i])
    for i, down in enumerate(spans(rows)):
        logsum_ref[down, :] = logsums[i]
    gated_end = end + gated_ref.shape[1]
    for at in range(0, whole.shape[0], 256):
        span = slice(at, at + 256)
        mamba = contract_cols(gated_ref[...], whole[span, end:gated_end])
        mamba_ref[:, span] = narrow(mamba)
        part = contract_cols(attended_ref[...], whole[span, gated_end:])
        mixed_ref[:, span] = narrow(factor_ref[...] * mamba + part)


def attention_backward_kernel(
    count,
    column,
    rank_ref,
    starts_ref,
    mix_ref,
    turned_ref,
    key_ref,
    value_ref,
    logsum_ref,
    info_ref,
    label_ref,
    cosine_ref,
    sinusoid_ref,
    *refs,
):
    pieces = refs[:count]
    grad_query_ref, grad_keyvalue_ref, bias, down, done = refs[count:]
    copies = copies_of(starts_ref, pieces, down, done, column)
    rows = turned_ref.shape[0]
    cosine, sinusoid = cosine_ref[...], sinusoid_ref[...]
    bias[...] = pair_bias(info_ref[:, 4:5], label_ref[0:1, :])
    keys, values = key_ref[...], value_ref[...]
    wait_all(copies)
    grad_attended = narrow(mm(mix_ref[...], down[...]))
    scaling = 1.0 / math.sqrt(HEAD_SIZE)
    zero = jnp.zeros((BLOCK, 128), jnp.float32)
    key_grads = [zero for _ in spans(rows)]
    value_grads = [zero for _ in spans(rows)]
    for pair in range(turned_ref.shape[1] // 128):
        columns = slice(128 * pair, 128 * pair + 128)
        query_grads = [zero for _ in spans(rows)]
        for which in range(2):
            queries = half_lanes(turned_ref[:, columns], which)
            incoming = half_lanes(grad_attended[:, columns], which)
            reading = half_lanes(keys, which)
            head = 2 * pair + which
            for i, down in enumerate(spans(rows)):
                width = BLOCK * (i + 1)
                scores = contract_cols(queries[down], keys[:width]) * scaling + bias[down, :width]
                probs = jnp.exp(scores - logsum_ref[down, head : head + 1])
                grad_probs = contract_cols(incoming[down], values[:width])
                inner_sum = jnp.sum(grad_probs * probs, 1, keepdims=True)
                grad_scores = narrow(probs * (grad_probs - inner_sum))
                probs_low = narrow(probs)
                query_grads[i] += mm(grad_scores, reading[:width])
                for j, across in enumerate(spans(rows)[: i + 1]):
                    key_grads[j] += contract_rows(grad_scores[:, across], queries[down])
                    value_grads[j] += contract_rows(probs_low[:, across], incoming[down])
        grad_query_ref[:, columns] = narrow(
            rotated(jnp.concatenate(query_grads, 0) * scaling, cosine, -sinusoid)
        )
    lanes = lax.broadcasted_iota(jnp.int32, (rows, 128), 1)
    own = (lanes < HEAD_SIZE) == (rank_ref[0] == 0)

    def placed(values):
        return jnp.where(own, values + pltpu.roll(values, HEAD_SIZE, 1), 0.0)

    key_grad = rotated(placed(jnp.concatenate(key_grads, 0) * scaling), cosine, -sinusoid)
    grad_keyvalue_ref[:, :128] = narrow(key_grad)
    grad_keyvalue_ref[:, 128:] = narrow(placed(jnp.concatenate(value_grads, 0)))


def block_spec(shape, index):
    return pl.BlockSpec(shape, index)


def fixed(array):
    return pl.BlockSpec(array.shape, lambda p: (0, 0))


def params():
    return pltpu.CompilerParams(vmem_limit_bytes=62 * 1024 * 1024)


def mixer_forward(projected, widths, info, labels, channel, state_channel, heads):
    rows = info.shape[0]
    width, state_at, steps_at = widths
    pairs = width // 128
    state_width = state_channel.shape[1]
    column = lambda p: (0, p)
    return pl.pallas_call(
        mixer_forward_kernel,
        grid=(pairs,),
        in_specs=[
            block_spec((rows, 128), column),
            block_spec((rows, 128), lambda p: (0, pairs + p)),
            block_spec((rows, state_width), lambda p: (0, state_at // state_width)),
            block_spec((rows, 128), lambda p: (0, steps_at // 128)),
            fixed(info),
            fixed(labels),
            block_spec((8, 128), column),
            fixed(state_channel),
            fixed(heads),
        ],
        out_specs=[
            block_spec((rows, 128), column),
            block_spec((rows, 128), column),
            block_spec((rows, 128), lambda p: (0, 0)),
            block_spec((rows, 128), lambda p: (0, 0)),
            block_spec((rows, 128), lambda p: (0, 0)),
        ],
        out_shape=[
            jax.ShapeDtypeStruct((rows, width), jnp.bfloat16),
            jax.ShapeDtypeStruct((rows, width), jnp.float32),
            jax.ShapeDtypeStruct((rows, 128), jnp.float32),
            jax.ShapeDtypeStruct((rows, 128), jnp.float32),
            jax.ShapeDtypeStruct((rows, 128), jnp.float32),
        ],
        scratch_shapes=[
            pltpu.VMEM((rows, rows), jnp.float32),
            pltpu.VMEM((rows, rows), jnp.float32),
            pltpu.VMEM((128, rows), jnp.float32),
        ],
        compiler_params=params(),
        cost_estimate=pl.CostEstimate(flops=1, bytes_accessed=1, transcendentals=0),
        name="mixer_forward",
    )(projected, projected, projected, projected, info, labels, channel, state_channel, heads)


def mixer_backward(
    projected, widths, info, labels, channel, state_channel, heads, scanned, incoming, dt, cum
):
    rows = info.shape[0]
    width, state_at, steps_at = widths
    pairs = width // 128
    state_width = state_channel.shape[1]
    column = lambda p: (0, p)
    still = lambda p: (0, 0)
    return pl.pallas_call(
        mixer_backward_kernel,
        grid=(pairs,),
        in_specs=[
            block_spec((rows, 128), column),
            block_spec((rows, 128), lambda p: (0, pairs + p)),
            block_spec((rows, state_width), lambda p: (0, state_at // state_width)),
            block_spec((rows, 128), lambda p: (0, steps_at // 128)),
            fixed(info),
            fixed(labels),
            block_spec((8, 128), column),
            fixed(state_channel),
            fixed(heads),
            block_spec((rows, 128), column),
            block_spec((rows, 128), column),
            fixed(dt),
            fixed(cum),
        ],
        out_specs=[
            block_spec((rows, 128), column),
            block_spec((rows, state_width), still),
            block_spec((rows, 128), still),
            block_spec((8, 128), column),
            block_spec((8, state_width), still),
            block_spec((8, 128), still),
        ],
        out_shape=[
            jax.ShapeDtypeStruct((rows, width), jnp.bfloat16),
            jax.ShapeDtypeStruct((rows, state_width), jnp.bfloat16),
            jax.ShapeDtypeStruct((rows, 128), jnp.bfloat16),
            jax.ShapeDtypeStruct((8, width), jnp.float32),
            jax.ShapeDtypeStruct((8, state_width), jnp.float32),
            jax.ShapeDtypeStruct((8, 128), jnp.float32),
        ],
        scratch_shapes=[
            pltpu.VMEM((rows, rows), jnp.float32),
            pltpu.VMEM((rows, rows), jnp.float32),
            pltpu.VMEM((rows, rows), jnp.float32),
            pltpu.VMEM((rows, state_width), jnp.bfloat16),
            pltpu.VMEM((128, rows), jnp.float32),
            pltpu.VMEM((128, rows), jnp.float32),
            pltpu.VMEM((rows, 128), jnp.float32),
            pltpu.VMEM((128, rows), jnp.float32),
        ],
        compiler_params=params(),
        cost_estimate=pl.CostEstimate(flops=1, bytes_accessed=1, transcendentals=0),
        name="mixer_backward",
    )(
        projected,
        projected,
        projected,
        projected,
        info,
        labels,
        channel,
        state_channel,
        heads,
        scanned,
        incoming,
        dt,
        cum,
    )


def attention_forward(
    rank, starts, normed, info, labels, cosine, sinusoid, gated, factor, pieces, query_width
):
    rows, model = normed.shape
    count = len(pieces)
    columns = pieces[0].shape[1]
    end = columns - gated.shape[1] - query_width
    arrays = (normed, info, labels, cosine, sinusoid, gated, factor)
    return pl.pallas_call(
        lambda *refs: attention_forward_kernel(count, query_width, *refs),
        in_specs=[smem(), smem()] + [vmem()] * len(arrays) + [hbm()] * count,
        out_specs=[vmem()] * 7,
        out_shape=[
            jax.ShapeDtypeStruct((rows, query_width), jnp.bfloat16),
            jax.ShapeDtypeStruct((rows, query_width), jnp.bfloat16),
            jax.ShapeDtypeStruct((rows, 128), jnp.bfloat16),
            jax.ShapeDtypeStruct((rows, 128), jnp.bfloat16),
            jax.ShapeDtypeStruct((rows, 128), jnp.float32),
            jax.ShapeDtypeStruct((rows, model), jnp.bfloat16),
            jax.ShapeDtypeStruct((rows, model), jnp.bfloat16),
        ],
        scratch_shapes=[
            pltpu.VMEM((rows, rows), jnp.float32),
            pltpu.VMEM((rows, end), jnp.float32),
            pltpu.VMEM((model, columns), jnp.bfloat16),
            pltpu.SemaphoreType.DMA((count,)),
        ],
        compiler_params=params(),
        cost_estimate=pl.CostEstimate(flops=1, bytes_accessed=1, transcendentals=0),
        name="attention_forward",
    )(rank, starts, *arrays, *pieces)


def attention_backward(
    rank, starts, mix, turned, keys, values, logsum, info, labels, cosine, sinusoid, pieces, column
):
    rows, query_width = turned.shape
    count = len(pieces)
    model = mix.shape[1]
    arrays = (mix, turned, keys, values, logsum, info, labels, cosine, sinusoid)
    return pl.pallas_call(
        lambda *refs: attention_backward_kernel(count, column, *refs),
        in_specs=[smem(), smem()] + [vmem()] * len(arrays) + [hbm()] * count,
        out_specs=[vmem()] * 2,
        out_shape=[
            jax.ShapeDtypeStruct((rows, query_width), jnp.bfloat16),
            jax.ShapeDtypeStruct((rows, 256), jnp.bfloat16),
        ],
        scratch_shapes=[
            pltpu.VMEM((rows, rows), jnp.float32),
            pltpu.VMEM((model, query_width), jnp.bfloat16),
            pltpu.SemaphoreType.DMA((count,)),
        ],
        compiler_params=params(),
        cost_estimate=pl.CostEstimate(flops=1, bytes_accessed=1, transcendentals=0),
        name="attention_backward",
    )(rank, starts, *arrays, *pieces)


def project_kernel(count, starts_ref, input_ref, gain_ref, *refs):
    pieces, out_ref, normed_ref, whole, done = refs[:count], *refs[count:]
    copies = copies_of(starts_ref, pieces, whole, done)
    residual = wide(input_ref[...])
    normed_ref[...] = narrow(residual * inverse_rms(residual) * gain_ref[...])
    wait_all(copies)
    left = normed_ref[...]
    columns = out_ref.shape[1]
    for at in range(0, columns, 256):
        span = slice(at, min(at + 256, columns))
        out_ref[:, span] = mm(left, whole[:, span])


def project(starts, pieces, left, gain):
    count = len(pieces)
    rows, columns = pieces[0].shape
    return pl.pallas_call(
        lambda *refs: project_kernel(count, *refs),
        in_specs=[
            pl.BlockSpec(memory_space=pltpu.SMEM),
            pl.BlockSpec(memory_space=pltpu.VMEM),
            pl.BlockSpec(memory_space=pltpu.VMEM),
        ]
        + [pl.BlockSpec(memory_space=pltpu.HBM)] * count,
        out_specs=[pl.BlockSpec(memory_space=pltpu.VMEM)] * 2,
        out_shape=[
            jax.ShapeDtypeStruct((left.shape[0], columns), jnp.float32),
            jax.ShapeDtypeStruct(left.shape, jnp.bfloat16),
        ],
        scratch_shapes=[
            pltpu.VMEM((count * rows, columns), jnp.bfloat16),
            pltpu.SemaphoreType.DMA((count,)),
        ],
        compiler_params=params(),
        cost_estimate=pl.CostEstimate(flops=1, bytes_accessed=1, transcendentals=0),
        name="project",
    )(starts, left, gain, *pieces)


def back_kernel(count, parts, starts_ref, *refs):
    lefts, pieces = refs[:parts], refs[parts : parts + 2 * count]
    out_ref, whole, shared, done, shared_done = refs[-5:]
    copies = copies_of(starts_ref, pieces[:count], whole, done)
    copies += copies_of(starts_ref, pieces[count:], shared, shared_done)
    wait_all(copies)
    model = whole.shape[0]
    for at in range(0, model, 256):
        span = slice(at, at + 256)
        total = jnp.zeros((out_ref.shape[0], 256), jnp.float32)
        for weight, several in ((whole, lefts[:-2]), (shared, lefts[-2:])):
            column = 0
            for left in several:
                total += contract_cols(left[...], weight[span, column : column + left.shape[1]])
                column += left.shape[1]
        out_ref[:, span] = narrow(total)


def back_project(starts, pieces, shared_pieces, lefts):
    count = len(pieces)
    rows, columns = pieces[0].shape
    shared = lefts[-2].shape[1] + lefts[-1].shape[1]
    parts = len(lefts)
    tokens = lefts[0].shape[0]
    return pl.pallas_call(
        lambda *refs: back_kernel(count, parts, *refs),
        in_specs=[smem()] + [vmem()] * parts + [hbm()] * (2 * count),
        out_specs=vmem(),
        out_shape=jax.ShapeDtypeStruct((tokens, count * rows), jnp.bfloat16),
        scratch_shapes=[
            pltpu.VMEM((count * rows, columns), jnp.bfloat16),
            pltpu.VMEM((count * rows, shared), jnp.bfloat16),
            pltpu.SemaphoreType.DMA((count,)),
            pltpu.SemaphoreType.DMA((count,)),
        ],
        compiler_params=params(),
        cost_estimate=pl.CostEstimate(flops=1, bytes_accessed=1, transcendentals=0),
        name="back_project",
    )(starts, *lefts, *pieces, *shared_pieces)


def feed_kernel(
    count, hidden, starts_ref, residual_ref, mixed_ref, far_ref, gain_ref, cotangent_ref, *refs
):
    pieces = refs[:count]
    middle_ref, input_ref, activated_ref, grad_ref, low_ref, forward_ref, whole, done = refs[count:]
    copies = copies_of(starts_ref, pieces, whole, done)
    middle = wide(residual_ref[...]) + (wide(mixed_ref[...]) + wide(far_ref[...]))
    middle_ref[...] = middle
    input_ref[...] = narrow(middle * inverse_rms(middle) * gain_ref[...])
    wait_all(copies)

    def tile(step, carry):
        at = pl.multiple_of(step * 256, 256)
        far = pl.multiple_of(hidden + step * 256, 256)
        last = pl.multiple_of(2 * hidden + step * 256, 256)
        gate = mm(input_ref[...], whole[:, pl.ds(at, 256)])
        up = mm(input_ref[...], whole[:, pl.ds(far, 256)])
        grad = mm(cotangent_ref[...], whole[:, pl.ds(last, 256)])
        opened = sigmoid(gate)
        silu = gate * opened
        activated_ref[:, pl.ds(at, 256)] = narrow(silu * up)
        grad_ref[:, pl.ds(far, 256)] = narrow(grad * silu)
        grad_ref[:, pl.ds(at, 256)] = narrow(grad * up * opened * (1.0 + gate * (1.0 - opened)))
        return carry

    lax.fori_loop(0, hidden // 256, tile, 0)
    model = whole.shape[0]
    for at in range(0, model, 256):
        span = slice(at, at + 256)
        low_ref[:, span] = narrow(contract_cols(grad_ref[...], whole[span, : 2 * hidden]))
    for at in range(0, model, 256):
        span = slice(at, at + 256)
        forward_ref[:, span] = narrow(contract_cols(activated_ref[...], whole[span, 2 * hidden :]))


def feed_forward(starts, pieces, hidden, residual, mixed, far, gain, cotangent):
    count = len(pieces)
    rows, columns = pieces[0].shape
    tokens, model = residual.shape
    return pl.pallas_call(
        lambda *refs: feed_kernel(count, hidden, *refs),
        in_specs=[smem()] + [vmem()] * 5 + [hbm()] * count,
        out_specs=[vmem()] * 6,
        out_shape=[
            jax.ShapeDtypeStruct((tokens, model), jnp.float32),
            jax.ShapeDtypeStruct((tokens, model), jnp.bfloat16),
            jax.ShapeDtypeStruct((tokens, hidden), jnp.bfloat16),
            jax.ShapeDtypeStruct((tokens, 2 * hidden), jnp.bfloat16),
            jax.ShapeDtypeStruct((tokens, model), jnp.bfloat16),
            jax.ShapeDtypeStruct((tokens, model), jnp.bfloat16),
        ],
        scratch_shapes=[
            pltpu.VMEM((count * rows, columns), jnp.bfloat16),
            pltpu.SemaphoreType.DMA((count,)),
        ],
        compiler_params=params(),
        cost_estimate=pl.CostEstimate(flops=1, bytes_accessed=1, transcendentals=0),
        name="feed_forward",
    )(starts, residual, mixed, far, gain, cotangent, *pieces)


def gate_kernel(
    count,
    column,
    starts_ref,
    grad_mamba_ref,
    gate_ref,
    scanned_ref,
    gain_ref,
    square_ref,
    turned_ref,
    *refs,
):
    pieces = refs[:count]
    incoming_ref, grad_ref, far_ref, line_ref, own_ref, weight, done = refs[count:]
    copies = copies_of(starts_ref, pieces, weight, done, column)
    gate = gate_ref[...]
    opened = sigmoid(gate)
    scanned = scanned_ref[...]
    wait_all(copies)
    incoming = mm(grad_mamba_ref[...], weight[...])
    incoming_ref[...] = incoming
    grad_gated = incoming * gain_ref[...] + 2.0 * scanned * (gate * opened) * square_ref[...]
    grad_ref[...] = narrow(grad_gated * scanned * opened * (1.0 + gate * (1.0 - opened)))
    grads_kernel(turned_ref[...], [grad_ref], far_ref, line_ref, own_ref, 0)


def gate_backward(starts, grad_mamba, projected, scanned, gain, square, turned, pieces, column):
    rows, width = scanned.shape
    model = turned.shape[0]
    count = len(pieces)
    still = lambda p: (0, 0)
    return pl.pallas_call(
        lambda *refs: gate_kernel(count, column, *refs),
        grid=(1,),
        in_specs=[
            smem(),
            fixed(grad_mamba),
            block_spec((rows, width), still),
            fixed(scanned),
            fixed(gain),
            fixed(square),
            fixed(turned),
        ]
        + [hbm()] * count,
        out_specs=[
            block_spec((rows, width), still),
            block_spec((rows, width), still),
            block_spec((model // 2, width), still),
            block_spec((model // 4, width), still),
            block_spec((model // 4, width), still),
        ],
        out_shape=[
            jax.ShapeDtypeStruct((rows, width), jnp.float32),
            jax.ShapeDtypeStruct((rows, width), jnp.bfloat16),
            jax.ShapeDtypeStruct((model // 2, width), jnp.bfloat16),
            jax.ShapeDtypeStruct((model // 4, width), jnp.bfloat16),
            jax.ShapeDtypeStruct((model // 4, width), jnp.bfloat16),
        ],
        scratch_shapes=[
            pltpu.VMEM((model, width), jnp.bfloat16),
            pltpu.SemaphoreType.DMA((count,)),
        ],
        compiler_params=params(),
        cost_estimate=pl.CostEstimate(flops=1, bytes_accessed=1, transcendentals=0),
        name="gate_backward",
    )(starts, grad_mamba, projected, scanned, gain, square, turned, *pieces)


def swaps(size, bit):
    return [(i, i ^ bit) for i in range(size)]


def ring(size):
    return [(i, (i + 4) % size) for i in range(size)]


def tie(*values):
    return lax.optimization_barrier(values)


class Gathering:
    def __init__(self, shards, size):
        self.size = size
        self.held = {(group, 0): shard for group, shard in enumerate(shards)}
        self.lined, self.crossed, self.flying = {}, {}, {}

    def step(self, begun, awaited, main):
        def send(value, pairs):
            return lax.ppermute(value, "fsdp", pairs)

        for kind, group, k in begun:
            if kind == "z":
                value = send(self.held[group, k - 1], ring(self.size))
            elif kind == "r":
                value = send(self.held[group, 0], [(j, i) for i, j in ring(self.size)])
            elif kind == "x":
                value = send(self.held[group, k], swaps(self.size, 2))
            else:
                self.crossed[group, k] = [
                    send(self.held[group, k], swaps(self.size, 1)),
                    send(self.lined[group, k], swaps(self.size, 1)),
                ]
                continue
            self.flying[kind, group, k] = value
        values = main()
        self.held, landed, values = lax.optimization_barrier(
            (self.held, [self.flying.pop(key) for key in awaited], values)
        )
        for (kind, group, k), value in zip(awaited, landed):
            (self.lined if kind == "x" else self.held)[group, k] = value
        return values

    def pieces(self, group):
        return [
            piece
            for k in range(self.size // 4)
            for piece in (
                self.held[group, k],
                self.crossed[group, k][0],
                self.lined[group, k],
                self.crossed[group, k][1],
            )
        ]


def grads_kernel(turned, rights, far_ref, line_ref, own_ref, column):
    half = turned.shape[0] // 2
    quarter = half // 2
    for right in rights:
        width = right.shape[1]
        for at in range(0, width, 256):
            size = min(256, width - at)
            product = narrow(mm(turned, right[:, at : at + size]))
            span = slice(column + at, column + at + size)
            far_ref[:, span] = product[half:]
            line_ref[:, span] = product[quarter:half]
            own_ref[:, span] = product[:quarter]
        column += width
    return column


def last_kernel(turned_ref, *refs):
    grads_kernel(turned_ref[...], refs[:-3], *refs[-3:], 0)


def feed_grads_kernel(order_ref, turned_ref, input_ref, activated_ref, grad_ref, *outs):
    column = grads_kernel(turned_ref[...], [activated_ref], *outs, 0)
    turned = narrow(contract_cols(order_ref[...], input_ref[...]))
    grads_kernel(turned, [grad_ref], *outs, column)


def second_kernel(
    order_ref, mix_ref, factor_ref, normed_ref, gated_ref, attended_ref, query_ref, key_ref, *outs
):
    turned = narrow(contract_cols(order_ref[...], mix_ref[...]))
    mamba = narrow(factor_ref[...] * wide(turned))
    column = grads_kernel(mamba, [gated_ref], *outs, 0)
    column = grads_kernel(turned, [attended_ref], *outs, column)
    grads_kernel(normed_ref[...], [query_ref, key_ref], *outs, column)


def weight_grads(kernel, arrays, model, columns, name):
    return pl.pallas_call(
        kernel,
        in_specs=[vmem()] * len(arrays),
        out_specs=[vmem()] * 3,
        out_shape=[
            jax.ShapeDtypeStruct((rows, columns), jnp.bfloat16)
            for rows in (model // 2, model // 4, model // 4)
        ],
        compiler_params=params(),
        cost_estimate=pl.CostEstimate(flops=1, bytes_accessed=1, transcendentals=0),
        name=name,
    )(*arrays)


def send_core(far, size):
    return lax.ppermute(far, "fsdp", swaps(size, 1))


def send_line(line, size):
    return lax.ppermute(line, "fsdp", swaps(size, 2))


def send_ring(total, size):
    return lax.ppermute(total, "fsdp", ring(size))


def add_core(came, line, own):
    half = own.shape[0]
    return narrow(wide(line) + wide(came[half:])), narrow(wide(own) + wide(came[:half]))


def add_line(came, own, size):
    return narrow(wide(own) + wide(came)).reshape(size // 4, -1, own.shape[1])


def add_ring(parts, came, step):
    total = wide(parts[(step + 1) % parts.shape[0]]) + wide(came)
    return total if step + 1 == parts.shape[0] else narrow(total)


def packed_body(
    size,
    block_input,
    segment_ids,
    output_cotangent,
    input_gain,
    inner_weight,
    timestep_weight,
    state_weight,
    query_weight,
    keyvalue_matrix,
    conv_kernel,
    conv_offset,
    timestep_bias,
    decay_log,
    skip_scale,
    gated_gain,
    mamba_down,
    attention_down,
    middle_gain,
    gateup_weight,
    down_weight,
):
    rank = lax.axis_index("tp")
    at = lax.axis_index("fsdp")
    depth = size // 4
    rows = segment_ids.shape[0]
    own_rows = rows // 2
    shard, _, width = inner_weight.shape
    model = shard * size
    heads = timestep_weight.shape[1]
    state_width = state_weight.shape[1]
    query_width = query_weight.shape[1]
    keyvalue_width = keyvalue_matrix.shape[1]
    attended_width = attention_down.shape[0]
    hidden = gateup_weight.shape[2]
    ssm_width = gated_gain.shape[0]
    state_at = 2 * width
    steps_at = state_at + state_width

    def other(values):
        return lax.ppermute(values, "tp", swaps(2, 1))

    def joined(own, far):
        first = jnp.where(rank == 0, own, far)
        second = jnp.where(rank == 0, far, own)
        return jnp.concatenate([first, second], 0)

    def own_half(values):
        return lax.dynamic_slice_in_dim(values, rank * own_rows, own_rows, 0)

    def far_half(values):
        return lax.dynamic_slice_in_dim(values, (1 - rank) * own_rows, own_rows, 0)

    first_shard = jnp.concatenate(
        [
            inner_weight.reshape(shard, 2 * width),
            state_weight,
            jnp.pad(timestep_weight, ((0, 0), (0, 128 - heads))),
        ],
        1,
    )
    second_shard = jnp.concatenate(
        [query_weight, keyvalue_matrix, jnp.concatenate([mamba_down, attention_down], 0).T], 1
    )
    third_shard = jnp.concatenate([gateup_weight.reshape(shard, 2 * hidden), down_weight.T], 1)
    ring_at, x_at, core_at = at // 4, (at // 2) % 2, at % 2

    def block_of(distance, x_flip, core_flip):
        return ((ring_at - distance + depth) % depth) * 4 + (x_at ^ x_flip) * 2 + (
            core_at ^ core_flip
        )

    starts = jnp.stack(
        [block_of(k, i, j) for k in range(depth) for i in range(2) for j in range(2)]
    ).astype(jnp.int32)
    relative = jnp.arange(model, dtype=jnp.int32)
    piece_at = relative // shard
    absolute = (
        block_of(piece_at % depth, (piece_at // depth) % 2, piece_at // (2 * depth)) * shard
        + relative % shard
    )
    order = (absolute[:, None] == relative[None, :]).astype(jnp.bfloat16)

    labels = segment_ids.astype(jnp.float32)
    info = [jnp.zeros((rows, 1), jnp.float32)]
    for distance in range(1, 4):
        earlier = jnp.concatenate([jnp.full((distance,), -1.0), labels[:-distance]], 0)
        info.append((earlier == labels).astype(jnp.float32)[:, None])
    info = jnp.concatenate(info + [labels[:, None], jnp.zeros((rows, 123), jnp.float32)], 1)
    label_rows = jnp.broadcast_to(labels[None, :], (8, rows))
    repeat = width // heads
    local_skip = lax.dynamic_slice_in_dim(skip_scale, rank * heads, heads, 0)
    local = lambda array: lax.dynamic_slice_in_dim(array, rank * width, width, array.ndim - 1)
    local_gain = local(gated_gain)
    channel = jnp.concatenate(
        [
            local(conv_kernel),
            local(conv_offset)[None],
            jnp.repeat(local_skip, repeat)[None],
            local_gain[None],
            jnp.zeros((1, width), jnp.float32),
        ],
        0,
    )
    state_channel = jnp.concatenate(
        [
            conv_kernel[:, ssm_width:],
            conv_offset[None, ssm_width:],
            jnp.zeros((3, state_width), jnp.float32),
        ],
        0,
    )
    local_head = lambda array: lax.dynamic_slice_in_dim(array, rank * heads, heads, 0)
    head_rows = jnp.pad(
        jnp.stack([local_head(timestep_bias), -jnp.exp(local_head(decay_log))]),
        ((0, 6), (0, 128 - heads)),
    )
    quarter = HEAD_SIZE // 2
    frequency = jnp.exp(
        jnp.arange(quarter, dtype=jnp.float32) * (-2.0 * math.log(ROPE_BASE) / HEAD_SIZE)
    )
    angles = jnp.arange(rows, dtype=jnp.float32)[:, None] * frequency[None, :]
    cosine = jnp.tile(jnp.cos(angles), (1, 4))
    sinusoid = jnp.sin(angles)
    sinusoid = jnp.concatenate([-sinusoid, sinusoid, -sinusoid, sinusoid], 1)
    rank_array = rank.astype(jnp.int32)[None]
    mixer_widths = (width, state_at, steps_at)

    gathering = Gathering([first_shard, second_shard, third_shard], size)
    step = gathering.step
    empty = lambda: ()
    far_input = other(block_input)
    step([("z", 0, 1), ("x", 0, 0)], [("z", 0, 1)], empty)
    tables = step(
        [("z", 0, 2), ("x", 0, 1)],
        [("z", 0, 2), ("x", 0, 0)],
        lambda: (info, label_rows, channel, state_channel, head_rows),
    )
    info, label_rows, channel, state_channel, head_rows = tables
    group_input, cosine, sinusoid, order = step(
        [("z", 0, 3), ("x", 0, 2), ("c", 0, 0)],
        [("z", 0, 3), ("x", 0, 1)],
        lambda: (joined(block_input, far_input), cosine, sinusoid, order),
    )
    step(
        [("x", 0, 3), ("z", 1, 1), ("c", 0, 1)], [("z", 1, 1), ("x", 0, 2), ("x", 0, 3)], empty
    )
    projected, normed = step(
        [("c", 0, 2), ("c", 0, 3), ("x", 1, 0), ("x", 1, 1), ("z", 1, 2)],
        [("z", 1, 2), ("x", 1, 0)],
        lambda: project(starts, gathering.pieces(0), group_input, input_gain[None]),
    )

    def mix_forward():
        return mixer_forward(
            projected, mixer_widths, info, label_rows, channel, state_channel, head_rows
        )

    gated_low, scanned, square_lanes, dt, cum = step(
        [("x", 1, 2), ("z", 1, 3), ("z", 2, 1), ("c", 1, 0)],
        [("z", 1, 3), ("x", 1, 1), ("x", 1, 2)],
        mix_forward,
    )
    square_own = jnp.sum(square_lanes, 1)
    squares, far_cotangent = step(
        [("x", 1, 3), ("x", 2, 0), ("c", 1, 1), ("c", 1, 2)],
        [("x", 1, 3), ("z", 2, 1)],
        lambda: (square_own + other(square_own), other(output_cotangent)),
    )
    norm_factor = lax.rsqrt(squares / ssm_width + EPSILON)
    factor = wide(narrow(norm_factor))[:, None]

    def attend():
        return (
            attention_forward(
                rank_array,
                starts,
                normed,
                info,
                label_rows,
                cosine,
                sinusoid,
                gated_low,
                factor,
                gathering.pieces(1),
                query_width,
            ),
            joined(output_cotangent, far_cotangent),
        )

    attending, cotangent = step(
        [("c", 1, 3), ("x", 2, 1), ("z", 2, 2)],
        [("z", 2, 2), ("x", 2, 0), ("x", 2, 1)],
        attend,
    )
    attended, turned, keys, values, logsum, mamba_own, mixed_low = attending
    mixed_first, normed_turned = step(
        [("z", 2, 3), ("x", 2, 2), ("c", 2, 0)],
        [("z", 2, 3), ("x", 2, 2)],
        lambda: (other(mixed_low[:own_rows]), narrow(contract_cols(order, normed))),
    )
    mixed_second, cotangent_turned = step(
        [("x", 2, 3), ("c", 2, 1)],
        [("x", 2, 3)],
        lambda: (other(mixed_low[own_rows:]), narrow(contract_cols(order, cotangent))),
    )
    step([("c", 2, 2), ("c", 2, 3)], [], empty)
    mixed_far = jnp.concatenate([mixed_first, mixed_second], 0)
    middle, hidden_in, activated, grad_gateup, hidden_low, feedforward_low = feed_forward(
        starts,
        gathering.pieces(2),
        hidden,
        group_input,
        mixed_low,
        mixed_far,
        middle_gain[None],
        cotangent,
    )

    hidden_first = other(hidden_low[:own_rows])
    feed_far, feed_line, feed_own = weight_grads(
        feed_grads_kernel,
        [order, cotangent_turned, hidden_in, activated, grad_gateup],
        model,
        3 * hidden,
        "feed_grads",
    )
    hidden_first, feed_far, hidden_low, feedforward_low = tie(
        hidden_first, feed_far, hidden_low, feedforward_low
    )
    hidden_second = other(hidden_low[own_rows:])
    feed_came = send_core(feed_far, size)
    hidden_first, hidden_second, feed_came, feedforward_low = tie(
        hidden_first, hidden_second, feed_came, feedforward_low
    )
    cuts = [0, hidden + 256, 2 * hidden, 3 * hidden]
    lines, owns = [], []
    for i, j in zip(cuts, cuts[1:]):
        line, own = add_core(feed_came[:, i:j], feed_line[:, i:j], feed_own[:, i:j])
        lines.append(line)
        owns.append(own)

    came = send_line(lines[0], size)
    grad_hidden = wide(hidden_low) + wide(jnp.concatenate([hidden_first, hidden_second], 0))
    middle_rms = inverse_rms(middle)
    middle_normal = middle * middle_rms
    middle_gain_part = jnp.sum(grad_hidden * middle_normal, 0)
    middle_scaled = grad_hidden * middle_gain
    grad_middle = wide(cotangent) + middle_rms * (
        middle_scaled - middle_normal * jnp.mean(middle_scaled * middle_normal, -1, keepdims=True)
    )
    mix_low = narrow(grad_middle)
    mix = wide(mix_low)
    square_sum = jnp.sum(mix * wide(mamba_own), -1)
    square_sum = square_sum + other(square_sum)
    grad_mamba = narrow(factor * mix)
    second_pieces = gathering.pieces(1)
    mamba_at = query_width + keyvalue_width
    grad_query, grad_keyvalue = attention_backward(
        rank_array,
        starts,
        mix_low,
        turned,
        keys,
        values,
        logsum,
        info,
        label_rows,
        cosine,
        sinusoid,
        second_pieces,
        mamba_at + width,
    )
    came, square_sum, grad_query, grad_mamba, lines, owns = tie(
        came, square_sum, grad_query, grad_mamba, lines, owns
    )
    first_parts = add_line(came, owns[0], size)
    ring_first = send_ring(first_parts[1], size)
    square_column = wide(
        narrow(square_sum * -0.5 * norm_factor * norm_factor * norm_factor / ssm_width)
    )[:, None]
    came = send_line(lines[1], size)
    second_far, second_line, second_own = weight_grads(
        second_kernel,
        [
            order,
            mix_low,
            factor.reshape(1, rows),
            normed_turned,
            gated_low,
            attended,
            grad_query,
            grad_keyvalue,
        ],
        model,
        width + attended_width + query_width + keyvalue_width,
        "second_grads",
    )
    came, second_far, square_column, lines, ring_first = tie(
        came, second_far, square_column, lines, ring_first
    )
    feed_parts = [add_line(came, owns[1], size)]
    first_total = add_ring(first_parts, ring_first, 1)
    ring_first = send_ring(first_total, size)

    second_came = send_core(second_far, size)
    came = send_line(lines[2], size)
    grad_gated_low, grad_gate, gate_far, gate_line, gate_own = gate_backward(
        starts,
        grad_mamba,
        projected,
        scanned,
        local_gain[None],
        square_column,
        normed_turned,
        second_pieces,
        mamba_at,
    )
    second_came, came, grad_gated_low, gate_far, ring_first, feedforward_low = tie(
        second_came, came, grad_gated_low, gate_far, ring_first, feedforward_low
    )
    feedforward_far = other(far_half(feedforward_low))
    first_total = add_ring(first_parts, ring_first, 2)
    ring_first = send_ring(first_total, size)
    second_line, second_own = add_core(second_came, second_line, second_own)
    second_came = send_line(second_line, size)
    gate_came = send_core(gate_far, size)
    feed_parts.append(add_line(came, owns[2], size))
    feed_parts = jnp.concatenate(feed_parts, 2)
    ring_feed = send_ring(feed_parts[1], size)
    lanes = jnp.arange(128, dtype=jnp.int32)[None, :]
    info = jnp.where(lanes == 5, square_column, info)
    grad_value, grad_state, grad_steps, channel_grad, state_grad, head_grad = mixer_backward(
        projected,
        mixer_widths,
        info,
        label_rows,
        channel,
        state_channel,
        head_rows,
        scanned,
        grad_gated_low,
        dt,
        cum,
    )
    grad_value, ring_feed, second_came, gate_came, ring_first, feedforward_far = tie(
        grad_value, ring_feed, second_came, gate_came, ring_first, feedforward_far
    )
    first_total = add_ring(first_parts, ring_first, 3)

    gate_line, gate_own = add_core(gate_came, gate_line, gate_own)
    gate_came = send_line(gate_line, size)
    feed_total = add_ring(feed_parts, ring_feed, 1)
    ring_feed = send_ring(feed_total, size)
    last_far, last_line, last_own = weight_grads(
        last_kernel,
        [normed_turned, grad_value, grad_state, grad_steps],
        model,
        width + state_width + 128,
        "last_grads",
    )
    last_far, ring_feed, grad_value = tie(last_far, ring_feed, grad_value)
    last_came = send_core(last_far, size)
    last_came, gate_came, grad_value = tie(last_came, gate_came, grad_value)
    last_line, last_own = add_core(last_came, last_line, last_own)
    last_came = send_line(last_line, size)
    feed_total = add_ring(feed_parts, ring_feed, 2)
    ring_feed = send_ring(feed_total, size)
    second_parts = jnp.concatenate(
        [add_line(second_came, second_own, size), add_line(gate_came, gate_own, size)], 2
    )
    ring_second = send_ring(second_parts[1], size)
    normed_low = back_project(
        starts,
        gathering.pieces(0),
        second_pieces,
        [grad_gate, grad_value, grad_state, grad_steps, grad_query, grad_keyvalue],
    )
    normed_low, last_came, ring_feed, ring_second = tie(
        normed_low, last_came, ring_feed, ring_second
    )
    feed_total = add_ring(feed_parts, ring_feed, 3)
    second_total = add_ring(second_parts, ring_second, 1)
    spread = lambda part, total, start: lax.dynamic_update_slice_in_dim(
        jnp.zeros(part.shape[:-1] + (total,), jnp.float32), part, start, part.ndim - 1
    )
    block_output = (
        own_half(middle)
        + wide(own_half(feedforward_low))
        + wide(feedforward_far)
    )
    residual = wide(group_input)
    first_rms = inverse_rms(residual)
    first_normal = residual * first_rms
    input_gain_part = jnp.sum(wide(normed_low) * first_normal, 0)
    channel_parts = jnp.concatenate(
        [spread(channel_grad[:5], ssm_width, rank * width), state_grad[:5]], 1
    )
    skip_grad = jnp.sum(channel_grad[5].reshape(heads, repeat), 1)
    head_parts = spread(
        jnp.concatenate([head_grad[:2, :heads], skip_grad[None]], 0),
        timestep_bias.shape[0],
        rank * heads,
    )
    gain_parts = spread(channel_grad[6], ssm_width, rank * width)
    leader = (rank == 0).astype(jnp.float32)
    parts = [input_gain_part, middle_gain_part * leader, gain_parts, channel_parts, head_parts]
    flat = jnp.concatenate([part.reshape(-1) for part in parts])
    flat = jnp.pad(flat, (0, -flat.shape[0] % 1024)).reshape(-1, 128)

    last_parts = add_line(last_came, last_own, size)
    ring_last = send_ring(last_parts[1], size)
    normed_far = other(far_half(normed_low))
    ring_second = send_ring(second_total, size)
    flat_far = lax.ppermute(flat, "fsdp", swaps(size, 1))
    ring_last, ring_second, flat_far = tie(ring_last, ring_second, flat_far)
    last_total = add_ring(last_parts, ring_last, 1)
    ring_last = send_ring(last_total, size)
    second_total = add_ring(second_parts, ring_second, 2)
    flat = flat + flat_far
    ring_second = send_ring(second_total, size)
    flat_far = lax.ppermute(flat, "fsdp", swaps(size, 2))
    ring_last, ring_second, flat_far = tie(ring_last, ring_second, flat_far)
    last_total = add_ring(last_parts, ring_last, 2)
    ring_last = send_ring(last_total, size)
    second_total = add_ring(second_parts, ring_second, 3)
    flat = flat + flat_far
    lined = [
        lax.ppermute(flat, "fsdp", [(i, (i + 4 * k) % size) for i in range(size)])
        for k in range(1, depth)
    ]
    ring_last, normed_far, *lined = tie(ring_last, normed_far, *lined)
    last_total = add_ring(last_parts, ring_last, 3)
    placed = jnp.stack([flat] + lined)
    flat = sum(placed[(ring_at - k + depth) % depth] for k in range(depth))
    flat = (flat + other(flat)).reshape(-1)
    shared_at = width + attended_width + query_width
    shared = jnp.concatenate(
        [last_total[:, width : width + state_width], second_total[:, shared_at : shared_at + keyvalue_width]],
        1,
    )
    shared = shared + other(shared)
    normed_grad = wide(own_half(normed_low)) + wide(normed_far)
    own_normal = own_half(first_normal)
    first_scaled = normed_grad * input_gain
    input_grad = own_half(grad_middle) + own_half(first_rms) * (
        first_scaled - own_normal * jnp.mean(first_scaled * own_normal, -1, keepdims=True)
    )

    summed = []
    for part in parts:
        summed.append(flat[: part.size].reshape(part.shape))
        flat = flat[part.size :]
    inner_grad = jnp.stack(
        [second_total[:, shared_at + keyvalue_width :], last_total[:, :width]], 1
    )
    return (
        block_output,
        input_grad,
        summed[0],
        inner_grad,
        last_total[:, width + state_width : width + state_width + heads],
        shared[:, :state_width],
        second_total[:, width + attended_width : shared_at],
        shared[:, state_width:],
        summed[3][:4],
        summed[3][4],
        summed[4][0],
        summed[4][1],
        summed[4][2],
        summed[2],
        second_total[:, :width].T,
        second_total[:, width : width + attended_width].T,
        summed[1],
        jnp.concatenate([first_total[:, hidden:], feed_total], 1).reshape(shard, 2, hidden),
        first_total[:, :hidden].T,
    )


def solution(mesh):
    fsdp, tp = mesh.shape["fsdp"], mesh.shape["tp"]

    def body(*operands):
        rows = operands[1].shape[0]
        if tp == 2 and fsdp == 16 and rows == 2 * BLOCK:
            return packed_body(fsdp, *operands)
        return general_body(*operands)

    return jax.shard_map(
        body,
        mesh=mesh,
        in_specs=(
            P(("fsdp", "tp"), None),
            P("fsdp"),
            P(("fsdp", "tp"), None),
            P(),
            P("fsdp", None, "tp"),
            P("fsdp", "tp"),
            P("fsdp", None),
            P("fsdp", "tp"),
            P("fsdp", None),
            P(),
            P(),
            P(),
            P(),
            P(),
            P(),
            P("tp", "fsdp"),
            P("tp", "fsdp"),
            P(),
            P("fsdp", None, "tp"),
            P("tp", "fsdp"),
        ),
        out_specs=(
            P(("fsdp", "tp"), None),
            P(("fsdp", "tp"), None),
            P(),
            P("fsdp", None, "tp"),
            P("fsdp", "tp"),
            P("fsdp", None),
            P("fsdp", "tp"),
            P("fsdp", None),
            P(),
            P(),
            P(),
            P(),
            P(),
            P(),
            P("tp", "fsdp"),
            P("tp", "fsdp"),
            P(),
            P("fsdp", None, "tp"),
            P("tp", "fsdp"),
        ),
        check_vma=False,
    )
```

```python
import math

import jax
import jax.numpy as jnp
from jax import lax
from jax.experimental import pallas as pl
from jax.experimental.pallas import tpu as pltpu
from jax.sharding import PartitionSpec as P

QUERY_HEADS = 8
KEYVALUE_HEADS = 2
HEAD_SIZE = 64
SCAN_BLOCK = 256
QUERY_BLOCK = 512


EPSILON = 1e-05
MASKED_SCORE = -1e30
ROPE_BASE = 100000000000.0
PRECISE = lax.Precision.HIGHEST


def inverse_rms(values):
    return lax.rsqrt(jnp.mean(values * values, -1, keepdims=True) + EPSILON)


def contract_rows(left, right):
    return lax.dot_general(
        left, right, (((0,), (0,)), ((), ())), preferred_element_type=jnp.float32
    )


def contract_cols(left, right):
    return lax.dot_general(
        left, right, (((1,), (1,)), ((), ())), preferred_element_type=jnp.float32
    )


def causal_conv(signal, kernel, offset, segment):
    length_tokens = signal.shape[0]
    result = offset[None, :] + kernel[0][None, :] * signal
    for distance in range(1, kernel.shape[0]):
        shifted = jnp.concatenate(
            [
                jnp.zeros((distance, signal.shape[1]), signal.dtype),
                signal[: length_tokens - distance],
            ],
            0,
        )
        earlier = jnp.concatenate(
            [jnp.full((distance,), -1, jnp.int32), segment[: length_tokens - distance]], 0
        )
        retained = (earlier == segment).astype(signal.dtype)
        result = result + kernel[distance][None, :] * shifted * retained[:, None]
    return result


def state_scan(values, timesteps, decays, key_row_block, query_rows, segment, block):
    total, head_count, channels = values.shape
    count = total // block
    states = key_row_block.shape[1]
    lower = jnp.arange(block)[:, None] >= jnp.arange(block)[None, :]

    def advance(carry, pieces):
        memory, previous = carry
        value_block, step_block, key_block, query_block, labels = pieces
        rates = step_block * decays[None, :]
        cumulative = jnp.cumsum(rates, 0)
        linked = jnp.logical_and(labels[:, None] == labels[None, :], lower)
        gaps = cumulative[:, None, :] - cumulative[None, :, :]
        weights = jnp.exp(jnp.where(linked[:, :, None], gaps, 0.0)) * linked[:, :, None].astype(
            jnp.float32
        )
        intersections = jnp.dot(query_block, key_block.T, precision=PRECISE)
        scaled = value_block * step_block[:, :, None]
        within = jnp.einsum(
            "tsh,shp->thp", intersections[:, :, None] * weights, scaled, precision=PRECISE
        )
        carried = jnp.exp(cumulative) * (labels == previous).astype(jnp.float32)[:, None]
        across = (
            jnp.einsum("tn,hpn->thp", query_block, memory, precision=PRECISE) * carried[:, :, None]
        )
        final = cumulative[block - 1]
        ending = labels[block - 1]
        toward = (
            jnp.exp(final[None, :] - cumulative) * (labels == ending).astype(jnp.float32)[:, None]
        )
        fresh = jnp.einsum("sh,shp,sn->hpn", toward, scaled, key_block, precision=PRECISE)
        kept = jnp.exp(final) * (ending == previous).astype(jnp.float32)
        memory = memory * kept[:, None, None] + fresh
        return ((memory, ending), within + across)

    start = (jnp.zeros((head_count, channels, states), jnp.float32), jnp.array(-1, jnp.int32))
    pieces = (
        values.reshape(count, block, head_count, channels),
        timesteps.reshape(count, block, head_count),
        key_row_block.reshape(count, block, states),
        query_rows.reshape(count, block, states),
        segment.reshape(count, block),
    )
    folded, outputs = lax.scan(jax.checkpoint(advance), start, pieces)
    return outputs.reshape(total, head_count, channels)


def mixer_core(
    values, raw_steps, step_bias, decay_log, skip_scale, key_row_block, query_rows, segment, block
):
    timesteps = jax.nn.softplus(raw_steps + step_bias[None, :])
    decays = -jnp.exp(decay_log)
    head_count = timesteps.shape[1]
    shaped = values.reshape(values.shape[0], head_count, -1)
    output = state_scan(shaped, timesteps, decays, key_row_block, query_rows, segment, block)
    return (output + skip_scale[None, :, None] * shaped).reshape(values.shape)


def rotary_apply(vectors, direction):
    length_tokens, head_count, columns = vectors.shape
    halfway = columns // 2
    frequency = jnp.exp(
        jnp.arange(halfway, dtype=jnp.float32) * (-2.0 * math.log(ROPE_BASE) / columns)
    )
    angles = jnp.arange(length_tokens, dtype=jnp.float32)[:, None] * frequency[None, :] * direction
    cosine = jnp.cos(angles)[:, None, :]
    sinusoid = jnp.sin(angles)[:, None, :]
    former = vectors[..., :halfway]
    latter = vectors[..., halfway:]
    return jnp.concatenate(
        [former * cosine - latter * sinusoid, latter * cosine + former * sinusoid], -1
    )


def attention_mask(segment, start, rowcount):
    positions = start + jnp.arange(rowcount, dtype=jnp.int32)
    columns = jnp.arange(segment.shape[0], dtype=jnp.int32)
    labels = lax.dynamic_slice_in_dim(segment, start, rowcount)
    return jnp.logical_and(
        columns[None, :] <= positions[:, None], segment[None, :] == labels[:, None]
    )


def general_body(
    block_input,
    segment_ids,
    output_cotangent,
    input_gain,
    inner_weight,
    timestep_weight,
    state_weight,
    query_weight,
    keyvalue_matrix,
    conv_kernel,
    conv_offset,
    timestep_bias,
    decay_log,
    skip_scale,
    gated_gain,
    mamba_down,
    attention_down,
    middle_gain,
    gateup_weight,
    down_weight,
):
    tensor_parallel_rank = lax.axis_index("tp")
    residual = block_input.astype(jnp.float32)
    first_rms = inverse_rms(residual)
    normed = lax.all_gather(
        (residual * first_rms * input_gain).astype(jnp.bfloat16), "tp", axis=0, tiled=True
    )
    (
        inner_full,
        timestep_full,
        state_full,
        query_full,
        keyvalue_full,
        mamba_full,
        attention_full,
        gateup_full,
        down_full,
    ) = (
        lax.all_gather(inner_weight, "fsdp", axis=0, tiled=True),
        lax.all_gather(timestep_weight, "fsdp", axis=0, tiled=True),
        lax.all_gather(state_weight, "fsdp", axis=0, tiled=True),
        lax.all_gather(query_weight, "fsdp", axis=0, tiled=True),
        lax.all_gather(keyvalue_matrix, "fsdp", axis=0, tiled=True),
        lax.all_gather(mamba_down, "fsdp", axis=1, tiled=True),
        lax.all_gather(attention_down, "fsdp", axis=1, tiled=True),
        lax.all_gather(gateup_weight, "fsdp", axis=0, tiled=True),
        lax.all_gather(down_weight, "fsdp", axis=1, tiled=True),
    )
    length_tokens = normed.shape[0]
    local_heads = timestep_full.shape[1]
    local_width = inner_full.shape[2]
    ssm_width = gated_gain.shape[0]
    state_dim = state_full.shape[1] // 2
    query_head_count = query_full.shape[1] // HEAD_SIZE
    head_start = tensor_parallel_rank * local_heads
    width_start = tensor_parallel_rank * local_width
    inner = jnp.einsum("gd,dkc->gkc", normed, inner_full, preferred_element_type=jnp.float32)
    raw_steps = jnp.dot(normed, timestep_full, preferred_element_type=jnp.float32)
    state_proj = jnp.dot(normed, state_full, preferred_element_type=jnp.float32)
    query_proj = jnp.dot(normed, query_full, preferred_element_type=jnp.float32)
    keyvalue_projected = jnp.dot(normed, keyvalue_full, preferred_element_type=jnp.float32)
    gate_half = inner[:, 0]
    local_kernel = jnp.concatenate(
        [
            lax.dynamic_slice_in_dim(conv_kernel, width_start, local_width, 1),
            conv_kernel[:, ssm_width:],
        ],
        1,
    )
    local_offset = jnp.concatenate(
        [
            lax.dynamic_slice_in_dim(conv_offset, width_start, local_width, 0),
            conv_offset[ssm_width:],
        ],
        0,
    )
    local_bias = lax.dynamic_slice_in_dim(timestep_bias, head_start, local_heads, 0)
    local_decay = lax.dynamic_slice_in_dim(decay_log, head_start, local_heads, 0)
    local_skip = lax.dynamic_slice_in_dim(skip_scale, head_start, local_heads, 0)
    local_gain = lax.dynamic_slice_in_dim(gated_gain, width_start, local_width, 0)

    def convolve(signal, kernel, offset):
        return jax.nn.silu(causal_conv(signal, kernel, offset, segment_ids))

    convolved, conv_pullback = jax.vjp(
        convolve, jnp.concatenate([inner[:, 1], state_proj], 1), local_kernel, local_offset
    )
    conv_values = convolved[:, :local_width].astype(jnp.bfloat16)
    conv_states = convolved[:, local_width:].astype(jnp.bfloat16).astype(jnp.float32)

    def scan_heads(values, steps_in, bias_in, decay_in, skip_in, key_rows_in, query_rows_in):
        return mixer_core(
            values,
            steps_in,
            bias_in,
            decay_in,
            skip_in,
            key_rows_in,
            query_rows_in,
            segment_ids,
            SCAN_BLOCK,
        )

    scanned, scan_pullback = jax.vjp(
        scan_heads,
        conv_values.astype(jnp.float32),
        raw_steps,
        local_bias,
        local_decay,
        local_skip,
        conv_states[:, :state_dim],
        conv_states[:, state_dim:],
    )
    silu_gate = jax.nn.silu(gate_half)
    gated = scanned * silu_gate
    gated_low = (gated * local_gain).astype(jnp.bfloat16)
    mamba_partial = jnp.dot(gated_low, mamba_full, preferred_element_type=jnp.float32)
    queries = rotary_apply(
        query_proj.reshape(length_tokens, query_head_count, HEAD_SIZE), 1.0
    ).astype(jnp.bfloat16)
    key_gathered = rotary_apply(
        keyvalue_projected[:, : KEYVALUE_HEADS * HEAD_SIZE].reshape(
            length_tokens, KEYVALUE_HEADS, HEAD_SIZE
        ),
        1.0,
    ).astype(jnp.bfloat16)
    value_gathered = (
        keyvalue_projected[:, KEYVALUE_HEADS * HEAD_SIZE :]
        .reshape(length_tokens, KEYVALUE_HEADS, HEAD_SIZE)
        .astype(jnp.bfloat16)
    )
    owner_ranks = (
        tensor_parallel_rank * query_head_count + jnp.arange(query_head_count, dtype=jnp.int32)
    ) // (QUERY_HEADS // KEYVALUE_HEADS)
    choice_picker = (
        owner_ranks[:, None] == jnp.arange(KEYVALUE_HEADS, dtype=jnp.int32)[None, :]
    ).astype(jnp.bfloat16)
    key_row_block = jnp.einsum(
        "jh,ghd->gjd", choice_picker, key_gathered, preferred_element_type=jnp.float32
    ).astype(jnp.bfloat16)
    value_row_block = jnp.einsum(
        "jh,ghd->gjd", choice_picker, value_gathered, preferred_element_type=jnp.float32
    ).astype(jnp.bfloat16)
    scaling = 1.0 / math.sqrt(HEAD_SIZE)
    block_count = length_tokens // QUERY_BLOCK
    query_blocks = queries.reshape(block_count, QUERY_BLOCK, query_head_count, HEAD_SIZE)
    block_starts = jnp.arange(block_count, dtype=jnp.int32) * QUERY_BLOCK

    def block_scores(query_block, start):
        scores = (
            jnp.einsum(
                "qjd,kjd->jqk", query_block, key_row_block, preferred_element_type=jnp.float32
            )
            * scaling
        )
        allowed = attention_mask(segment_ids, start, QUERY_BLOCK)
        return jnp.where(allowed[None], scores, MASKED_SCORE)

    def forward_block(pieces):
        query_block, start = pieces
        masked = block_scores(query_block, start)
        highest = jnp.max(masked, -1, keepdims=True)
        weights = jnp.exp(masked - highest)
        totals = jnp.sum(weights, -1, keepdims=True)
        probs_low = (weights / totals).astype(jnp.bfloat16)
        result = jnp.einsum(
            "jqk,kjd->qjd", probs_low, value_row_block, preferred_element_type=jnp.float32
        )
        return (result, (highest + jnp.log(totals))[..., 0])

    attended, logsums = lax.map(forward_block, (query_blocks, block_starts))
    attended_low = attended.reshape(length_tokens, query_head_count * HEAD_SIZE).astype(
        jnp.bfloat16
    )
    attention_partial = jnp.dot(attended_low, attention_full, preferred_element_type=jnp.float32)
    square_local = jnp.sum(gated * gated, -1)
    mamba_rows, attention_rows, square_rows = (
        lax.psum_scatter(mamba_partial, "tp", scatter_dimension=0, tiled=True),
        lax.psum_scatter(attention_partial, "tp", scatter_dimension=0, tiled=True),
        lax.psum_scatter(square_local, "tp", scatter_dimension=0, tiled=True),
    )
    norm_factor = lax.rsqrt(square_rows / ssm_width + EPSILON)
    factor_low = norm_factor.astype(jnp.bfloat16)
    factor_own = lax.optimization_barrier(factor_low).astype(jnp.float32)
    middle = residual + (factor_own[:, None] * mamba_rows + attention_rows)
    middle_rms = inverse_rms(middle)
    hidden_in = lax.all_gather(
        (middle * middle_rms * middle_gain).astype(jnp.bfloat16), "tp", axis=0, tiled=True
    )
    gateup = jnp.einsum("gd,dkf->gkf", hidden_in, gateup_full, preferred_element_type=jnp.float32)
    gate_part = gateup[:, 0]
    up_part = gateup[:, 1]
    activated = (jax.nn.silu(gate_part) * up_part).astype(jnp.bfloat16)
    feedforward = lax.psum_scatter(
        jnp.dot(activated, down_full, preferred_element_type=jnp.float32).astype(jnp.bfloat16),
        "tp",
        scatter_dimension=0,
        tiled=True,
    ).astype(jnp.float32)
    block_output = middle + feedforward
    cotangent_all = lax.all_gather(output_cotangent, "tp", axis=0, tiled=True)
    grad_activated = contract_cols(cotangent_all, down_full)
    down_wgrad = contract_rows(activated, cotangent_all)
    gate_sigmoid = jax.nn.sigmoid(gate_part)
    grad_gate_part = (
        grad_activated * up_part * gate_sigmoid * (1.0 + gate_part * (1.0 - gate_sigmoid))
    )
    grad_up_part = grad_activated * jax.nn.silu(gate_part)
    grad_gateup = jnp.stack([grad_gate_part, grad_up_part], 1).astype(jnp.bfloat16)
    gateup_wgrad = jnp.einsum(
        "gd,gkf->dkf", hidden_in, grad_gateup, preferred_element_type=jnp.float32
    )
    grad_hidden = lax.psum_scatter(
        jnp.einsum("gkf,dkf->gd", grad_gateup, gateup_full, preferred_element_type=jnp.float32),
        "tp",
        scatter_dimension=0,
        tiled=True,
    )
    middle_normal = middle * middle_rms
    middle_gain_part = jnp.sum(grad_hidden * middle_normal, 0)
    middle_scaled = grad_hidden * middle_gain
    grad_middle = output_cotangent.astype(jnp.float32) + middle_rms * (
        middle_scaled - middle_normal * jnp.mean(middle_scaled * middle_normal, -1, keepdims=True)
    )
    mix_low = grad_middle.astype(jnp.bfloat16)
    mix_own = mix_low.astype(jnp.float32)
    grad_factor = jnp.sum(mix_own * mamba_rows, -1)
    grad_square = (grad_factor * -0.5 * norm_factor * norm_factor * norm_factor / ssm_width).astype(
        jnp.bfloat16
    )
    mix_all, factor_rows, square_rows_grad = (
        lax.all_gather(mix_low, "tp", axis=0, tiled=True),
        lax.all_gather(factor_low, "tp", axis=0, tiled=True),
        lax.all_gather(grad_square, "tp", axis=0, tiled=True),
    )
    grad_mamba = (factor_rows.astype(jnp.float32)[:, None] * mix_all.astype(jnp.float32)).astype(
        jnp.bfloat16
    )
    mamba_wgrad = contract_rows(gated_low, grad_mamba)
    grad_gated_low = contract_cols(grad_mamba, mamba_full)
    gain_grad = jnp.sum(grad_gated_low * gated, 0)
    grad_gated = (
        grad_gated_low * local_gain + 2.0 * gated * square_rows_grad.astype(jnp.float32)[:, None]
    )
    zsigmoid = jax.nn.sigmoid(gate_half)
    grad_scanned = grad_gated * silu_gate
    grad_gate = grad_gated * scanned * zsigmoid * (1.0 + gate_half * (1.0 - zsigmoid))
    grad_values, grad_steps, grad_bias, grad_decay, grad_skip, grad_keys_in, grad_queries_in = (
        scan_pullback(grad_scanned)
    )
    grad_signal, kernel_local, offset_local = conv_pullback(
        jnp.concatenate([grad_values, grad_keys_in, grad_queries_in], 1)
    )
    attention_wgrad = contract_rows(attended_low, mix_all)
    grad_attended = (
        contract_cols(mix_all, attention_full)
        .astype(jnp.bfloat16)
        .reshape(block_count, QUERY_BLOCK, query_head_count, HEAD_SIZE)
    )

    def backward_block(carry, pieces):
        key_grad, value_grad = carry
        query_block, grad_block, logsum_block, start = pieces
        masked = block_scores(query_block, start)
        probs = jnp.exp(masked - logsum_block[..., None])
        grad_probs = jnp.einsum(
            "qjd,kjd->jqk", grad_block, value_row_block, preferred_element_type=jnp.float32
        )
        inner_sum = jnp.sum(grad_probs * probs, -1, keepdims=True)
        grad_scores = (probs * (grad_probs - inner_sum)).astype(jnp.bfloat16)
        query_grad = (
            jnp.einsum(
                "jqk,kjd->qjd", grad_scores, key_row_block, preferred_element_type=jnp.float32
            )
            * scaling
        )
        key_grad = (
            key_grad
            + jnp.einsum(
                "jqk,qjd->kjd", grad_scores, query_block, preferred_element_type=jnp.float32
            )
            * scaling
        )
        value_grad = value_grad + jnp.einsum(
            "jqk,qjd->kjd",
            probs.astype(jnp.bfloat16),
            grad_block,
            preferred_element_type=jnp.float32,
        )
        return ((key_grad, value_grad), query_grad)

    empty_rows = jnp.zeros((length_tokens, query_head_count, HEAD_SIZE), jnp.float32)
    (key_grad, value_grad), query_grads = lax.scan(
        backward_block,
        (empty_rows, empty_rows),
        (query_blocks, grad_attended, logsums, block_starts),
    )
    query_back = rotary_apply(
        query_grads.reshape(length_tokens, query_head_count, HEAD_SIZE), -1.0
    ).reshape(length_tokens, query_head_count * HEAD_SIZE)
    selector_float = choice_picker.astype(jnp.float32)
    key_returned = rotary_apply(
        jnp.einsum("jh,gjd->ghd", selector_float, key_grad, precision=PRECISE), -1.0
    )
    value_returned = jnp.einsum("jh,gjd->ghd", selector_float, value_grad, precision=PRECISE)
    keyvalue_partial = jnp.concatenate(
        [
            key_returned.reshape(length_tokens, KEYVALUE_HEADS * HEAD_SIZE),
            value_returned.reshape(length_tokens, KEYVALUE_HEADS * HEAD_SIZE),
        ],
        1,
    )
    state_total, keyvalue_total = (
        lax.psum(grad_signal[:, local_width:].astype(jnp.bfloat16), "tp").astype(jnp.float32),
        lax.psum(keyvalue_partial.astype(jnp.bfloat16), "tp").astype(jnp.float32),
    )
    inner_low = jnp.stack([grad_gate, grad_signal[:, :local_width]], 1).astype(jnp.bfloat16)
    steps_low = grad_steps.astype(jnp.bfloat16)
    query_low = query_back.astype(jnp.bfloat16)
    state_low = state_total.astype(jnp.bfloat16)
    keyvalue_low = keyvalue_total.astype(jnp.bfloat16)
    inner_wgrad = jnp.einsum("gd,gkc->dkc", normed, inner_low, preferred_element_type=jnp.float32)
    timestep_wgrad = contract_rows(normed, steps_low)
    state_wgrad = contract_rows(normed, state_low)
    query_wgrad = contract_rows(normed, query_low)
    keyvalue_wgrad = contract_rows(normed, keyvalue_low)
    normed_partial = (
        jnp.einsum("gkc,dkc->gd", inner_low, inner_full, preferred_element_type=jnp.float32)
        + contract_cols(steps_low, timestep_full)
        + contract_cols(query_low, query_full)
    )
    leader = (tensor_parallel_rank == 0).astype(jnp.float32)
    normed_partial = normed_partial + leader * (
        contract_cols(state_low, state_full) + contract_cols(keyvalue_low, keyvalue_full)
    )
    normed_grad = lax.psum_scatter(
        normed_partial.astype(jnp.bfloat16), "tp", scatter_dimension=0, tiled=True
    ).astype(jnp.float32)
    first_normal = residual * first_rms
    input_gain_part = jnp.sum(normed_grad * first_normal, 0)
    first_scaled = normed_grad * input_gain
    input_grad = grad_middle + first_rms * (
        first_scaled - first_normal * jnp.mean(first_scaled * first_normal, -1, keepdims=True)
    )
    gated_part = lax.dynamic_update_slice_in_dim(
        jnp.zeros((ssm_width,), jnp.float32), gain_grad, width_start, 0
    )
    kernel_part = jnp.concatenate(
        [
            lax.dynamic_update_slice_in_dim(
                jnp.zeros((conv_kernel.shape[0], ssm_width), jnp.float32),
                kernel_local[:, :local_width],
                width_start,
                1,
            ),
            kernel_local[:, local_width:],
        ],
        1,
    )
    offset_part = jnp.concatenate(
        [
            lax.dynamic_update_slice_in_dim(
                jnp.zeros((ssm_width,), jnp.float32), offset_local[:local_width], width_start, 0
            ),
            offset_local[local_width:],
        ],
        0,
    )
    head_zeros = jnp.zeros((timestep_bias.shape[0],), jnp.float32)
    bias_part = lax.dynamic_update_slice_in_dim(head_zeros, grad_bias, head_start, 0)
    decay_part = lax.dynamic_update_slice_in_dim(head_zeros, grad_decay, head_start, 0)
    skip_part = lax.dynamic_update_slice_in_dim(head_zeros, grad_skip, head_start, 0)
    summed = lax.psum(
        (
            input_gain_part,
            middle_gain_part,
            kernel_part,
            offset_part,
            bias_part,
            decay_part,
            skip_part,
            gated_part,
        ),
        ("fsdp", "tp"),
    )
    (
        inner_out,
        timestep_out,
        state_out,
        query_out,
        keyvalue_out,
        mamba_out,
        attention_out,
        gateup_out,
        down_out,
    ) = (
        lax.psum_scatter(
            inner_wgrad.astype(jnp.bfloat16), "fsdp", scatter_dimension=0, tiled=True
        ).astype(jnp.float32),
        lax.psum_scatter(
            timestep_wgrad.astype(jnp.bfloat16), "fsdp", scatter_dimension=0, tiled=True
        ).astype(jnp.float32),
        lax.psum_scatter(
            state_wgrad.astype(jnp.bfloat16), "fsdp", scatter_dimension=0, tiled=True
        ).astype(jnp.float32),
        lax.psum_scatter(
            query_wgrad.astype(jnp.bfloat16), "fsdp", scatter_dimension=0, tiled=True
        ).astype(jnp.float32),
        lax.psum_scatter(
            keyvalue_wgrad.astype(jnp.bfloat16), "fsdp", scatter_dimension=0, tiled=True
        ).astype(jnp.float32),
        lax.psum_scatter(
            mamba_wgrad.astype(jnp.bfloat16), "fsdp", scatter_dimension=1, tiled=True
        ).astype(jnp.float32),
        lax.psum_scatter(
            attention_wgrad.astype(jnp.bfloat16), "fsdp", scatter_dimension=1, tiled=True
        ).astype(jnp.float32),
        lax.psum_scatter(
            gateup_wgrad.astype(jnp.bfloat16), "fsdp", scatter_dimension=0, tiled=True
        ).astype(jnp.float32),
        lax.psum_scatter(
            down_wgrad.astype(jnp.bfloat16), "fsdp", scatter_dimension=1, tiled=True
        ).astype(jnp.float32),
    )
    return (
        block_output,
        input_grad,
        summed[0],
        inner_out,
        timestep_out,
        state_out,
        query_out,
        keyvalue_out,
        summed[2],
        summed[3],
        summed[4],
        summed[5],
        summed[6],
        summed[7],
        mamba_out,
        attention_out,
        summed[1],
        gateup_out,
        down_out,
    )


BLOCK = 256
LOG2E = 1.4426950408889634
HIDDEN_BIAS = -1e30


def narrow(values):
    return values.astype(jnp.bfloat16)


def wide(values):
    return values.astype(jnp.float32)


def mm(left, right):
    return jnp.dot(left, right, preferred_element_type=jnp.float32)


def sigmoid(values):
    return 1.0 / (1.0 + jnp.exp(-values))


def dot_wide(ones, values):
    first = narrow(values)
    rest = values - wide(first)
    second = narrow(rest)
    third = narrow(rest - wide(second))
    return mm(ones, first) + mm(ones, second) + mm(ones, third)


def triangle(rows, upper):
    down = lax.broadcasted_iota(jnp.int32, (rows, rows), 0)
    across = lax.broadcasted_iota(jnp.int32, (rows, rows), 1)
    keep = (across >= down) if upper else (down >= across)
    return jnp.where(keep, 1.0, 0.0).astype(jnp.bfloat16)


def pair_bias(label_column, label_row):
    rows = label_column.shape[0]
    down = lax.broadcasted_iota(jnp.int32, (rows, rows), 0)
    across = lax.broadcasted_iota(jnp.int32, (rows, rows), 1)
    keep = jnp.logical_and(label_column == label_row, down >= across)
    return jnp.where(keep, 0.0, HIDDEN_BIAS)


def conv_taps(signal, info):
    taps = [signal]
    for distance in range(1, 4):
        taps.append(pltpu.roll(signal, distance, 0) * info[:, distance : distance + 1])
    return taps


def conv_pre(taps, channel):
    result = channel[4:5, :]
    for distance in range(4):
        result = result + channel[distance : distance + 1, :] * taps[distance]
    return result


def conv_back(grad_pre, channel, info):
    rows = grad_pre.shape[0]
    result = channel[0:1, :] * grad_pre
    for distance in range(1, 4):
        masked = grad_pre * info[:, distance : distance + 1]
        result = result + channel[distance : distance + 1, :] * pltpu.roll(masked, rows - distance, 0)
    return result


def column_of(values, lane):
    lanes = lax.broadcasted_iota(jnp.int32, values.shape, 1)
    return jnp.sum(jnp.where(lanes == lane, values, 0.0), 1, keepdims=True)


def half_lanes(values, which):
    lanes = lax.broadcasted_iota(jnp.int32, values.shape, 1)
    keep = (lanes < HEAD_SIZE) if which == 0 else (lanes >= HEAD_SIZE)
    return jnp.where(keep, values, jnp.zeros_like(values))


def spans(rows):
    return [slice(at, at + BLOCK) for at in range(0, rows, BLOCK)]


def mixer_forward_kernel(
    gate_ref,
    value_ref,
    state_ref,
    steps_ref,
    info_ref,
    label_ref,
    channel_ref,
    state_channel_ref,
    head_ref,
    low_ref,
    scanned_ref,
    square_ref,
    dt_ref,
    cum_ref,
    crossed,
    bias,
    source_rows,
):
    pair = pl.program_id(0)
    info = info_ref[...]
    rows = info.shape[0]

    @pl.when(pair == 0)
    def _():
        taps = conv_taps(state_ref[...], info)
        pre = conv_pre(taps, state_channel_ref[...])
        states = narrow(pre * sigmoid(pre))
        half = states.shape[1] // 2
        crossed[...] = contract_cols(states[:, half:], states[:, :half])
        bias[...] = pair_bias(info[:, 4:5], label_ref[0:1, :])
        raw = steps_ref[...] + head_ref[0:1, :]
        dt = jnp.maximum(raw, 0.0) + jnp.log1p(jnp.exp(-jnp.abs(raw)))
        cum = dot_wide(triangle(rows, False), dt * (head_ref[1:2, :] * LOG2E))
        dt_ref[...] = dt
        cum_ref[...] = cum
        source_rows[...] = (cum - jnp.log(dt) * LOG2E).T
        square_ref[...] = jnp.zeros_like(square_ref)

    channel = channel_ref[...]
    pre = conv_pre(conv_taps(value_ref[...], info), channel)
    values = narrow(pre * sigmoid(pre))
    outputs = [channel[5:6, :] * wide(values[span]) for span in spans(rows)]
    for which in range(2):
        head = 2 * pair + which
        target = column_of(cum_ref[...], head)
        source = source_rows[pl.ds(head, 1), :]
        chosen = half_lanes(values, which)
        for i, down in enumerate(spans(rows)):
            for across in spans(rows)[: i + 1]:
                weights = jnp.exp2((target[down] - source[:, across]) + bias[down, across])
                outputs[i] += mm(narrow(weights * crossed[down, across]), chosen[across])
    scanned = jnp.concatenate(outputs, 0)
    scanned_ref[...] = scanned
    gate = gate_ref[...]
    gated = scanned * (gate * sigmoid(gate))
    low_ref[...] = narrow(gated * channel[6:7, :])
    square_ref[...] += gated * gated


def mixer_backward_kernel(
    gate_ref,
    value_ref,
    state_ref,
    steps_ref,
    info_ref,
    label_ref,
    channel_ref,
    state_channel_ref,
    head_ref,
    scanned_ref,
    incoming_ref,
    dt_ref,
    cum_ref,
    grad_value_ref,
    grad_state_ref,
    grad_steps_ref,
    channel_grad_ref,
    state_grad_ref,
    head_grad_ref,
    crossed,
    bias,
    summed,
    states_low,
    source_rows,
    dt_rows,
    target_sums,
    source_sums,
):
    pair = pl.program_id(0)
    info = info_ref[...]
    rows = info.shape[0]
    half = state_ref.shape[1] // 2

    @pl.when(pair == 0)
    def _():
        pre = conv_pre(conv_taps(state_ref[...], info), state_channel_ref[...])
        states = narrow(pre * sigmoid(pre))
        states_low[...] = states
        crossed[...] = contract_cols(states[:, half:], states[:, :half])
        bias[...] = pair_bias(info[:, 4:5], label_ref[0:1, :])
        source_rows[...] = cum_ref[...].T
        dt_rows[...] = dt_ref[...].T
        summed[...] = jnp.zeros_like(summed)
        target_sums[...] = jnp.zeros_like(target_sums)
        source_sums[...] = jnp.zeros_like(source_sums)

    channel = channel_ref[...]
    taps = conv_taps(value_ref[...], info)
    pre = conv_pre(taps, channel)
    opened = sigmoid(pre)
    values = narrow(pre * opened)
    gate = gate_ref[...]
    gate_open = sigmoid(gate)
    silu_gate = gate * gate_open
    scanned = scanned_ref[...]
    gated = scanned * silu_gate
    incoming = incoming_ref[...]
    gain_grad = jnp.sum(incoming * gated, 0, keepdims=True)
    grad_gated = incoming * channel[6:7, :] + 2.0 * gated * info[:, 5:6]
    grad_scanned = grad_gated * silu_gate
    skip_grad = jnp.sum(grad_scanned * wide(values), 0, keepdims=True)
    low_grad = narrow(grad_scanned)
    value_grads = [channel[5:6, :] * grad_scanned[span] for span in spans(rows)]
    lanes = lax.broadcasted_iota(jnp.int32, (BLOCK, 128), 1)
    for which in range(2):
        head = 2 * pair + which
        target = column_of(cum_ref[...], head)
        dt_column = column_of(dt_ref[...], head)
        source = source_rows[pl.ds(head, 1), :]
        dt_row = dt_rows[pl.ds(head, 1), :]
        chosen = half_lanes(low_grad, which)
        returned = [jnp.zeros((BLOCK, 128), jnp.float32) for _ in spans(rows)]
        column_sums = [jnp.zeros((1, BLOCK), jnp.float32) for _ in spans(rows)]
        for i, down in enumerate(spans(rows)):
            row_sum = jnp.zeros((BLOCK, 1), jnp.float32)
            for j, across in enumerate(spans(rows)[: i + 1]):
                decay = jnp.exp2((target[down] - source[:, across]) + bias[down, across])
                linked = crossed[down, across]
                returned[j] += contract_rows(narrow(decay * linked), chosen[down])
                reach = decay * contract_cols(chosen[down], values[across])
                scaled = reach * dt_row[:, across]
                summed[down, across] += scaled
                column_sums[j] += jnp.sum(reach * linked, 0, keepdims=True)
                row_sum += jnp.sum(scaled * linked, 1, keepdims=True)
            target_sums[down, :] += jnp.where(lanes == head, row_sum, 0.0)
        for j, across in enumerate(spans(rows)):
            value_grads[j] += dt_column[across] * returned[j]
            source_sums[pl.ds(head, 1), across] = column_sums[j]
    grad_pre = jnp.concatenate(value_grads, 0) * (opened * (1.0 + pre * (1.0 - opened)))
    grad_value_ref[...] = narrow(conv_back(grad_pre, channel, info))
    channel_grad_ref[...] = jnp.concatenate(
        [jnp.sum(grad_pre * tap, 0, keepdims=True) for tap in taps]
        + [jnp.sum(grad_pre, 0, keepdims=True), skip_grad, gain_grad, jnp.zeros_like(gain_grad)],
        0,
    )

    @pl.when(pair == pl.num_programs(0) - 1)
    def _():
        low = narrow(summed[...])
        states = states_low[...]
        grad_keys = contract_rows(low, states[:, half:])
        grad_queries = mm(low, states[:, :half])
        state_channel = state_channel_ref[...]
        state_taps = conv_taps(state_ref[...], info)
        state_pre = conv_pre(state_taps, state_channel)
        state_open = sigmoid(state_pre)
        grad_state_pre = jnp.concatenate([grad_keys, grad_queries], 1) * (
            state_open * (1.0 + state_pre * (1.0 - state_open))
        )
        grad_state_ref[...] = narrow(conv_back(grad_state_pre, state_channel, info))
        state_grad_ref[...] = jnp.concatenate(
            [jnp.sum(grad_state_pre * tap, 0, keepdims=True) for tap in state_taps]
            + [jnp.sum(grad_state_pre, 0, keepdims=True)]
            + [jnp.zeros((3, 2 * half), jnp.float32)],
            0,
        )
        dt = dt_ref[...]
        rate = head_ref[1:2, :]
        source_columns = source_sums[...].T
        grad_rate = dot_wide(triangle(rows, True), target_sums[...] - dt * source_columns)
        grad_dt = source_columns + rate * grad_rate
        grad_steps = grad_dt * sigmoid(steps_ref[...] + head_ref[0:1, :])
        grad_steps_ref[...] = narrow(grad_steps)
        head_grad_ref[...] = jnp.concatenate(
            [
                jnp.sum(grad_steps, 0, keepdims=True),
                jnp.sum(grad_rate * dt * rate, 0, keepdims=True),
                jnp.zeros((6, 128), jnp.float32),
            ],
            0,
        )


def copies_of(starts_ref, pieces, whole, done, column=0):
    rows = pieces[0].shape[0]
    width = whole.shape[1]
    copies = []
    for at, piece in enumerate(pieces):
        start = pl.multiple_of(starts_ref[at] * rows, rows)
        copies.append(
            pltpu.make_async_copy(
                piece.at[:, column : column + width], whole.at[pl.ds(start, rows)], done.at[at]
            )
        )
    for copy in copies:
        copy.start()
    return copies


def wait_all(copies):
    for copy in copies:
        copy.wait()


def smem():
    return pl.BlockSpec(memory_space=pltpu.SMEM)


def vmem():
    return pl.BlockSpec(memory_space=pltpu.VMEM)


def hbm():
    return pl.BlockSpec(memory_space=pltpu.HBM)


def rotated(values, cosine, sinusoid):
    lanes = lax.broadcasted_iota(jnp.int32, values.shape, 1)
    quarter = HEAD_SIZE // 2
    swapped = jnp.where(
        lanes % HEAD_SIZE < quarter,
        pltpu.roll(values, values.shape[1] - quarter, 1),
        pltpu.roll(values, quarter, 1),
    )
    return values * cosine + swapped * sinusoid


def attention_forward_kernel(
    count,
    query_width,
    rank_ref,
    starts_ref,
    normed_ref,
    info_ref,
    label_ref,
    cosine_ref,
    sinusoid_ref,
    gated_ref,
    factor_ref,
    *refs,
):
    pieces = refs[:count]
    attended_ref, turned_ref, key_ref, value_ref, logsum_ref, mamba_ref, mixed_ref = refs[count:-4]
    bias, projected, whole, done = refs[-4:]
    copies = copies_of(starts_ref, pieces, whole, done)
    rows = normed_ref.shape[0]
    cosine, sinusoid = cosine_ref[...], sinusoid_ref[...]
    bias[...] = pair_bias(info_ref[:, 4:5], label_ref[0:1, :])
    wait_all(copies)
    end = projected.shape[1]
    for at in range(0, end, 256):
        projected[:, at : at + 256] = mm(normed_ref[...], whole[:, at : at + 256])
    lanes = lax.broadcasted_iota(jnp.int32, (rows, 128), 1)
    own = (lanes < HEAD_SIZE) == (rank_ref[0] == 0)

    def doubled(values):
        return jnp.where(own, values, pltpu.roll(values, HEAD_SIZE, 1))

    middle = query_width + 128
    keys = narrow(doubled(rotated(projected[:, query_width:middle], cosine, sinusoid)))
    values = narrow(doubled(projected[:, middle : middle + 128]))
    key_ref[...] = keys
    value_ref[...] = values
    scaling = 1.0 / math.sqrt(HEAD_SIZE)
    logsums = [jnp.zeros((BLOCK, 128), jnp.float32) for _ in spans(rows)]
    block_lanes = lax.broadcasted_iota(jnp.int32, (BLOCK, 128), 1)
    for pair in range(query_width // 128):
        columns = slice(128 * pair, 128 * pair + 128)
        queries = narrow(rotated(projected[:, columns], cosine, sinusoid))
        turned_ref[:, columns] = queries
        results = [jnp.zeros((BLOCK, 128), jnp.float32) for _ in spans(rows)]
        for which in range(2):
            chosen = half_lanes(queries, which)
            reading = half_lanes(values, which)
            for i, down in enumerate(spans(rows)):
                width = BLOCK * (i + 1)
                scores = contract_cols(chosen[down], keys[:width]) * scaling + bias[down, :width]
                highest = jnp.max(scores, 1, keepdims=True)
                weights = jnp.exp(scores - highest)
                total = jnp.sum(weights, 1, keepdims=True)
                results[i] += mm(narrow(weights * (1.0 / total)), reading[:width])
                logsums[i] = jnp.where(
                    block_lanes == 2 * pair + which, highest + jnp.log(total), logsums[i]
                )
        for i, down in enumerate(spans(rows)):
            attended_ref[down, columns] = narrow(results[i])
    for i, down in enumerate(spans(rows)):
        logsum_ref[down, :] = logsums[i]
    gated_end = end + gated_ref.shape[1]
    for at in range(0, whole.shape[0], 256):
        span = slice(at, at + 256)
        mamba = contract_cols(gated_ref[...], whole[span, end:gated_end])
        mamba_ref[:, span] = narrow(mamba)
        part = contract_cols(attended_ref[...], whole[span, gated_end:])
        mixed_ref[:, span] = narrow(factor_ref[...] * mamba + part)


def attention_backward_kernel(
    count,
    column,
    rank_ref,
    starts_ref,
    mix_ref,
    turned_ref,
    key_ref,
    value_ref,
    logsum_ref,
    info_ref,
    label_ref,
    cosine_ref,
    sinusoid_ref,
    *refs,
):
    pieces = refs[:count]
    grad_query_ref, grad_keyvalue_ref, bias, down, done = refs[count:]
    copies = copies_of(starts_ref, pieces, down, done, column)
    rows = turned_ref.shape[0]
    cosine, sinusoid = cosine_ref[...], sinusoid_ref[...]
    bias[...] = pair_bias(info_ref[:, 4:5], label_ref[0:1, :])
    keys, values = key_ref[...], value_ref[...]
    wait_all(copies)
    grad_attended = narrow(mm(mix_ref[...], down[...]))
    scaling = 1.0 / math.sqrt(HEAD_SIZE)
    zero = jnp.zeros((BLOCK, 128), jnp.float32)
    key_grads = [zero for _ in spans(rows)]
    value_grads = [zero for _ in spans(rows)]
    for pair in range(turned_ref.shape[1] // 128):
        columns = slice(128 * pair, 128 * pair + 128)
        query_grads = [zero for _ in spans(rows)]
        for which in range(2):
            queries = half_lanes(turned_ref[:, columns], which)
            incoming = half_lanes(grad_attended[:, columns], which)
            reading = half_lanes(keys, which)
            head = 2 * pair + which
            for i, down in enumerate(spans(rows)):
                width = BLOCK * (i + 1)
                scores = contract_cols(queries[down], keys[:width]) * scaling + bias[down, :width]
                probs = jnp.exp(scores - logsum_ref[down, head : head + 1])
                grad_probs = contract_cols(incoming[down], values[:width])
                inner_sum = jnp.sum(grad_probs * probs, 1, keepdims=True)
                grad_scores = narrow(probs * (grad_probs - inner_sum))
                probs_low = narrow(probs)
                query_grads[i] += mm(grad_scores, reading[:width])
                for j, across in enumerate(spans(rows)[: i + 1]):
                    key_grads[j] += contract_rows(grad_scores[:, across], queries[down])
                    value_grads[j] += contract_rows(probs_low[:, across], incoming[down])
        grad_query_ref[:, columns] = narrow(
            rotated(jnp.concatenate(query_grads, 0) * scaling, cosine, -sinusoid)
        )
    lanes = lax.broadcasted_iota(jnp.int32, (rows, 128), 1)
    own = (lanes < HEAD_SIZE) == (rank_ref[0] == 0)

    def placed(values):
        return jnp.where(own, values + pltpu.roll(values, HEAD_SIZE, 1), 0.0)

    key_grad = rotated(placed(jnp.concatenate(key_grads, 0) * scaling), cosine, -sinusoid)
    grad_keyvalue_ref[:, :128] = narrow(key_grad)
    grad_keyvalue_ref[:, 128:] = narrow(placed(jnp.concatenate(value_grads, 0)))


def block_spec(shape, index):
    return pl.BlockSpec(shape, index)


def fixed(array):
    return pl.BlockSpec(array.shape, lambda p: (0, 0))


def params():
    return pltpu.CompilerParams(vmem_limit_bytes=62 * 1024 * 1024)


def mixer_forward(projected, widths, info, labels, channel, state_channel, heads):
    rows = info.shape[0]
    width, state_at, steps_at = widths
    pairs = width // 128
    state_width = state_channel.shape[1]
    column = lambda p: (0, p)
    return pl.pallas_call(
        mixer_forward_kernel,
        grid=(pairs,),
        in_specs=[
            block_spec((rows, 128), column),
            block_spec((rows, 128), lambda p: (0, pairs + p)),
            block_spec((rows, state_width), lambda p: (0, state_at // state_width)),
            block_spec((rows, 128), lambda p: (0, steps_at // 128)),
            fixed(info),
            fixed(labels),
            block_spec((8, 128), column),
            fixed(state_channel),
            fixed(heads),
        ],
        out_specs=[
            block_spec((rows, 128), column),
            block_spec((rows, 128), column),
            block_spec((rows, 128), lambda p: (0, 0)),
            block_spec((rows, 128), lambda p: (0, 0)),
            block_spec((rows, 128), lambda p: (0, 0)),
        ],
        out_shape=[
            jax.ShapeDtypeStruct((rows, width), jnp.bfloat16),
            jax.ShapeDtypeStruct((rows, width), jnp.float32),
            jax.ShapeDtypeStruct((rows, 128), jnp.float32),
            jax.ShapeDtypeStruct((rows, 128), jnp.float32),
            jax.ShapeDtypeStruct((rows, 128), jnp.float32),
        ],
        scratch_shapes=[
            pltpu.VMEM((rows, rows), jnp.float32),
            pltpu.VMEM((rows, rows), jnp.float32),
            pltpu.VMEM((128, rows), jnp.float32),
        ],
        compiler_params=params(),
        cost_estimate=pl.CostEstimate(flops=1, bytes_accessed=1, transcendentals=0),
        name="mixer_forward",
    )(projected, projected, projected, projected, info, labels, channel, state_channel, heads)


def mixer_backward(
    projected, widths, info, labels, channel, state_channel, heads, scanned, incoming, dt, cum
):
    rows = info.shape[0]
    width, state_at, steps_at = widths
    pairs = width // 128
    state_width = state_channel.shape[1]
    column = lambda p: (0, p)
    still = lambda p: (0, 0)
    return pl.pallas_call(
        mixer_backward_kernel,
        grid=(pairs,),
        in_specs=[
            block_spec((rows, 128), column),
            block_spec((rows, 128), lambda p: (0, pairs + p)),
            block_spec((rows, state_width), lambda p: (0, state_at // state_width)),
            block_spec((rows, 128), lambda p: (0, steps_at // 128)),
            fixed(info),
            fixed(labels),
            block_spec((8, 128), column),
            fixed(state_channel),
            fixed(heads),
            block_spec((rows, 128), column),
            block_spec((rows, 128), column),
            fixed(dt),
            fixed(cum),
        ],
        out_specs=[
            block_spec((rows, 128), column),
            block_spec((rows, state_width), still),
            block_spec((rows, 128), still),
            block_spec((8, 128), column),
            block_spec((8, state_width), still),
            block_spec((8, 128), still),
        ],
        out_shape=[
            jax.ShapeDtypeStruct((rows, width), jnp.bfloat16),
            jax.ShapeDtypeStruct((rows, state_width), jnp.bfloat16),
            jax.ShapeDtypeStruct((rows, 128), jnp.bfloat16),
            jax.ShapeDtypeStruct((8, width), jnp.float32),
            jax.ShapeDtypeStruct((8, state_width), jnp.float32),
            jax.ShapeDtypeStruct((8, 128), jnp.float32),
        ],
        scratch_shapes=[
            pltpu.VMEM((rows, rows), jnp.float32),
            pltpu.VMEM((rows, rows), jnp.float32),
            pltpu.VMEM((rows, rows), jnp.float32),
            pltpu.VMEM((rows, state_width), jnp.bfloat16),
            pltpu.VMEM((128, rows), jnp.float32),
            pltpu.VMEM((128, rows), jnp.float32),
            pltpu.VMEM((rows, 128), jnp.float32),
            pltpu.VMEM((128, rows), jnp.float32),
        ],
        compiler_params=params(),
        cost_estimate=pl.CostEstimate(flops=1, bytes_accessed=1, transcendentals=0),
        name="mixer_backward",
    )(
        projected,
        projected,
        projected,
        projected,
        info,
        labels,
        channel,
        state_channel,
        heads,
        scanned,
        incoming,
        dt,
        cum,
    )


def attention_forward(
    rank, starts, normed, info, labels, cosine, sinusoid, gated, factor, pieces, query_width
):
    rows, model = normed.shape
    count = len(pieces)
    columns = pieces[0].shape[1]
    end = columns - gated.shape[1] - query_width
    arrays = (normed, info, labels, cosine, sinusoid, gated, factor)
    return pl.pallas_call(
        lambda *refs: attention_forward_kernel(count, query_width, *refs),
        in_specs=[smem(), smem()] + [vmem()] * len(arrays) + [hbm()] * count,
        out_specs=[vmem()] * 7,
        out_shape=[
            jax.ShapeDtypeStruct((rows, query_width), jnp.bfloat16),
            jax.ShapeDtypeStruct((rows, query_width), jnp.bfloat16),
            jax.ShapeDtypeStruct((rows, 128), jnp.bfloat16),
            jax.ShapeDtypeStruct((rows, 128), jnp.bfloat16),
            jax.ShapeDtypeStruct((rows, 128), jnp.float32),
            jax.ShapeDtypeStruct((rows, model), jnp.bfloat16),
            jax.ShapeDtypeStruct((rows, model), jnp.bfloat16),
        ],
        scratch_shapes=[
            pltpu.VMEM((rows, rows), jnp.float32),
            pltpu.VMEM((rows, end), jnp.float32),
            pltpu.VMEM((model, columns), jnp.bfloat16),
            pltpu.SemaphoreType.DMA((count,)),
        ],
        compiler_params=params(),
        cost_estimate=pl.CostEstimate(flops=1, bytes_accessed=1, transcendentals=0),
        name="attention_forward",
    )(rank, starts, *arrays, *pieces)


def attention_backward(
    rank, starts, mix, turned, keys, values, logsum, info, labels, cosine, sinusoid, pieces, column
):
    rows, query_width = turned.shape
    count = len(pieces)
    model = mix.shape[1]
    arrays = (mix, turned, keys, values, logsum, info, labels, cosine, sinusoid)
    return pl.pallas_call(
        lambda *refs: attention_backward_kernel(count, column, *refs),
        in_specs=[smem(), smem()] + [vmem()] * len(arrays) + [hbm()] * count,
        out_specs=[vmem()] * 2,
        out_shape=[
            jax.ShapeDtypeStruct((rows, query_width), jnp.bfloat16),
            jax.ShapeDtypeStruct((rows, 256), jnp.bfloat16),
        ],
        scratch_shapes=[
            pltpu.VMEM((rows, rows), jnp.float32),
            pltpu.VMEM((model, query_width), jnp.bfloat16),
            pltpu.SemaphoreType.DMA((count,)),
        ],
        compiler_params=params(),
        cost_estimate=pl.CostEstimate(flops=1, bytes_accessed=1, transcendentals=0),
        name="attention_backward",
    )(rank, starts, *arrays, *pieces)


def project_kernel(count, starts_ref, input_ref, gain_ref, *refs):
    pieces, out_ref, normed_ref, whole, done = refs[:count], *refs[count:]
    copies = copies_of(starts_ref, pieces, whole, done)
    residual = wide(input_ref[...])
    normed_ref[...] = narrow(residual * inverse_rms(residual) * gain_ref[...])
    wait_all(copies)
    left = normed_ref[...]
    columns = out_ref.shape[1]
    for at in range(0, columns, 256):
        span = slice(at, min(at + 256, columns))
        out_ref[:, span] = mm(left, whole[:, span])


def project(starts, pieces, left, gain):
    count = len(pieces)
    rows, columns = pieces[0].shape
    return pl.pallas_call(
        lambda *refs: project_kernel(count, *refs),
        in_specs=[
            pl.BlockSpec(memory_space=pltpu.SMEM),
            pl.BlockSpec(memory_space=pltpu.VMEM),
            pl.BlockSpec(memory_space=pltpu.VMEM),
        ]
        + [pl.BlockSpec(memory_space=pltpu.HBM)] * count,
        out_specs=[pl.BlockSpec(memory_space=pltpu.VMEM)] * 2,
        out_shape=[
            jax.ShapeDtypeStruct((left.shape[0], columns), jnp.float32),
            jax.ShapeDtypeStruct(left.shape, jnp.bfloat16),
        ],
        scratch_shapes=[
            pltpu.VMEM((count * rows, columns), jnp.bfloat16),
            pltpu.SemaphoreType.DMA((count,)),
        ],
        compiler_params=params(),
        cost_estimate=pl.CostEstimate(flops=1, bytes_accessed=1, transcendentals=0),
        name="project",
    )(starts, left, gain, *pieces)


def back_kernel(count, parts, starts_ref, *refs):
    lefts, pieces = refs[:parts], refs[parts : parts + 2 * count]
    out_ref, whole, shared, done, shared_done = refs[-5:]
    copies = copies_of(starts_ref, pieces[:count], whole, done)
    copies += copies_of(starts_ref, pieces[count:], shared, shared_done)
    wait_all(copies)
    model = whole.shape[0]
    for at in range(0, model, 256):
        span = slice(at, at + 256)
        total = jnp.zeros((out_ref.shape[0], 256), jnp.float32)
        for weight, several in ((whole, lefts[:-2]), (shared, lefts[-2:])):
            column = 0
            for left in several:
                total += contract_cols(left[...], weight[span, column : column + left.shape[1]])
                column += left.shape[1]
        out_ref[:, span] = narrow(total)


def back_project(starts, pieces, shared_pieces, lefts):
    count = len(pieces)
    rows, columns = pieces[0].shape
    shared = lefts[-2].shape[1] + lefts[-1].shape[1]
    parts = len(lefts)
    tokens = lefts[0].shape[0]
    return pl.pallas_call(
        lambda *refs: back_kernel(count, parts, *refs),
        in_specs=[smem()] + [vmem()] * parts + [hbm()] * (2 * count),
        out_specs=vmem(),
        out_shape=jax.ShapeDtypeStruct((tokens, count * rows), jnp.bfloat16),
        scratch_shapes=[
            pltpu.VMEM((count * rows, columns), jnp.bfloat16),
            pltpu.VMEM((count * rows, shared), jnp.bfloat16),
            pltpu.SemaphoreType.DMA((count,)),
            pltpu.SemaphoreType.DMA((count,)),
        ],
        compiler_params=params(),
        cost_estimate=pl.CostEstimate(flops=1, bytes_accessed=1, transcendentals=0),
        name="back_project",
    )(starts, *lefts, *pieces, *shared_pieces)


def feed_kernel(
    count, hidden, starts_ref, residual_ref, mixed_ref, far_ref, gain_ref, cotangent_ref, *refs
):
    pieces = refs[:count]
    middle_ref, input_ref, activated_ref, grad_ref, low_ref, forward_ref, whole, done = refs[count:]
    copies = copies_of(starts_ref, pieces, whole, done)
    middle = wide(residual_ref[...]) + (wide(mixed_ref[...]) + wide(far_ref[...]))
    middle_ref[...] = middle
    input_ref[...] = narrow(middle * inverse_rms(middle) * gain_ref[...])
    wait_all(copies)

    def tile(step, carry):
        at = pl.multiple_of(step * 256, 256)
        far = pl.multiple_of(hidden + step * 256, 256)
        last = pl.multiple_of(2 * hidden + step * 256, 256)
        gate = mm(input_ref[...], whole[:, pl.ds(at, 256)])
        up = mm(input_ref[...], whole[:, pl.ds(far, 256)])
        grad = mm(cotangent_ref[...], whole[:, pl.ds(last, 256)])
        opened = sigmoid(gate)
        silu = gate * opened
        activated_ref[:, pl.ds(at, 256)] = narrow(silu * up)
        grad_ref[:, pl.ds(far, 256)] = narrow(grad * silu)
        grad_ref[:, pl.ds(at, 256)] = narrow(grad * up * opened * (1.0 + gate * (1.0 - opened)))
        return carry

    lax.fori_loop(0, hidden // 256, tile, 0)
    model = whole.shape[0]
    for at in range(0, model, 256):
        span = slice(at, at + 256)
        low_ref[:, span] = narrow(contract_cols(grad_ref[...], whole[span, : 2 * hidden]))
    for at in range(0, model, 256):
        span = slice(at, at + 256)
        forward_ref[:, span] = narrow(contract_cols(activated_ref[...], whole[span, 2 * hidden :]))


def feed_forward(starts, pieces, hidden, residual, mixed, far, gain, cotangent):
    count = len(pieces)
    rows, columns = pieces[0].shape
    tokens, model = residual.shape
    return pl.pallas_call(
        lambda *refs: feed_kernel(count, hidden, *refs),
        in_specs=[smem()] + [vmem()] * 5 + [hbm()] * count,
        out_specs=[vmem()] * 6,
        out_shape=[
            jax.ShapeDtypeStruct((tokens, model), jnp.float32),
            jax.ShapeDtypeStruct((tokens, model), jnp.bfloat16),
            jax.ShapeDtypeStruct((tokens, hidden), jnp.bfloat16),
            jax.ShapeDtypeStruct((tokens, 2 * hidden), jnp.bfloat16),
            jax.ShapeDtypeStruct((tokens, model), jnp.bfloat16),
            jax.ShapeDtypeStruct((tokens, model), jnp.bfloat16),
        ],
        scratch_shapes=[
            pltpu.VMEM((count * rows, columns), jnp.bfloat16),
            pltpu.SemaphoreType.DMA((count,)),
        ],
        compiler_params=params(),
        cost_estimate=pl.CostEstimate(flops=1, bytes_accessed=1, transcendentals=0),
        name="feed_forward",
    )(starts, residual, mixed, far, gain, cotangent, *pieces)


def gate_kernel(
    count,
    column,
    starts_ref,
    grad_mamba_ref,
    gate_ref,
    scanned_ref,
    gain_ref,
    square_ref,
    turned_ref,
    order_ref,
    mix_ref,
    factor_ref,
    gated_ref,
    attended_ref,
    query_ref,
    key_ref,
    *refs,
):
    pieces = refs[:count]
    incoming_ref, grad_ref, far_ref, line_ref, own_ref, weight, done = refs[count:]
    copies = copies_of(starts_ref, pieces, weight, done, column)
    outs = (far_ref, line_ref, own_ref)
    mixed = narrow(contract_cols(order_ref[...], mix_ref[...]))
    end = grads_kernel(narrow(factor_ref[...] * wide(mixed)), [gated_ref], *outs, 0)
    end = grads_kernel(mixed, [attended_ref], *outs, end)
    end = grads_kernel(turned_ref[...], [query_ref, key_ref], *outs, end)
    gate = gate_ref[...]
    opened = sigmoid(gate)
    scanned = scanned_ref[...]
    wait_all(copies)
    incoming = mm(grad_mamba_ref[...], weight[...])
    incoming_ref[...] = incoming
    grad_gated = incoming * gain_ref[...] + 2.0 * scanned * (gate * opened) * square_ref[...]
    grad_ref[...] = narrow(grad_gated * scanned * opened * (1.0 + gate * (1.0 - opened)))
    grads_kernel(turned_ref[...], [grad_ref], *outs, end)


def gate_backward(starts, projected, scanned, arrays, pieces, column, columns):
    rows, width = scanned.shape
    model = pieces[0].shape[0] * len(pieces)
    count = len(pieces)
    still = lambda p: (0, 0)
    grad_mamba, *others = arrays
    shapes = [
        ((rows, width), jnp.float32),
        ((rows, width), jnp.bfloat16),
        ((model // 2, columns), jnp.bfloat16),
        ((model // 4, columns), jnp.bfloat16),
        ((model // 4, columns), jnp.bfloat16),
    ]
    return pl.pallas_call(
        lambda *refs: gate_kernel(count, column, *refs),
        grid=(1,),
        in_specs=[
            smem(),
            fixed(grad_mamba),
            block_spec((rows, width), still),
            fixed(scanned),
        ]
        + [fixed(array) for array in others]
        + [hbm()] * count,
        out_specs=[block_spec(shape, still) for shape, _ in shapes],
        out_shape=[jax.ShapeDtypeStruct(shape, kind) for shape, kind in shapes],
        scratch_shapes=[
            pltpu.VMEM((model, width), jnp.bfloat16),
            pltpu.SemaphoreType.DMA((count,)),
        ],
        compiler_params=params(),
        cost_estimate=pl.CostEstimate(flops=1, bytes_accessed=1, transcendentals=0),
        name="gate_backward",
    )(starts, grad_mamba, projected, scanned, *others, *pieces)


def swaps(size, bit):
    return [(i, i ^ bit) for i in range(size)]


def ring(size):
    return [(i, (i + 4) % size) for i in range(size)]


def tie(*values):
    return lax.optimization_barrier(values)


class Gathering:
    def __init__(self, shards, size):
        self.size = size
        self.held = {(group, 0): shard for group, shard in enumerate(shards)}
        self.lined, self.crossed, self.flying = {}, {}, {}

    def step(self, begun, awaited, main):
        def send(value, pairs):
            return lax.ppermute(value, "fsdp", pairs)

        for kind, group, k in begun:
            if kind == "z":
                value = send(self.held[group, k - 1], ring(self.size))
            elif kind == "r":
                value = send(self.held[group, 0], [(j, i) for i, j in ring(self.size)])
            elif kind == "x":
                value = send(self.held[group, k], swaps(self.size, 2))
            else:
                value = [
                    send(self.held[group, k], swaps(self.size, 1)),
                    send(self.lined[group, k], swaps(self.size, 1)),
                ]
                if (kind, group, k) not in awaited:
                    self.crossed[group, k] = value
                    continue
            self.flying[kind, group, k] = value
        values = main()
        self.held, landed, values = lax.optimization_barrier(
            (self.held, [self.flying.pop(key) for key in awaited], values)
        )
        for (kind, group, k), value in zip(awaited, landed):
            kept = {"x": self.lined, "c": self.crossed}.get(kind, self.held)
            kept[group, k] = value
        return values

    def pieces(self, group):
        return [
            piece
            for k in range(self.size // 4)
            for piece in (
                self.held[group, k],
                self.crossed[group, k][0],
                self.lined[group, k],
                self.crossed[group, k][1],
            )
        ]


def grads_kernel(turned, rights, far_ref, line_ref, own_ref, column):
    half = turned.shape[0] // 2
    quarter = half // 2
    for right in rights:
        width = right.shape[1]
        for at in range(0, width, 256):
            size = min(256, width - at)
            product = narrow(mm(turned, right[:, at : at + size]))
            span = slice(column + at, column + at + size)
            far_ref[:, span] = product[half:]
            line_ref[:, span] = product[quarter:half]
            own_ref[:, span] = product[:quarter]
        column += width
    return column


def last_kernel(turned_ref, *refs):
    grads_kernel(turned_ref[...], refs[:-3], *refs[-3:], 0)


def feed_grads_kernel(order_ref, turned_ref, input_ref, activated_ref, grad_ref, *outs):
    column = grads_kernel(turned_ref[...], [activated_ref], *outs, 0)
    turned = narrow(contract_cols(order_ref[...], input_ref[...]))
    grads_kernel(turned, [grad_ref], *outs, column)


def weight_grads(kernel, arrays, model, columns, name):
    return pl.pallas_call(
        kernel,
        in_specs=[vmem()] * len(arrays),
        out_specs=[vmem()] * 3,
        out_shape=[
            jax.ShapeDtypeStruct((rows, columns), jnp.bfloat16)
            for rows in (model // 2, model // 4, model // 4)
        ],
        compiler_params=params(),
        cost_estimate=pl.CostEstimate(flops=1, bytes_accessed=1, transcendentals=0),
        name=name,
    )(*arrays)


def send_core(far, size):
    return lax.ppermute(far, "fsdp", swaps(size, 1))


def send_line(line, size):
    return lax.ppermute(line, "fsdp", swaps(size, 2))


def send_ring(total, size):
    return lax.ppermute(total, "fsdp", ring(size))


def add_core(came, line, own):
    half = own.shape[0]
    return narrow(wide(line) + wide(came[half:])), narrow(wide(own) + wide(came[:half]))


def add_line(came, own, size):
    return narrow(wide(own) + wide(came)).reshape(size // 4, -1, own.shape[1])


def add_ring(parts, came, step):
    total = wide(parts[(step + 1) % parts.shape[0]]) + wide(came)
    return total if step + 1 == parts.shape[0] else narrow(total)


def packed_body(
    size,
    block_input,
    segment_ids,
    output_cotangent,
    input_gain,
    inner_weight,
    timestep_weight,
    state_weight,
    query_weight,
    keyvalue_matrix,
    conv_kernel,
    conv_offset,
    timestep_bias,
    decay_log,
    skip_scale,
    gated_gain,
    mamba_down,
    attention_down,
    middle_gain,
    gateup_weight,
    down_weight,
):
    rank = lax.axis_index("tp")
    at = lax.axis_index("fsdp")
    depth = size // 4
    rows = segment_ids.shape[0]
    own_rows = rows // 2
    shard, _, width = inner_weight.shape
    model = shard * size
    heads = timestep_weight.shape[1]
    state_width = state_weight.shape[1]
    query_width = query_weight.shape[1]
    keyvalue_width = keyvalue_matrix.shape[1]
    attended_width = attention_down.shape[0]
    hidden = gateup_weight.shape[2]
    ssm_width = gated_gain.shape[0]
    state_at = 2 * width
    steps_at = state_at + state_width

    def other(values):
        return lax.ppermute(values, "tp", swaps(2, 1))

    def joined(own, far):
        first = jnp.where(rank == 0, own, far)
        second = jnp.where(rank == 0, far, own)
        return jnp.concatenate([first, second], 0)

    def own_half(values):
        return lax.dynamic_slice_in_dim(values, rank * own_rows, own_rows, 0)

    def far_half(values):
        return lax.dynamic_slice_in_dim(values, (1 - rank) * own_rows, own_rows, 0)

    first_shard = jnp.concatenate(
        [
            inner_weight.reshape(shard, 2 * width),
            state_weight,
            jnp.pad(timestep_weight, ((0, 0), (0, 128 - heads))),
        ],
        1,
    )
    second_shard = jnp.concatenate(
        [query_weight, keyvalue_matrix, jnp.concatenate([mamba_down, attention_down], 0).T], 1
    )
    third_shard = jnp.concatenate([gateup_weight.reshape(shard, 2 * hidden), down_weight.T], 1)
    ring_at, x_at, core_at = at // 4, (at // 2) % 2, at % 2

    def block_of(distance, x_flip, core_flip):
        return ((ring_at - distance + depth) % depth) * 4 + (x_at ^ x_flip) * 2 + (
            core_at ^ core_flip
        )

    starts = jnp.stack(
        [block_of(k, i, j) for k in range(depth) for i in range(2) for j in range(2)]
    ).astype(jnp.int32)
    relative = jnp.arange(model, dtype=jnp.int32)
    piece_at = relative // shard
    absolute = (
        block_of(piece_at % depth, (piece_at // depth) % 2, piece_at // (2 * depth)) * shard
        + relative % shard
    )
    order = (absolute[:, None] == relative[None, :]).astype(jnp.bfloat16)

    labels = segment_ids.astype(jnp.float32)
    info = [jnp.zeros((rows, 1), jnp.float32)]
    for distance in range(1, 4):
        earlier = jnp.concatenate([jnp.full((distance,), -1.0), labels[:-distance]], 0)
        info.append((earlier == labels).astype(jnp.float32)[:, None])
    info = jnp.concatenate(info + [labels[:, None], jnp.zeros((rows, 123), jnp.float32)], 1)
    label_rows = jnp.broadcast_to(labels[None, :], (8, rows))
    repeat = width // heads
    local_skip = lax.dynamic_slice_in_dim(skip_scale, rank * heads, heads, 0)
    local = lambda array: lax.dynamic_slice_in_dim(array, rank * width, width, array.ndim - 1)
    local_gain = local(gated_gain)
    channel = jnp.concatenate(
        [
            local(conv_kernel),
            local(conv_offset)[None],
            jnp.repeat(local_skip, repeat)[None],
            local_gain[None],
            jnp.zeros((1, width), jnp.float32),
        ],
        0,
    )
    state_channel = jnp.concatenate(
        [
            conv_kernel[:, ssm_width:],
            conv_offset[None, ssm_width:],
            jnp.zeros((3, state_width), jnp.float32),
        ],
        0,
    )
    local_head = lambda array: lax.dynamic_slice_in_dim(array, rank * heads, heads, 0)
    head_rows = jnp.pad(
        jnp.stack([local_head(timestep_bias), -jnp.exp(local_head(decay_log))]),
        ((0, 6), (0, 128 - heads)),
    )
    quarter = HEAD_SIZE // 2
    frequency = jnp.exp(
        jnp.arange(quarter, dtype=jnp.float32) * (-2.0 * math.log(ROPE_BASE) / HEAD_SIZE)
    )
    angles = jnp.arange(rows, dtype=jnp.float32)[:, None] * frequency[None, :]
    cosine = jnp.concatenate([jnp.cos(angles)] * 4, 1)
    sinusoid = jnp.sin(angles)
    sinusoid = jnp.concatenate([-sinusoid, sinusoid, -sinusoid, sinusoid], 1)
    rank_array = rank.astype(jnp.int32)[None]
    mixer_widths = (width, state_at, steps_at)

    gathering = Gathering([first_shard, second_shard, third_shard], size)
    step = gathering.step
    empty = lambda: ()
    far_input = other(block_input)
    step([("z", 0, 1), ("x", 0, 0)], [("z", 0, 1)], empty)
    tables = step(
        [("z", 0, 2), ("x", 0, 1)],
        [("z", 0, 2), ("x", 0, 0)],
        lambda: (info, label_rows, channel, state_channel, head_rows),
    )
    info, label_rows, channel, state_channel, head_rows = tables
    group_input, cosine, sinusoid, order = step(
        [("z", 0, 3), ("x", 0, 2), ("c", 0, 0)],
        [("z", 0, 3), ("x", 0, 1)],
        lambda: (joined(block_input, far_input), cosine, sinusoid, order),
    )
    step(
        [("x", 0, 3), ("z", 1, 1), ("c", 0, 1)], [("z", 1, 1), ("x", 0, 2), ("x", 0, 3)], empty
    )
    projected, normed = step(
        [("c", 0, 2), ("c", 0, 3), ("x", 1, 0), ("z", 1, 2), ("x", 1, 1), ("r", 1, 3)],
        [("z", 1, 2), ("x", 1, 0), ("r", 1, 3), ("x", 1, 1)],
        lambda: project(starts, gathering.pieces(0), group_input, input_gain[None]),
    )

    def mix_forward():
        return mixer_forward(
            projected, mixer_widths, info, label_rows, channel, state_channel, head_rows
        )

    gated_low, scanned, square_lanes, dt, cum = step(
        [("x", 1, 2), ("x", 1, 3), ("z", 2, 1), ("x", 2, 0), ("c", 1, 0), ("c", 1, 1)],
        [("x", 1, 2), ("x", 1, 3), ("z", 2, 1)],
        mix_forward,
    )
    square_own = jnp.sum(square_lanes, 1)
    squares, far_cotangent = step(
        [("c", 1, 2), ("c", 1, 3)],
        [("c", 1, 2), ("c", 1, 3)],
        lambda: (square_own + other(square_own), other(output_cotangent)),
    )
    norm_factor = lax.rsqrt(squares / ssm_width + EPSILON)
    factor = wide(narrow(norm_factor))[:, None]

    def attend():
        return (
            attention_forward(
                rank_array,
                starts,
                normed,
                info,
                label_rows,
                cosine,
                sinusoid,
                gated_low,
                factor,
                gathering.pieces(1),
                query_width,
            ),
            far_cotangent,
        )

    attending, far_cotangent = step(
        [("x", 2, 1), ("z", 2, 2)], [("z", 2, 2), ("x", 2, 0)], attend
    )
    attended, turned, keys, values, logsum, mamba_own, mixed_low = attending
    mixed_first, normed_turned, cotangent = step(
        [("z", 2, 3), ("x", 2, 2), ("c", 2, 0)],
        [("z", 2, 3), ("x", 2, 1)],
        lambda: (
            other(mixed_low[:own_rows]),
            narrow(contract_cols(order, normed)),
            joined(output_cotangent, far_cotangent),
        ),
    )
    mixed_second, cotangent_turned = step(
        [("x", 2, 3), ("c", 2, 1)],
        [("x", 2, 2), ("x", 2, 3)],
        lambda: (other(mixed_low[own_rows:]), narrow(contract_cols(order, cotangent))),
    )
    step([("c", 2, 2), ("c", 2, 3)], [], empty)
    mixed_far = jnp.concatenate([mixed_first, mixed_second], 0)
    middle, hidden_in, activated, grad_gateup, hidden_low, feedforward_low = feed_forward(
        starts,
        gathering.pieces(2),
        hidden,
        group_input,
        mixed_low,
        mixed_far,
        middle_gain[None],
        cotangent,
    )

    hidden_first = other(hidden_low[:own_rows])
    feed_far, feed_line, feed_own = weight_grads(
        feed_grads_kernel,
        [order, cotangent_turned, hidden_in, activated, grad_gateup],
        model,
        3 * hidden,
        "feed_grads",
    )
    hidden_first, feed_far, hidden_low, feedforward_low = tie(
        hidden_first, feed_far, hidden_low, feedforward_low
    )
    hidden_second = other(hidden_low[own_rows:])
    feed_came = send_core(feed_far, size)
    feed_came, hidden_low, feedforward_low = tie(feed_came, hidden_low, feedforward_low)
    cuts = [0, 3 * hidden // 2, 3 * hidden]
    lines, owns = [], []
    for i, j in zip(cuts, cuts[1:]):
        line, own = add_core(feed_came[:, i:j], feed_line[:, i:j], feed_own[:, i:j])
        lines.append(line)
        owns.append(own)
    came = send_line(lines[0], size)
    hidden_first, hidden_second, lines, owns, feedforward_low = tie(
        hidden_first, hidden_second, lines, owns, feedforward_low
    )

    grad_hidden = wide(hidden_low) + wide(jnp.concatenate([hidden_first, hidden_second], 0))
    middle_rms = inverse_rms(middle)
    middle_normal = middle * middle_rms
    middle_gain_part = jnp.sum(grad_hidden * middle_normal, 0)
    middle_scaled = grad_hidden * middle_gain
    grad_middle = wide(cotangent) + middle_rms * (
        middle_scaled - middle_normal * jnp.mean(middle_scaled * middle_normal, -1, keepdims=True)
    )
    mix_low = narrow(grad_middle)
    mix = wide(mix_low)
    square_sum = jnp.sum(mix * wide(mamba_own), -1)
    square_sum = square_sum + other(square_sum)
    grad_mamba = narrow(factor * mix)
    second_pieces = gathering.pieces(1)
    mamba_at = query_width + keyvalue_width
    grad_query, grad_keyvalue = attention_backward(
        rank_array,
        starts,
        mix_low,
        turned,
        keys,
        values,
        logsum,
        info,
        label_rows,
        cosine,
        sinusoid,
        second_pieces,
        mamba_at + width,
    )
    came_first, square_sum, grad_query, grad_mamba, lines, owns = tie(
        came, square_sum, grad_query, grad_mamba, lines, owns
    )
    came = send_line(lines[1], size)
    first_parts = add_line(came_first, owns[0], size)
    ring_first = send_ring(first_parts[1], size)
    square_column = wide(
        narrow(square_sum * -0.5 * norm_factor * norm_factor * norm_factor / ssm_width)
    )[:, None]
    second_width = width + attended_width + query_width + keyvalue_width
    grad_gated_low, grad_gate, second_far, second_line, second_own = gate_backward(
        starts,
        projected,
        scanned,
        [
            grad_mamba,
            local_gain[None],
            square_column,
            normed_turned,
            order,
            mix_low,
            factor.reshape(1, rows),
            gated_low,
            attended,
            grad_query,
            grad_keyvalue,
        ],
        second_pieces,
        mamba_at,
        second_width + width,
    )
    came, second_far, ring_first, feedforward_low = tie(
        came, second_far, ring_first, feedforward_low
    )

    second_came = send_core(second_far, size)
    first_total = add_ring(first_parts, ring_first, 1)
    ring_first = send_ring(first_total, size)
    feed_parts = add_line(came, owns[1], size)
    ring_feed = send_ring(feed_parts[1], size)
    second_came, ring_first, ring_feed, grad_gated_low = tie(
        second_came, ring_first, ring_feed, grad_gated_low
    )
    second_line, second_own = add_core(second_came, second_line, second_own)
    second_came = send_line(second_line, size)
    first_total = add_ring(first_parts, ring_first, 2)
    ring_first = send_ring(first_total, size)
    feed_total = add_ring(feed_parts, ring_feed, 1)
    ring_feed = send_ring(feed_total, size)
    feedforward_far = other(far_half(feedforward_low))
    lanes = jnp.arange(128, dtype=jnp.int32)[None, :]
    info = jnp.where(lanes == 5, square_column, info)
    grad_value, grad_state, grad_steps, channel_grad, state_grad, head_grad = mixer_backward(
        projected,
        mixer_widths,
        info,
        label_rows,
        channel,
        state_channel,
        head_rows,
        scanned,
        grad_gated_low,
        dt,
        cum,
    )
    grad_value, ring_feed, ring_first, feedforward_far = tie(
        grad_value, ring_feed, ring_first, feedforward_far
    )

    last_far, last_line, last_own = weight_grads(
        last_kernel,
        [normed_turned, grad_value, grad_state, grad_steps],
        model,
        width + state_width + 128,
        "last_grads",
    )
    last_far, ring_feed, ring_first, second_own = tie(last_far, ring_feed, ring_first, second_own)
    last_came = send_core(last_far, size)
    feed_total = add_ring(feed_parts, ring_feed, 2)
    ring_feed = send_ring(feed_total, size)
    last_came, grad_value, second_came = tie(last_came, grad_value, second_came)
    last_line, last_own = add_core(last_came, last_line, last_own)
    last_came = send_line(last_line, size)
    second_parts = add_line(second_came, second_own, size)
    ring_second = send_ring(second_parts[1], size)
    normed_low = back_project(
        starts,
        gathering.pieces(0),
        second_pieces,
        [grad_gate, grad_value, grad_state, grad_steps, grad_query, grad_keyvalue],
    )
    normed_low, last_came, ring_second, ring_feed, ring_first, feedforward_far = tie(
        normed_low, last_came, ring_second, ring_feed, ring_first, feedforward_far
    )
    last_parts = add_line(last_came, last_own, size)
    ring_last = send_ring(last_parts[1], size)
    second_total = add_ring(second_parts, ring_second, 1)
    ring_second = send_ring(second_total, size)
    normed_far = other(far_half(normed_low))
    feed_total = add_ring(feed_parts, ring_feed, 3)
    first_total = add_ring(first_parts, ring_first, 3)
    spread = lambda part, total, start: lax.dynamic_update_slice_in_dim(
        jnp.zeros(part.shape[:-1] + (total,), jnp.float32), part, start, part.ndim - 1
    )
    block_output = (
        own_half(middle)
        + wide(own_half(feedforward_low))
        + wide(feedforward_far)
    )
    residual = wide(group_input)
    first_rms = inverse_rms(residual)
    first_normal = residual * first_rms
    input_gain_part = jnp.sum(wide(normed_low) * first_normal, 0)
    channel_parts = jnp.concatenate(
        [spread(channel_grad[:5], ssm_width, rank * width), state_grad[:5]], 1
    )
    skip_grad = jnp.sum(channel_grad[5].reshape(heads, repeat), 1)
    head_parts = spread(
        jnp.concatenate([head_grad[:2, :heads], skip_grad[None]], 0),
        timestep_bias.shape[0],
        rank * heads,
    )
    gain_parts = spread(channel_grad[6], ssm_width, rank * width)
    leader = (rank == 0).astype(jnp.float32)
    parts = [input_gain_part, middle_gain_part * leader, gain_parts, channel_parts, head_parts]
    flat = jnp.concatenate([part.reshape(-1) for part in parts])
    flat = jnp.pad(flat, (0, -flat.shape[0] % 1024)).reshape(-1, 128)

    flat_far = lax.ppermute(flat, "fsdp", swaps(size, 1))
    ring_last, flat_far, ring_second = tie(ring_last, flat_far, ring_second)
    last_total = add_ring(last_parts, ring_last, 1)
    ring_last = send_ring(last_total, size)
    second_total = add_ring(second_parts, ring_second, 2)
    ring_second = send_ring(second_total, size)
    flat = flat + flat_far
    flat_far = lax.ppermute(flat, "fsdp", swaps(size, 2))
    ring_last, flat_far, ring_second = tie(ring_last, flat_far, ring_second)
    last_total = add_ring(last_parts, ring_last, 2)
    ring_last = send_ring(last_total, size)
    second_total = add_ring(second_parts, ring_second, 3)
    flat = flat + flat_far
    lined = [
        lax.ppermute(flat, "fsdp", [(i, (i + 4 * k) % size) for i in range(size)])
        for k in range(1, depth)
    ]
    ring_last, normed_far, *lined = tie(ring_last, normed_far, *lined)
    last_total = add_ring(last_parts, ring_last, 3)
    placed = jnp.stack([flat] + lined)
    flat = sum(placed[(ring_at - k + depth) % depth] for k in range(depth))
    flat = (flat + other(flat)).reshape(-1)
    shared_at = width + attended_width + query_width
    shared = jnp.concatenate(
        [last_total[:, width : width + state_width], second_total[:, shared_at : shared_at + keyvalue_width]],
        1,
    )
    shared = shared + other(shared)
    normed_grad = wide(own_half(normed_low)) + wide(normed_far)
    own_normal = own_half(first_normal)
    first_scaled = normed_grad * input_gain
    input_grad = own_half(grad_middle) + own_half(first_rms) * (
        first_scaled - own_normal * jnp.mean(first_scaled * own_normal, -1, keepdims=True)
    )

    summed = []
    for part in parts:
        summed.append(flat[: part.size].reshape(part.shape))
        flat = flat[part.size :]
    inner_grad = jnp.stack(
        [second_total[:, second_width:], last_total[:, :width]], 1
    )
    return (
        block_output,
        input_grad,
        summed[0],
        inner_grad,
        last_total[:, width + state_width : width + state_width + heads],
        shared[:, :state_width],
        second_total[:, width + attended_width : shared_at],
        shared[:, state_width:],
        summed[3][:4],
        summed[3][4],
        summed[4][0],
        summed[4][1],
        summed[4][2],
        summed[2],
        second_total[:, :width].T,
        second_total[:, width : width + attended_width].T,
        summed[1],
        jnp.concatenate([first_total[:, hidden:], feed_total], 1).reshape(shard, 2, hidden),
        first_total[:, :hidden].T,
    )


def solution(mesh):
    fsdp, tp = mesh.shape["fsdp"], mesh.shape["tp"]

    def body(*operands):
        rows = operands[1].shape[0]
        if tp == 2 and fsdp == 16 and rows == 2 * BLOCK:
            return packed_body(fsdp, *operands)
        return general_body(*operands)

    return jax.shard_map(
        body,
        mesh=mesh,
        in_specs=(
            P(("fsdp", "tp"), None),
            P("fsdp"),
            P(("fsdp", "tp"), None),
            P(),
            P("fsdp", None, "tp"),
            P("fsdp", "tp"),
            P("fsdp", None),
            P("fsdp", "tp"),
            P("fsdp", None),
            P(),
            P(),
            P(),
            P(),
            P(),
            P(),
            P("tp", "fsdp"),
            P("tp", "fsdp"),
            P(),
            P("fsdp", None, "tp"),
            P("tp", "fsdp"),
        ),
        out_specs=(
            P(("fsdp", "tp"), None),
            P(("fsdp", "tp"), None),
            P(),
            P("fsdp", None, "tp"),
            P("fsdp", "tp"),
            P("fsdp", None),
            P("fsdp", "tp"),
            P("fsdp", None),
            P(),
            P(),
            P(),
            P(),
            P(),
            P(),
            P("tp", "fsdp"),
            P("tp", "fsdp"),
            P(),
            P("fsdp", None, "tp"),
            P("tp", "fsdp"),
        ),
        check_vma=False,
    )
```

```python
import math

import jax
import jax.numpy as jnp
from jax import lax
from jax.experimental import pallas as pl
from jax.experimental.pallas import tpu as pltpu
from jax.sharding import PartitionSpec as P

QUERY_HEADS = 8
KEYVALUE_HEADS = 2
HEAD_SIZE = 64
SCAN_BLOCK = 256
QUERY_BLOCK = 512


EPSILON = 1e-05
MASKED_SCORE = -1e30
ROPE_BASE = 100000000000.0
PRECISE = lax.Precision.HIGHEST


def inverse_rms(values):
    return lax.rsqrt(jnp.mean(values * values, -1, keepdims=True) + EPSILON)


def contract_rows(left, right):
    return lax.dot_general(
        left, right, (((0,), (0,)), ((), ())), preferred_element_type=jnp.float32
    )


def contract_cols(left, right):
    return lax.dot_general(
        left, right, (((1,), (1,)), ((), ())), preferred_element_type=jnp.float32
    )


def causal_conv(signal, kernel, offset, segment):
    length_tokens = signal.shape[0]
    result = offset[None, :] + kernel[0][None, :] * signal
    for distance in range(1, kernel.shape[0]):
        shifted = jnp.concatenate(
            [
                jnp.zeros((distance, signal.shape[1]), signal.dtype),
                signal[: length_tokens - distance],
            ],
            0,
        )
        earlier = jnp.concatenate(
            [jnp.full((distance,), -1, jnp.int32), segment[: length_tokens - distance]], 0
        )
        retained = (earlier == segment).astype(signal.dtype)
        result = result + kernel[distance][None, :] * shifted * retained[:, None]
    return result


def state_scan(values, timesteps, decays, key_row_block, query_rows, segment, block):
    total, head_count, channels = values.shape
    count = total // block
    states = key_row_block.shape[1]
    lower = jnp.arange(block)[:, None] >= jnp.arange(block)[None, :]

    def advance(carry, pieces):
        memory, previous = carry
        value_block, step_block, key_block, query_block, labels = pieces
        rates = step_block * decays[None, :]
        cumulative = jnp.cumsum(rates, 0)
        linked = jnp.logical_and(labels[:, None] == labels[None, :], lower)
        gaps = cumulative[:, None, :] - cumulative[None, :, :]
        weights = jnp.exp(jnp.where(linked[:, :, None], gaps, 0.0)) * linked[:, :, None].astype(
            jnp.float32
        )
        intersections = jnp.dot(query_block, key_block.T, precision=PRECISE)
        scaled = value_block * step_block[:, :, None]
        within = jnp.einsum(
            "tsh,shp->thp", intersections[:, :, None] * weights, scaled, precision=PRECISE
        )
        carried = jnp.exp(cumulative) * (labels == previous).astype(jnp.float32)[:, None]
        across = (
            jnp.einsum("tn,hpn->thp", query_block, memory, precision=PRECISE) * carried[:, :, None]
        )
        final = cumulative[block - 1]
        ending = labels[block - 1]
        toward = (
            jnp.exp(final[None, :] - cumulative) * (labels == ending).astype(jnp.float32)[:, None]
        )
        fresh = jnp.einsum("sh,shp,sn->hpn", toward, scaled, key_block, precision=PRECISE)
        kept = jnp.exp(final) * (ending == previous).astype(jnp.float32)
        memory = memory * kept[:, None, None] + fresh
        return ((memory, ending), within + across)

    start = (jnp.zeros((head_count, channels, states), jnp.float32), jnp.array(-1, jnp.int32))
    pieces = (
        values.reshape(count, block, head_count, channels),
        timesteps.reshape(count, block, head_count),
        key_row_block.reshape(count, block, states),
        query_rows.reshape(count, block, states),
        segment.reshape(count, block),
    )
    folded, outputs = lax.scan(jax.checkpoint(advance), start, pieces)
    return outputs.reshape(total, head_count, channels)


def mixer_core(
    values, raw_steps, step_bias, decay_log, skip_scale, key_row_block, query_rows, segment, block
):
    timesteps = jax.nn.softplus(raw_steps + step_bias[None, :])
    decays = -jnp.exp(decay_log)
    head_count = timesteps.shape[1]
    shaped = values.reshape(values.shape[0], head_count, -1)
    output = state_scan(shaped, timesteps, decays, key_row_block, query_rows, segment, block)
    return (output + skip_scale[None, :, None] * shaped).reshape(values.shape)


def rotary_apply(vectors, direction):
    length_tokens, head_count, columns = vectors.shape
    halfway = columns // 2
    frequency = jnp.exp(
        jnp.arange(halfway, dtype=jnp.float32) * (-2.0 * math.log(ROPE_BASE) / columns)
    )
    angles = jnp.arange(length_tokens, dtype=jnp.float32)[:, None] * frequency[None, :] * direction
    cosine = jnp.cos(angles)[:, None, :]
    sinusoid = jnp.sin(angles)[:, None, :]
    former = vectors[..., :halfway]
    latter = vectors[..., halfway:]
    return jnp.concatenate(
        [former * cosine - latter * sinusoid, latter * cosine + former * sinusoid], -1
    )


def attention_mask(segment, start, rowcount):
    positions = start + jnp.arange(rowcount, dtype=jnp.int32)
    columns = jnp.arange(segment.shape[0], dtype=jnp.int32)
    labels = lax.dynamic_slice_in_dim(segment, start, rowcount)
    return jnp.logical_and(
        columns[None, :] <= positions[:, None], segment[None, :] == labels[:, None]
    )


def general_body(
    block_input,
    segment_ids,
    output_cotangent,
    input_gain,
    inner_weight,
    timestep_weight,
    state_weight,
    query_weight,
    keyvalue_matrix,
    conv_kernel,
    conv_offset,
    timestep_bias,
    decay_log,
    skip_scale,
    gated_gain,
    mamba_down,
    attention_down,
    middle_gain,
    gateup_weight,
    down_weight,
):
    tensor_parallel_rank = lax.axis_index("tp")
    residual = block_input.astype(jnp.float32)
    first_rms = inverse_rms(residual)
    normed = lax.all_gather(
        (residual * first_rms * input_gain).astype(jnp.bfloat16), "tp", axis=0, tiled=True
    )
    (
        inner_full,
        timestep_full,
        state_full,
        query_full,
        keyvalue_full,
        mamba_full,
        attention_full,
        gateup_full,
        down_full,
    ) = (
        lax.all_gather(inner_weight, "fsdp", axis=0, tiled=True),
        lax.all_gather(timestep_weight, "fsdp", axis=0, tiled=True),
        lax.all_gather(state_weight, "fsdp", axis=0, tiled=True),
        lax.all_gather(query_weight, "fsdp", axis=0, tiled=True),
        lax.all_gather(keyvalue_matrix, "fsdp", axis=0, tiled=True),
        lax.all_gather(mamba_down, "fsdp", axis=1, tiled=True),
        lax.all_gather(attention_down, "fsdp", axis=1, tiled=True),
        lax.all_gather(gateup_weight, "fsdp", axis=0, tiled=True),
        lax.all_gather(down_weight, "fsdp", axis=1, tiled=True),
    )
    length_tokens = normed.shape[0]
    local_heads = timestep_full.shape[1]
    local_width = inner_full.shape[2]
    ssm_width = gated_gain.shape[0]
    state_dim = state_full.shape[1] // 2
    query_head_count = query_full.shape[1] // HEAD_SIZE
    head_start = tensor_parallel_rank * local_heads
    width_start = tensor_parallel_rank * local_width
    inner = jnp.einsum("gd,dkc->gkc", normed, inner_full, preferred_element_type=jnp.float32)
    raw_steps = jnp.dot(normed, timestep_full, preferred_element_type=jnp.float32)
    state_proj = jnp.dot(normed, state_full, preferred_element_type=jnp.float32)
    query_proj = jnp.dot(normed, query_full, preferred_element_type=jnp.float32)
    keyvalue_projected = jnp.dot(normed, keyvalue_full, preferred_element_type=jnp.float32)
    gate_half = inner[:, 0]
    local_kernel = jnp.concatenate(
        [
            lax.dynamic_slice_in_dim(conv_kernel, width_start, local_width, 1),
            conv_kernel[:, ssm_width:],
        ],
        1,
    )
    local_offset = jnp.concatenate(
        [
            lax.dynamic_slice_in_dim(conv_offset, width_start, local_width, 0),
            conv_offset[ssm_width:],
        ],
        0,
    )
    local_bias = lax.dynamic_slice_in_dim(timestep_bias, head_start, local_heads, 0)
    local_decay = lax.dynamic_slice_in_dim(decay_log, head_start, local_heads, 0)
    local_skip = lax.dynamic_slice_in_dim(skip_scale, head_start, local_heads, 0)
    local_gain = lax.dynamic_slice_in_dim(gated_gain, width_start, local_width, 0)

    def convolve(signal, kernel, offset):
        return jax.nn.silu(causal_conv(signal, kernel, offset, segment_ids))

    convolved, conv_pullback = jax.vjp(
        convolve, jnp.concatenate([inner[:, 1], state_proj], 1), local_kernel, local_offset
    )
    conv_values = convolved[:, :local_width].astype(jnp.bfloat16)
    conv_states = convolved[:, local_width:].astype(jnp.bfloat16).astype(jnp.float32)

    def scan_heads(values, steps_in, bias_in, decay_in, skip_in, key_rows_in, query_rows_in):
        return mixer_core(
            values,
            steps_in,
            bias_in,
            decay_in,
            skip_in,
            key_rows_in,
            query_rows_in,
            segment_ids,
            SCAN_BLOCK,
        )

    scanned, scan_pullback = jax.vjp(
        scan_heads,
        conv_values.astype(jnp.float32),
        raw_steps,
        local_bias,
        local_decay,
        local_skip,
        conv_states[:, :state_dim],
        conv_states[:, state_dim:],
    )
    silu_gate = jax.nn.silu(gate_half)
    gated = scanned * silu_gate
    gated_low = (gated * local_gain).astype(jnp.bfloat16)
    mamba_partial = jnp.dot(gated_low, mamba_full, preferred_element_type=jnp.float32)
    queries = rotary_apply(
        query_proj.reshape(length_tokens, query_head_count, HEAD_SIZE), 1.0
    ).astype(jnp.bfloat16)
    key_gathered = rotary_apply(
        keyvalue_projected[:, : KEYVALUE_HEADS * HEAD_SIZE].reshape(
            length_tokens, KEYVALUE_HEADS, HEAD_SIZE
        ),
        1.0,
    ).astype(jnp.bfloat16)
    value_gathered = (
        keyvalue_projected[:, KEYVALUE_HEADS * HEAD_SIZE :]
        .reshape(length_tokens, KEYVALUE_HEADS, HEAD_SIZE)
        .astype(jnp.bfloat16)
    )
    owner_ranks = (
        tensor_parallel_rank * query_head_count + jnp.arange(query_head_count, dtype=jnp.int32)
    ) // (QUERY_HEADS // KEYVALUE_HEADS)
    choice_picker = (
        owner_ranks[:, None] == jnp.arange(KEYVALUE_HEADS, dtype=jnp.int32)[None, :]
    ).astype(jnp.bfloat16)
    key_row_block = jnp.einsum(
        "jh,ghd->gjd", choice_picker, key_gathered, preferred_element_type=jnp.float32
    ).astype(jnp.bfloat16)
    value_row_block = jnp.einsum(
        "jh,ghd->gjd", choice_picker, value_gathered, preferred_element_type=jnp.float32
    ).astype(jnp.bfloat16)
    scaling = 1.0 / math.sqrt(HEAD_SIZE)
    block_count = length_tokens // QUERY_BLOCK
    query_blocks = queries.reshape(block_count, QUERY_BLOCK, query_head_count, HEAD_SIZE)
    block_starts = jnp.arange(block_count, dtype=jnp.int32) * QUERY_BLOCK

    def block_scores(query_block, start):
        scores = (
            jnp.einsum(
                "qjd,kjd->jqk", query_block, key_row_block, preferred_element_type=jnp.float32
            )
            * scaling
        )
        allowed = attention_mask(segment_ids, start, QUERY_BLOCK)
        return jnp.where(allowed[None], scores, MASKED_SCORE)

    def forward_block(pieces):
        query_block, start = pieces
        masked = block_scores(query_block, start)
        highest = jnp.max(masked, -1, keepdims=True)
        weights = jnp.exp(masked - highest)
        totals = jnp.sum(weights, -1, keepdims=True)
        probs_low = (weights / totals).astype(jnp.bfloat16)
        result = jnp.einsum(
            "jqk,kjd->qjd", probs_low, value_row_block, preferred_element_type=jnp.float32
        )
        return (result, (highest + jnp.log(totals))[..., 0])

    attended, logsums = lax.map(forward_block, (query_blocks, block_starts))
    attended_low = attended.reshape(length_tokens, query_head_count * HEAD_SIZE).astype(
        jnp.bfloat16
    )
    attention_partial = jnp.dot(attended_low, attention_full, preferred_element_type=jnp.float32)
    square_local = jnp.sum(gated * gated, -1)
    mamba_rows, attention_rows, square_rows = (
        lax.psum_scatter(mamba_partial, "tp", scatter_dimension=0, tiled=True),
        lax.psum_scatter(attention_partial, "tp", scatter_dimension=0, tiled=True),
        lax.psum_scatter(square_local, "tp", scatter_dimension=0, tiled=True),
    )
    norm_factor = lax.rsqrt(square_rows / ssm_width + EPSILON)
    factor_low = norm_factor.astype(jnp.bfloat16)
    factor_own = lax.optimization_barrier(factor_low).astype(jnp.float32)
    middle = residual + (factor_own[:, None] * mamba_rows + attention_rows)
    middle_rms = inverse_rms(middle)
    hidden_in = lax.all_gather(
        (middle * middle_rms * middle_gain).astype(jnp.bfloat16), "tp", axis=0, tiled=True
    )
    gateup = jnp.einsum("gd,dkf->gkf", hidden_in, gateup_full, preferred_element_type=jnp.float32)
    gate_part = gateup[:, 0]
    up_part = gateup[:, 1]
    activated = (jax.nn.silu(gate_part) * up_part).astype(jnp.bfloat16)
    feedforward = lax.psum_scatter(
        jnp.dot(activated, down_full, preferred_element_type=jnp.float32).astype(jnp.bfloat16),
        "tp",
        scatter_dimension=0,
        tiled=True,
    ).astype(jnp.float32)
    block_output = middle + feedforward
    cotangent_all = lax.all_gather(output_cotangent, "tp", axis=0, tiled=True)
    grad_activated = contract_cols(cotangent_all, down_full)
    down_wgrad = contract_rows(activated, cotangent_all)
    gate_sigmoid = jax.nn.sigmoid(gate_part)
    grad_gate_part = (
        grad_activated * up_part * gate_sigmoid * (1.0 + gate_part * (1.0 - gate_sigmoid))
    )
    grad_up_part = grad_activated * jax.nn.silu(gate_part)
    grad_gateup = jnp.stack([grad_gate_part, grad_up_part], 1).astype(jnp.bfloat16)
    gateup_wgrad = jnp.einsum(
        "gd,gkf->dkf", hidden_in, grad_gateup, preferred_element_type=jnp.float32
    )
    grad_hidden = lax.psum_scatter(
        jnp.einsum("gkf,dkf->gd", grad_gateup, gateup_full, preferred_element_type=jnp.float32),
        "tp",
        scatter_dimension=0,
        tiled=True,
    )
    middle_normal = middle * middle_rms
    middle_gain_part = jnp.sum(grad_hidden * middle_normal, 0)
    middle_scaled = grad_hidden * middle_gain
    grad_middle = output_cotangent.astype(jnp.float32) + middle_rms * (
        middle_scaled - middle_normal * jnp.mean(middle_scaled * middle_normal, -1, keepdims=True)
    )
    mix_low = grad_middle.astype(jnp.bfloat16)
    mix_own = mix_low.astype(jnp.float32)
    grad_factor = jnp.sum(mix_own * mamba_rows, -1)
    grad_square = (grad_factor * -0.5 * norm_factor * norm_factor * norm_factor / ssm_width).astype(
        jnp.bfloat16
    )
    mix_all, factor_rows, square_rows_grad = (
        lax.all_gather(mix_low, "tp", axis=0, tiled=True),
        lax.all_gather(factor_low, "tp", axis=0, tiled=True),
        lax.all_gather(grad_square, "tp", axis=0, tiled=True),
    )
    grad_mamba = (factor_rows.astype(jnp.float32)[:, None] * mix_all.astype(jnp.float32)).astype(
        jnp.bfloat16
    )
    mamba_wgrad = contract_rows(gated_low, grad_mamba)
    grad_gated_low = contract_cols(grad_mamba, mamba_full)
    gain_grad = jnp.sum(grad_gated_low * gated, 0)
    grad_gated = (
        grad_gated_low * local_gain + 2.0 * gated * square_rows_grad.astype(jnp.float32)[:, None]
    )
    zsigmoid = jax.nn.sigmoid(gate_half)
    grad_scanned = grad_gated * silu_gate
    grad_gate = grad_gated * scanned * zsigmoid * (1.0 + gate_half * (1.0 - zsigmoid))
    grad_values, grad_steps, grad_bias, grad_decay, grad_skip, grad_keys_in, grad_queries_in = (
        scan_pullback(grad_scanned)
    )
    grad_signal, kernel_local, offset_local = conv_pullback(
        jnp.concatenate([grad_values, grad_keys_in, grad_queries_in], 1)
    )
    attention_wgrad = contract_rows(attended_low, mix_all)
    grad_attended = (
        contract_cols(mix_all, attention_full)
        .astype(jnp.bfloat16)
        .reshape(block_count, QUERY_BLOCK, query_head_count, HEAD_SIZE)
    )

    def backward_block(carry, pieces):
        key_grad, value_grad = carry
        query_block, grad_block, logsum_block, start = pieces
        masked = block_scores(query_block, start)
        probs = jnp.exp(masked - logsum_block[..., None])
        grad_probs = jnp.einsum(
            "qjd,kjd->jqk", grad_block, value_row_block, preferred_element_type=jnp.float32
        )
        inner_sum = jnp.sum(grad_probs * probs, -1, keepdims=True)
        grad_scores = (probs * (grad_probs - inner_sum)).astype(jnp.bfloat16)
        query_grad = (
            jnp.einsum(
                "jqk,kjd->qjd", grad_scores, key_row_block, preferred_element_type=jnp.float32
            )
            * scaling
        )
        key_grad = (
            key_grad
            + jnp.einsum(
                "jqk,qjd->kjd", grad_scores, query_block, preferred_element_type=jnp.float32
            )
            * scaling
        )
        value_grad = value_grad + jnp.einsum(
            "jqk,qjd->kjd",
            probs.astype(jnp.bfloat16),
            grad_block,
            preferred_element_type=jnp.float32,
        )
        return ((key_grad, value_grad), query_grad)

    empty_rows = jnp.zeros((length_tokens, query_head_count, HEAD_SIZE), jnp.float32)
    (key_grad, value_grad), query_grads = lax.scan(
        backward_block,
        (empty_rows, empty_rows),
        (query_blocks, grad_attended, logsums, block_starts),
    )
    query_back = rotary_apply(
        query_grads.reshape(length_tokens, query_head_count, HEAD_SIZE), -1.0
    ).reshape(length_tokens, query_head_count * HEAD_SIZE)
    selector_float = choice_picker.astype(jnp.float32)
    key_returned = rotary_apply(
        jnp.einsum("jh,gjd->ghd", selector_float, key_grad, precision=PRECISE), -1.0
    )
    value_returned = jnp.einsum("jh,gjd->ghd", selector_float, value_grad, precision=PRECISE)
    keyvalue_partial = jnp.concatenate(
        [
            key_returned.reshape(length_tokens, KEYVALUE_HEADS * HEAD_SIZE),
            value_returned.reshape(length_tokens, KEYVALUE_HEADS * HEAD_SIZE),
        ],
        1,
    )
    state_total, keyvalue_total = (
        lax.psum(grad_signal[:, local_width:].astype(jnp.bfloat16), "tp").astype(jnp.float32),
        lax.psum(keyvalue_partial.astype(jnp.bfloat16), "tp").astype(jnp.float32),
    )
    inner_low = jnp.stack([grad_gate, grad_signal[:, :local_width]], 1).astype(jnp.bfloat16)
    steps_low = grad_steps.astype(jnp.bfloat16)
    query_low = query_back.astype(jnp.bfloat16)
    state_low = state_total.astype(jnp.bfloat16)
    keyvalue_low = keyvalue_total.astype(jnp.bfloat16)
    inner_wgrad = jnp.einsum("gd,gkc->dkc", normed, inner_low, preferred_element_type=jnp.float32)
    timestep_wgrad = contract_rows(normed, steps_low)
    state_wgrad = contract_rows(normed, state_low)
    query_wgrad = contract_rows(normed, query_low)
    keyvalue_wgrad = contract_rows(normed, keyvalue_low)
    normed_partial = (
        jnp.einsum("gkc,dkc->gd", inner_low, inner_full, preferred_element_type=jnp.float32)
        + contract_cols(steps_low, timestep_full)
        + contract_cols(query_low, query_full)
    )
    leader = (tensor_parallel_rank == 0).astype(jnp.float32)
    normed_partial = normed_partial + leader * (
        contract_cols(state_low, state_full) + contract_cols(keyvalue_low, keyvalue_full)
    )
    normed_grad = lax.psum_scatter(
        normed_partial.astype(jnp.bfloat16), "tp", scatter_dimension=0, tiled=True
    ).astype(jnp.float32)
    first_normal = residual * first_rms
    input_gain_part = jnp.sum(normed_grad * first_normal, 0)
    first_scaled = normed_grad * input_gain
    input_grad = grad_middle + first_rms * (
        first_scaled - first_normal * jnp.mean(first_scaled * first_normal, -1, keepdims=True)
    )
    gated_part = lax.dynamic_update_slice_in_dim(
        jnp.zeros((ssm_width,), jnp.float32), gain_grad, width_start, 0
    )
    kernel_part = jnp.concatenate(
        [
            lax.dynamic_update_slice_in_dim(
                jnp.zeros((conv_kernel.shape[0], ssm_width), jnp.float32),
                kernel_local[:, :local_width],
                width_start,
                1,
            ),
            kernel_local[:, local_width:],
        ],
        1,
    )
    offset_part = jnp.concatenate(
        [
            lax.dynamic_update_slice_in_dim(
                jnp.zeros((ssm_width,), jnp.float32), offset_local[:local_width], width_start, 0
            ),
            offset_local[local_width:],
        ],
        0,
    )
    head_zeros = jnp.zeros((timestep_bias.shape[0],), jnp.float32)
    bias_part = lax.dynamic_update_slice_in_dim(head_zeros, grad_bias, head_start, 0)
    decay_part = lax.dynamic_update_slice_in_dim(head_zeros, grad_decay, head_start, 0)
    skip_part = lax.dynamic_update_slice_in_dim(head_zeros, grad_skip, head_start, 0)
    summed = lax.psum(
        (
            input_gain_part,
            middle_gain_part,
            kernel_part,
            offset_part,
            bias_part,
            decay_part,
            skip_part,
            gated_part,
        ),
        ("fsdp", "tp"),
    )
    (
        inner_out,
        timestep_out,
        state_out,
        query_out,
        keyvalue_out,
        mamba_out,
        attention_out,
        gateup_out,
        down_out,
    ) = (
        lax.psum_scatter(
            inner_wgrad.astype(jnp.bfloat16), "fsdp", scatter_dimension=0, tiled=True
        ).astype(jnp.float32),
        lax.psum_scatter(
            timestep_wgrad.astype(jnp.bfloat16), "fsdp", scatter_dimension=0, tiled=True
        ).astype(jnp.float32),
        lax.psum_scatter(
            state_wgrad.astype(jnp.bfloat16), "fsdp", scatter_dimension=0, tiled=True
        ).astype(jnp.float32),
        lax.psum_scatter(
            query_wgrad.astype(jnp.bfloat16), "fsdp", scatter_dimension=0, tiled=True
        ).astype(jnp.float32),
        lax.psum_scatter(
            keyvalue_wgrad.astype(jnp.bfloat16), "fsdp", scatter_dimension=0, tiled=True
        ).astype(jnp.float32),
        lax.psum_scatter(
            mamba_wgrad.astype(jnp.bfloat16), "fsdp", scatter_dimension=1, tiled=True
        ).astype(jnp.float32),
        lax.psum_scatter(
            attention_wgrad.astype(jnp.bfloat16), "fsdp", scatter_dimension=1, tiled=True
        ).astype(jnp.float32),
        lax.psum_scatter(
            gateup_wgrad.astype(jnp.bfloat16), "fsdp", scatter_dimension=0, tiled=True
        ).astype(jnp.float32),
        lax.psum_scatter(
            down_wgrad.astype(jnp.bfloat16), "fsdp", scatter_dimension=1, tiled=True
        ).astype(jnp.float32),
    )
    return (
        block_output,
        input_grad,
        summed[0],
        inner_out,
        timestep_out,
        state_out,
        query_out,
        keyvalue_out,
        summed[2],
        summed[3],
        summed[4],
        summed[5],
        summed[6],
        summed[7],
        mamba_out,
        attention_out,
        summed[1],
        gateup_out,
        down_out,
    )


BLOCK = 256
LOG2E = 1.4426950408889634
HIDDEN_BIAS = -1e30


def narrow(values):
    return values.astype(jnp.bfloat16)


def wide(values):
    return values.astype(jnp.float32)


def mm(left, right):
    return jnp.dot(left, right, preferred_element_type=jnp.float32)


def sigmoid(values):
    return 1.0 / (1.0 + jnp.exp(-values))


def dot_wide(ones, values):
    first = narrow(values)
    rest = values - wide(first)
    second = narrow(rest)
    third = narrow(rest - wide(second))
    return mm(ones, first) + mm(ones, second) + mm(ones, third)


def triangle(rows, upper):
    down = lax.broadcasted_iota(jnp.int32, (rows, rows), 0)
    across = lax.broadcasted_iota(jnp.int32, (rows, rows), 1)
    keep = (across >= down) if upper else (down >= across)
    return jnp.where(keep, 1.0, 0.0).astype(jnp.bfloat16)


def pair_bias(label_column, label_row):
    rows = label_column.shape[0]
    down = lax.broadcasted_iota(jnp.int32, (rows, rows), 0)
    across = lax.broadcasted_iota(jnp.int32, (rows, rows), 1)
    keep = jnp.logical_and(label_column == label_row, down >= across)
    return jnp.where(keep, 0.0, HIDDEN_BIAS)


def conv_taps(signal, info):
    taps = [signal]
    for distance in range(1, 4):
        taps.append(pltpu.roll(signal, distance, 0) * info[:, distance : distance + 1])
    return taps


def conv_pre(taps, channel):
    result = channel[4:5, :]
    for distance in range(4):
        result = result + channel[distance : distance + 1, :] * taps[distance]
    return result


def conv_back(grad_pre, channel, info):
    rows = grad_pre.shape[0]
    result = channel[0:1, :] * grad_pre
    for distance in range(1, 4):
        masked = grad_pre * info[:, distance : distance + 1]
        result = result + channel[distance : distance + 1, :] * pltpu.roll(masked, rows - distance, 0)
    return result


def column_of(values, lane):
    lanes = lax.broadcasted_iota(jnp.int32, values.shape, 1)
    return jnp.sum(jnp.where(lanes == lane, values, 0.0), 1, keepdims=True)


def half_lanes(values, which):
    lanes = lax.broadcasted_iota(jnp.int32, values.shape, 1)
    keep = (lanes < HEAD_SIZE) if which == 0 else (lanes >= HEAD_SIZE)
    return jnp.where(keep, values, jnp.zeros_like(values))


def spans(rows):
    return [slice(at, at + BLOCK) for at in range(0, rows, BLOCK)]


def mixer_forward_kernel(
    gate_ref,
    value_ref,
    state_ref,
    steps_ref,
    info_ref,
    label_ref,
    channel_ref,
    state_channel_ref,
    head_ref,
    low_ref,
    scanned_ref,
    square_ref,
    dt_ref,
    cum_ref,
    crossed,
    bias,
    source_rows,
):
    pair = pl.program_id(0)
    info = info_ref[...]
    rows = info.shape[0]

    @pl.when(pair == 0)
    def _():
        taps = conv_taps(state_ref[...], info)
        pre = conv_pre(taps, state_channel_ref[...])
        states = narrow(pre * sigmoid(pre))
        half = states.shape[1] // 2
        crossed[...] = contract_cols(states[:, half:], states[:, :half])
        bias[...] = pair_bias(info[:, 4:5], label_ref[0:1, :])
        raw = steps_ref[...] + head_ref[0:1, :]
        dt = jnp.maximum(raw, 0.0) + jnp.log1p(jnp.exp(-jnp.abs(raw)))
        cum = dot_wide(triangle(rows, False), dt * (head_ref[1:2, :] * LOG2E))
        dt_ref[...] = dt
        cum_ref[...] = cum
        source_rows[...] = (cum - jnp.log(dt) * LOG2E).T
        square_ref[...] = jnp.zeros_like(square_ref)

    channel = channel_ref[...]
    pre = conv_pre(conv_taps(value_ref[...], info), channel)
    values = narrow(pre * sigmoid(pre))
    outputs = [channel[5:6, :] * wide(values[span]) for span in spans(rows)]
    for which in range(2):
        head = 2 * pair + which
        target = column_of(cum_ref[...], head)
        source = source_rows[pl.ds(head, 1), :]
        chosen = half_lanes(values, which)
        for i, down in enumerate(spans(rows)):
            for across in spans(rows)[: i + 1]:
                weights = jnp.exp2((target[down] - source[:, across]) + bias[down, across])
                outputs[i] += mm(narrow(weights * crossed[down, across]), chosen[across])
    scanned = jnp.concatenate(outputs, 0)
    scanned_ref[...] = scanned
    gate = gate_ref[...]
    gated = scanned * (gate * sigmoid(gate))
    low_ref[...] = narrow(gated * channel[6:7, :])
    square_ref[...] += gated * gated


def mixer_backward_kernel(
    gate_ref,
    value_ref,
    state_ref,
    steps_ref,
    info_ref,
    label_ref,
    channel_ref,
    state_channel_ref,
    head_ref,
    scanned_ref,
    incoming_ref,
    dt_ref,
    cum_ref,
    grad_value_ref,
    grad_state_ref,
    grad_steps_ref,
    channel_grad_ref,
    state_grad_ref,
    head_grad_ref,
    crossed,
    bias,
    summed,
    states_low,
    source_rows,
    dt_rows,
    target_sums,
    source_sums,
):
    pair = pl.program_id(0)
    info = info_ref[...]
    rows = info.shape[0]
    half = state_ref.shape[1] // 2

    @pl.when(pair == 0)
    def _():
        pre = conv_pre(conv_taps(state_ref[...], info), state_channel_ref[...])
        states = narrow(pre * sigmoid(pre))
        states_low[...] = states
        crossed[...] = contract_cols(states[:, half:], states[:, :half])
        bias[...] = pair_bias(info[:, 4:5], label_ref[0:1, :])
        source_rows[...] = cum_ref[...].T
        dt_rows[...] = dt_ref[...].T
        summed[...] = jnp.zeros_like(summed)
        target_sums[...] = jnp.zeros_like(target_sums)
        source_sums[...] = jnp.zeros_like(source_sums)

    channel = channel_ref[...]
    taps = conv_taps(value_ref[...], info)
    pre = conv_pre(taps, channel)
    opened = sigmoid(pre)
    values = narrow(pre * opened)
    gate = gate_ref[...]
    gate_open = sigmoid(gate)
    silu_gate = gate * gate_open
    scanned = scanned_ref[...]
    gated = scanned * silu_gate
    incoming = incoming_ref[...]
    gain_grad = jnp.sum(incoming * gated, 0, keepdims=True)
    grad_gated = incoming * channel[6:7, :] + 2.0 * gated * info[:, 5:6]
    grad_scanned = grad_gated * silu_gate
    skip_grad = jnp.sum(grad_scanned * wide(values), 0, keepdims=True)
    low_grad = narrow(grad_scanned)
    value_grads = [channel[5:6, :] * grad_scanned[span] for span in spans(rows)]
    lanes = lax.broadcasted_iota(jnp.int32, (BLOCK, 128), 1)
    for which in range(2):
        head = 2 * pair + which
        target = column_of(cum_ref[...], head)
        dt_column = column_of(dt_ref[...], head)
        source = source_rows[pl.ds(head, 1), :]
        dt_row = dt_rows[pl.ds(head, 1), :]
        chosen = half_lanes(low_grad, which)
        returned = [jnp.zeros((BLOCK, 128), jnp.float32) for _ in spans(rows)]
        column_sums = [jnp.zeros((1, BLOCK), jnp.float32) for _ in spans(rows)]
        for i, down in enumerate(spans(rows)):
            row_sum = jnp.zeros((BLOCK, 1), jnp.float32)
            for j, across in enumerate(spans(rows)[: i + 1]):
                decay = jnp.exp2((target[down] - source[:, across]) + bias[down, across])
                linked = crossed[down, across]
                returned[j] += contract_rows(narrow(decay * linked), chosen[down])
                reach = decay * contract_cols(chosen[down], values[across])
                scaled = reach * dt_row[:, across]
                summed[down, across] += scaled
                column_sums[j] += jnp.sum(reach * linked, 0, keepdims=True)
                row_sum += jnp.sum(scaled * linked, 1, keepdims=True)
            target_sums[down, :] += jnp.where(lanes == head, row_sum, 0.0)
        for j, across in enumerate(spans(rows)):
            value_grads[j] += dt_column[across] * returned[j]
            source_sums[pl.ds(head, 1), across] = column_sums[j]
    grad_pre = jnp.concatenate(value_grads, 0) * (opened * (1.0 + pre * (1.0 - opened)))
    grad_value_ref[...] = narrow(conv_back(grad_pre, channel, info))
    channel_grad_ref[...] = jnp.concatenate(
        [jnp.sum(grad_pre * tap, 0, keepdims=True) for tap in taps]
        + [jnp.sum(grad_pre, 0, keepdims=True), skip_grad, gain_grad, jnp.zeros_like(gain_grad)],
        0,
    )

    @pl.when(pair == pl.num_programs(0) - 1)
    def _():
        low = narrow(summed[...])
        states = states_low[...]
        grad_keys = contract_rows(low, states[:, half:])
        grad_queries = mm(low, states[:, :half])
        state_channel = state_channel_ref[...]
        state_taps = conv_taps(state_ref[...], info)
        state_pre = conv_pre(state_taps, state_channel)
        state_open = sigmoid(state_pre)
        grad_state_pre = jnp.concatenate([grad_keys, grad_queries], 1) * (
            state_open * (1.0 + state_pre * (1.0 - state_open))
        )
        grad_state_ref[...] = narrow(conv_back(grad_state_pre, state_channel, info))
        state_grad_ref[...] = jnp.concatenate(
            [jnp.sum(grad_state_pre * tap, 0, keepdims=True) for tap in state_taps]
            + [jnp.sum(grad_state_pre, 0, keepdims=True)]
            + [jnp.zeros((3, 2 * half), jnp.float32)],
            0,
        )
        dt = dt_ref[...]
        rate = head_ref[1:2, :]
        source_columns = source_sums[...].T
        grad_rate = dot_wide(triangle(rows, True), target_sums[...] - dt * source_columns)
        grad_dt = source_columns + rate * grad_rate
        grad_steps = grad_dt * sigmoid(steps_ref[...] + head_ref[0:1, :])
        grad_steps_ref[...] = narrow(grad_steps)
        head_grad_ref[...] = jnp.concatenate(
            [
                jnp.sum(grad_steps, 0, keepdims=True),
                jnp.sum(grad_rate * dt * rate, 0, keepdims=True),
                jnp.zeros((6, 128), jnp.float32),
            ],
            0,
        )


def copies_of(starts_ref, pieces, whole, done, column=0):
    rows = pieces[0].shape[0]
    width = whole.shape[1]
    copies = []
    for at, piece in enumerate(pieces):
        start = pl.multiple_of(starts_ref[at] * rows, rows)
        copies.append(
            pltpu.make_async_copy(
                piece.at[:, column : column + width], whole.at[pl.ds(start, rows)], done.at[at]
            )
        )
    for copy in copies:
        copy.start()
    return copies


def wait_all(copies):
    for copy in copies:
        copy.wait()


def smem():
    return pl.BlockSpec(memory_space=pltpu.SMEM)


def vmem():
    return pl.BlockSpec(memory_space=pltpu.VMEM)


def hbm():
    return pl.BlockSpec(memory_space=pltpu.HBM)


def rotated(values, cosine, sinusoid):
    lanes = lax.broadcasted_iota(jnp.int32, values.shape, 1)
    quarter = HEAD_SIZE // 2
    swapped = jnp.where(
        lanes % HEAD_SIZE < quarter,
        pltpu.roll(values, values.shape[1] - quarter, 1),
        pltpu.roll(values, quarter, 1),
    )
    return values * cosine + swapped * sinusoid


def attention_forward_kernel(
    count,
    query_width,
    rank_ref,
    starts_ref,
    normed_ref,
    info_ref,
    label_ref,
    cosine_ref,
    sinusoid_ref,
    gated_ref,
    factor_ref,
    *refs,
):
    pieces = refs[:count]
    attended_ref, turned_ref, key_ref, value_ref, logsum_ref, mamba_ref, *mixed = refs[count:-4]
    bias, projected, whole, done = refs[-4:]
    copies = copies_of(starts_ref, pieces, whole, done)
    rows = normed_ref.shape[0]
    cosine, sinusoid = cosine_ref[...], sinusoid_ref[...]
    bias[...] = pair_bias(info_ref[:, 4:5], label_ref[0:1, :])
    wait_all(copies)
    end = projected.shape[1]
    for at in range(0, end, 256):
        projected[:, at : at + 256] = mm(normed_ref[...], whole[:, at : at + 256])
    lanes = lax.broadcasted_iota(jnp.int32, (rows, 128), 1)
    own = (lanes < HEAD_SIZE) == (rank_ref[0] == 0)

    def doubled(values):
        return jnp.where(own, values, pltpu.roll(values, HEAD_SIZE, 1))

    middle = query_width + 128
    keys = narrow(doubled(rotated(projected[:, query_width:middle], cosine, sinusoid)))
    values = narrow(doubled(projected[:, middle : middle + 128]))
    key_ref[...] = keys
    value_ref[...] = values
    scaling = 1.0 / math.sqrt(HEAD_SIZE)
    logsums = [jnp.zeros((BLOCK, 128), jnp.float32) for _ in spans(rows)]
    block_lanes = lax.broadcasted_iota(jnp.int32, (BLOCK, 128), 1)
    for pair in range(query_width // 128):
        columns = slice(128 * pair, 128 * pair + 128)
        queries = narrow(rotated(projected[:, columns], cosine, sinusoid))
        turned_ref[:, columns] = queries
        results = [jnp.zeros((BLOCK, 128), jnp.float32) for _ in spans(rows)]
        for which in range(2):
            chosen = half_lanes(queries, which)
            reading = half_lanes(values, which)
            for i, down in enumerate(spans(rows)):
                width = BLOCK * (i + 1)
                scores = contract_cols(chosen[down], keys[:width]) * scaling + bias[down, :width]
                highest = jnp.max(scores, 1, keepdims=True)
                weights = jnp.exp(scores - highest)
                total = jnp.sum(weights, 1, keepdims=True)
                results[i] += mm(narrow(weights * (1.0 / total)), reading[:width])
                logsums[i] = jnp.where(
                    block_lanes == 2 * pair + which, highest + jnp.log(total), logsums[i]
                )
        for i, down in enumerate(spans(rows)):
            attended_ref[down, columns] = narrow(results[i])
    for i, down in enumerate(spans(rows)):
        logsum_ref[down, :] = logsums[i]
    gated_end = end + gated_ref.shape[1]
    for at in range(0, whole.shape[0], 256):
        span = slice(at, at + 256)
        mamba = contract_cols(gated_ref[...], whole[span, end:gated_end])
        mamba_ref[:, span] = narrow(mamba)
        part = contract_cols(attended_ref[...], whole[span, gated_end:])
        low = narrow(factor_ref[...] * mamba + part)
        mixed[0][:, span] = low[: rows // 2]
        mixed[1][:, span] = low[rows // 2 :]


def attention_backward_kernel(
    count,
    column,
    rank_ref,
    starts_ref,
    mix_ref,
    turned_ref,
    key_ref,
    value_ref,
    logsum_ref,
    info_ref,
    label_ref,
    cosine_ref,
    sinusoid_ref,
    *refs,
):
    pieces = refs[:count]
    grad_query_ref, grad_keyvalue_ref, bias, down, done = refs[count:]
    copies = copies_of(starts_ref, pieces, down, done, column)
    rows = turned_ref.shape[0]
    cosine, sinusoid = cosine_ref[...], sinusoid_ref[...]
    bias[...] = pair_bias(info_ref[:, 4:5], label_ref[0:1, :])
    keys, values = key_ref[...], value_ref[...]
    wait_all(copies)
    grad_attended = narrow(mm(mix_ref[...], down[...]))
    scaling = 1.0 / math.sqrt(HEAD_SIZE)
    zero = jnp.zeros((BLOCK, 128), jnp.float32)
    key_grads = [zero for _ in spans(rows)]
    value_grads = [zero for _ in spans(rows)]
    for pair in range(turned_ref.shape[1] // 128):
        columns = slice(128 * pair, 128 * pair + 128)
        query_grads = [zero for _ in spans(rows)]
        for which in range(2):
            queries = half_lanes(turned_ref[:, columns], which)
            incoming = half_lanes(grad_attended[:, columns], which)
            reading = half_lanes(keys, which)
            head = 2 * pair + which
            for i, down in enumerate(spans(rows)):
                width = BLOCK * (i + 1)
                scores = contract_cols(queries[down], keys[:width]) * scaling + bias[down, :width]
                probs = jnp.exp(scores - logsum_ref[down, head : head + 1])
                grad_probs = contract_cols(incoming[down], values[:width])
                inner_sum = jnp.sum(grad_probs * probs, 1, keepdims=True)
                grad_scores = narrow(probs * (grad_probs - inner_sum))
                probs_low = narrow(probs)
                query_grads[i] += mm(grad_scores, reading[:width])
                for j, across in enumerate(spans(rows)[: i + 1]):
                    key_grads[j] += contract_rows(grad_scores[:, across], queries[down])
                    value_grads[j] += contract_rows(probs_low[:, across], incoming[down])
        grad_query_ref[:, columns] = narrow(
            rotated(jnp.concatenate(query_grads, 0) * scaling, cosine, -sinusoid)
        )
    lanes = lax.broadcasted_iota(jnp.int32, (rows, 128), 1)
    own = (lanes < HEAD_SIZE) == (rank_ref[0] == 0)

    def placed(values):
        return jnp.where(own, values + pltpu.roll(values, HEAD_SIZE, 1), 0.0)

    key_grad = rotated(placed(jnp.concatenate(key_grads, 0) * scaling), cosine, -sinusoid)
    grad_keyvalue_ref[:, :128] = narrow(key_grad)
    grad_keyvalue_ref[:, 128:] = narrow(placed(jnp.concatenate(value_grads, 0)))


def block_spec(shape, index):
    return pl.BlockSpec(shape, index)


def fixed(array):
    return pl.BlockSpec(array.shape, lambda p: (0, 0))


def params():
    return pltpu.CompilerParams(vmem_limit_bytes=62 * 1024 * 1024)


def mixer_forward(projected, widths, info, labels, channel, state_channel, heads):
    rows = info.shape[0]
    width, state_at, steps_at = widths
    pairs = width // 128
    state_width = state_channel.shape[1]
    column = lambda p: (0, p)
    return pl.pallas_call(
        mixer_forward_kernel,
        grid=(pairs,),
        in_specs=[
            block_spec((rows, 128), column),
            block_spec((rows, 128), lambda p: (0, pairs + p)),
            block_spec((rows, state_width), lambda p: (0, state_at // state_width)),
            block_spec((rows, 128), lambda p: (0, steps_at // 128)),
            fixed(info),
            fixed(labels),
            block_spec((8, 128), column),
            fixed(state_channel),
            fixed(heads),
        ],
        out_specs=[
            block_spec((rows, 128), column),
            block_spec((rows, 128), column),
            block_spec((rows, 128), lambda p: (0, 0)),
            block_spec((rows, 128), lambda p: (0, 0)),
            block_spec((rows, 128), lambda p: (0, 0)),
        ],
        out_shape=[
            jax.ShapeDtypeStruct((rows, width), jnp.bfloat16),
            jax.ShapeDtypeStruct((rows, width), jnp.float32),
            jax.ShapeDtypeStruct((rows, 128), jnp.float32),
            jax.ShapeDtypeStruct((rows, 128), jnp.float32),
            jax.ShapeDtypeStruct((rows, 128), jnp.float32),
        ],
        scratch_shapes=[
            pltpu.VMEM((rows, rows), jnp.float32),
            pltpu.VMEM((rows, rows), jnp.float32),
            pltpu.VMEM((128, rows), jnp.float32),
        ],
        compiler_params=params(),
        cost_estimate=pl.CostEstimate(flops=1, bytes_accessed=1, transcendentals=0),
        name="mixer_forward",
    )(projected, projected, projected, projected, info, labels, channel, state_channel, heads)


def mixer_backward(
    projected, widths, info, labels, channel, state_channel, heads, scanned, incoming, dt, cum
):
    rows = info.shape[0]
    width, state_at, steps_at = widths
    pairs = width // 128
    state_width = state_channel.shape[1]
    column = lambda p: (0, p)
    still = lambda p: (0, 0)
    return pl.pallas_call(
        mixer_backward_kernel,
        grid=(pairs,),
        in_specs=[
            block_spec((rows, 128), column),
            block_spec((rows, 128), lambda p: (0, pairs + p)),
            block_spec((rows, state_width), lambda p: (0, state_at // state_width)),
            block_spec((rows, 128), lambda p: (0, steps_at // 128)),
            fixed(info),
            fixed(labels),
            block_spec((8, 128), column),
            fixed(state_channel),
            fixed(heads),
            block_spec((rows, 128), column),
            block_spec((rows, 128), column),
            fixed(dt),
            fixed(cum),
        ],
        out_specs=[
            block_spec((rows, 128), column),
            block_spec((rows, state_width), still),
            block_spec((rows, 128), still),
            block_spec((8, 128), column),
            block_spec((8, state_width), still),
            block_spec((8, 128), still),
        ],
        out_shape=[
            jax.ShapeDtypeStruct((rows, width), jnp.bfloat16),
            jax.ShapeDtypeStruct((rows, state_width), jnp.bfloat16),
            jax.ShapeDtypeStruct((rows, 128), jnp.bfloat16),
            jax.ShapeDtypeStruct((8, width), jnp.float32),
            jax.ShapeDtypeStruct((8, state_width), jnp.float32),
            jax.ShapeDtypeStruct((8, 128), jnp.float32),
        ],
        scratch_shapes=[
            pltpu.VMEM((rows, rows), jnp.float32),
            pltpu.VMEM((rows, rows), jnp.float32),
            pltpu.VMEM((rows, rows), jnp.float32),
            pltpu.VMEM((rows, state_width), jnp.bfloat16),
            pltpu.VMEM((128, rows), jnp.float32),
            pltpu.VMEM((128, rows), jnp.float32),
            pltpu.VMEM((rows, 128), jnp.float32),
            pltpu.VMEM((128, rows), jnp.float32),
        ],
        compiler_params=params(),
        cost_estimate=pl.CostEstimate(flops=1, bytes_accessed=1, transcendentals=0),
        name="mixer_backward",
    )(
        projected,
        projected,
        projected,
        projected,
        info,
        labels,
        channel,
        state_channel,
        heads,
        scanned,
        incoming,
        dt,
        cum,
    )


def attention_forward(
    rank, starts, normed, info, labels, cosine, sinusoid, gated, factor, pieces, query_width
):
    rows, model = normed.shape
    count = len(pieces)
    columns = pieces[0].shape[1]
    end = columns - gated.shape[1] - query_width
    arrays = (normed, info, labels, cosine, sinusoid, gated, factor)
    return pl.pallas_call(
        lambda *refs: attention_forward_kernel(count, query_width, *refs),
        in_specs=[smem(), smem()] + [vmem()] * len(arrays) + [hbm()] * count,
        out_specs=[vmem()] * 8,
        out_shape=[
            jax.ShapeDtypeStruct((rows, query_width), jnp.bfloat16),
            jax.ShapeDtypeStruct((rows, query_width), jnp.bfloat16),
            jax.ShapeDtypeStruct((rows, 128), jnp.bfloat16),
            jax.ShapeDtypeStruct((rows, 128), jnp.bfloat16),
            jax.ShapeDtypeStruct((rows, 128), jnp.float32),
            jax.ShapeDtypeStruct((rows, model), jnp.bfloat16),
            jax.ShapeDtypeStruct((rows // 2, model), jnp.bfloat16),
            jax.ShapeDtypeStruct((rows // 2, model), jnp.bfloat16),
        ],
        scratch_shapes=[
            pltpu.VMEM((rows, rows), jnp.float32),
            pltpu.VMEM((rows, end), jnp.float32),
            pltpu.VMEM((model, columns), jnp.bfloat16),
            pltpu.SemaphoreType.DMA((count,)),
        ],
        compiler_params=params(),
        cost_estimate=pl.CostEstimate(flops=1, bytes_accessed=1, transcendentals=0),
        name="attention_forward",
    )(rank, starts, *arrays, *pieces)


def attention_backward(
    rank, starts, mix, turned, keys, values, logsum, info, labels, cosine, sinusoid, pieces, column
):
    rows, query_width = turned.shape
    count = len(pieces)
    model = mix.shape[1]
    arrays = (mix, turned, keys, values, logsum, info, labels, cosine, sinusoid)
    return pl.pallas_call(
        lambda *refs: attention_backward_kernel(count, column, *refs),
        in_specs=[smem(), smem()] + [vmem()] * len(arrays) + [hbm()] * count,
        out_specs=[vmem()] * 2,
        out_shape=[
            jax.ShapeDtypeStruct((rows, query_width), jnp.bfloat16),
            jax.ShapeDtypeStruct((rows, 256), jnp.bfloat16),
        ],
        scratch_shapes=[
            pltpu.VMEM((rows, rows), jnp.float32),
            pltpu.VMEM((model, query_width), jnp.bfloat16),
            pltpu.SemaphoreType.DMA((count,)),
        ],
        compiler_params=params(),
        cost_estimate=pl.CostEstimate(flops=1, bytes_accessed=1, transcendentals=0),
        name="attention_backward",
    )(rank, starts, *arrays, *pieces)


def project_kernel(count, starts_ref, input_ref, gain_ref, *refs):
    pieces, out_ref, normed_ref, whole, done = refs[:count], *refs[count:]
    copies = copies_of(starts_ref, pieces, whole, done)
    residual = wide(input_ref[...])
    normed_ref[...] = narrow(residual * inverse_rms(residual) * gain_ref[...])
    wait_all(copies)
    left = normed_ref[...]
    columns = out_ref.shape[1]
    for at in range(0, columns, 256):
        span = slice(at, min(at + 256, columns))
        out_ref[:, span] = mm(left, whole[:, span])


def project(starts, pieces, left, gain):
    count = len(pieces)
    rows, columns = pieces[0].shape
    return pl.pallas_call(
        lambda *refs: project_kernel(count, *refs),
        in_specs=[
            pl.BlockSpec(memory_space=pltpu.SMEM),
            pl.BlockSpec(memory_space=pltpu.VMEM),
            pl.BlockSpec(memory_space=pltpu.VMEM),
        ]
        + [pl.BlockSpec(memory_space=pltpu.HBM)] * count,
        out_specs=[pl.BlockSpec(memory_space=pltpu.VMEM)] * 2,
        out_shape=[
            jax.ShapeDtypeStruct((left.shape[0], columns), jnp.float32),
            jax.ShapeDtypeStruct(left.shape, jnp.bfloat16),
        ],
        scratch_shapes=[
            pltpu.VMEM((count * rows, columns), jnp.bfloat16),
            pltpu.SemaphoreType.DMA((count,)),
        ],
        compiler_params=params(),
        cost_estimate=pl.CostEstimate(flops=1, bytes_accessed=1, transcendentals=0),
        name="project",
    )(starts, left, gain, *pieces)


def back_kernel(count, parts, starts_ref, *refs):
    lefts, pieces = refs[:parts], refs[parts : parts + 2 * count]
    out_ref, whole, shared, done, shared_done = refs[-5:]
    copies = copies_of(starts_ref, pieces[:count], whole, done)
    copies += copies_of(starts_ref, pieces[count:], shared, shared_done)
    wait_all(copies)
    model = whole.shape[0]
    for at in range(0, model, 256):
        span = slice(at, at + 256)
        total = jnp.zeros((out_ref.shape[0], 256), jnp.float32)
        for weight, several in ((whole, lefts[:-2]), (shared, lefts[-2:])):
            column = 0
            for left in several:
                total += contract_cols(left[...], weight[span, column : column + left.shape[1]])
                column += left.shape[1]
        out_ref[:, span] = narrow(total)


def back_project(starts, pieces, shared_pieces, lefts):
    count = len(pieces)
    rows, columns = pieces[0].shape
    shared = lefts[-2].shape[1] + lefts[-1].shape[1]
    parts = len(lefts)
    tokens = lefts[0].shape[0]
    return pl.pallas_call(
        lambda *refs: back_kernel(count, parts, *refs),
        in_specs=[smem()] + [vmem()] * parts + [hbm()] * (2 * count),
        out_specs=vmem(),
        out_shape=jax.ShapeDtypeStruct((tokens, count * rows), jnp.bfloat16),
        scratch_shapes=[
            pltpu.VMEM((count * rows, columns), jnp.bfloat16),
            pltpu.VMEM((count * rows, shared), jnp.bfloat16),
            pltpu.SemaphoreType.DMA((count,)),
            pltpu.SemaphoreType.DMA((count,)),
        ],
        compiler_params=params(),
        cost_estimate=pl.CostEstimate(flops=1, bytes_accessed=1, transcendentals=0),
        name="back_project",
    )(starts, *lefts, *pieces, *shared_pieces)


def feed_kernel(
    count, hidden, starts_ref, residual_ref, one_ref, two_ref, first_ref, second_ref, *refs
):
    gain_ref, cotangent_ref, *refs = refs
    pieces = refs[:count]
    middle_ref, input_ref, activated_ref, grad_ref, *lows, forward_ref, whole, done = refs[count:]
    copies = copies_of(starts_ref, pieces, whole, done)
    half = one_ref.shape[0]
    for at, own_ref, far_ref in ((0, one_ref, first_ref), (half, two_ref, second_ref)):
        span = slice(at, at + half)
        middle = wide(residual_ref[span, :]) + (wide(own_ref[...]) + wide(far_ref[...]))
        middle_ref[span, :] = middle
        input_ref[span, :] = narrow(middle * inverse_rms(middle) * gain_ref[...])
    wait_all(copies)

    def tile(step, carry):
        at = pl.multiple_of(step * 256, 256)
        far = pl.multiple_of(hidden + step * 256, 256)
        last = pl.multiple_of(2 * hidden + step * 256, 256)
        gate = mm(input_ref[...], whole[:, pl.ds(at, 256)])
        up = mm(input_ref[...], whole[:, pl.ds(far, 256)])
        grad = mm(cotangent_ref[...], whole[:, pl.ds(last, 256)])
        opened = sigmoid(gate)
        silu = gate * opened
        activated_ref[:, pl.ds(at, 256)] = narrow(silu * up)
        grad_ref[:, pl.ds(far, 256)] = narrow(grad * silu)
        grad_ref[:, pl.ds(at, 256)] = narrow(grad * up * opened * (1.0 + gate * (1.0 - opened)))
        return carry

    lax.fori_loop(0, hidden // 256, tile, 0)
    model = whole.shape[0]
    for at in range(0, model, 256):
        span = slice(at, at + 256)
        low = narrow(contract_cols(grad_ref[...], whole[span, : 2 * hidden]))
        lows[0][:, span] = low[:half]
        lows[1][:, span] = low[half:]
    for at in range(0, model, 256):
        span = slice(at, at + 256)
        forward_ref[:, span] = narrow(contract_cols(activated_ref[...], whole[span, 2 * hidden :]))


def feed_forward(starts, pieces, hidden, residual, mixed, gain, cotangent):
    count = len(pieces)
    rows, columns = pieces[0].shape
    tokens, model = residual.shape
    return pl.pallas_call(
        lambda *refs: feed_kernel(count, hidden, *refs),
        in_specs=[smem()] + [vmem()] * 7 + [hbm()] * count,
        out_specs=[vmem()] * 7,
        out_shape=[
            jax.ShapeDtypeStruct((tokens, model), jnp.float32),
            jax.ShapeDtypeStruct((tokens, model), jnp.bfloat16),
            jax.ShapeDtypeStruct((tokens, hidden), jnp.bfloat16),
            jax.ShapeDtypeStruct((tokens, 2 * hidden), jnp.bfloat16),
            jax.ShapeDtypeStruct((tokens // 2, model), jnp.bfloat16),
            jax.ShapeDtypeStruct((tokens // 2, model), jnp.bfloat16),
            jax.ShapeDtypeStruct((tokens, model), jnp.bfloat16),
        ],
        scratch_shapes=[
            pltpu.VMEM((count * rows, columns), jnp.bfloat16),
            pltpu.SemaphoreType.DMA((count,)),
        ],
        compiler_params=params(),
        cost_estimate=pl.CostEstimate(flops=1, bytes_accessed=1, transcendentals=0),
        name="feed_forward",
    )(starts, residual, *mixed, gain, cotangent, *pieces)


def gate_kernel(
    count,
    column,
    starts_ref,
    grad_mamba_ref,
    gate_ref,
    scanned_ref,
    gain_ref,
    square_ref,
    turned_ref,
    order_ref,
    mix_ref,
    factor_ref,
    gated_ref,
    attended_ref,
    query_ref,
    key_ref,
    *refs,
):
    pieces = refs[:count]
    incoming_ref, grad_ref, far_ref, line_ref, own_ref, weight, done = refs[count:]
    copies = copies_of(starts_ref, pieces, weight, done, column)
    outs = (far_ref, line_ref, own_ref)
    mixed = narrow(contract_cols(order_ref[...], mix_ref[...]))
    end = grads_kernel(narrow(factor_ref[...] * wide(mixed)), [gated_ref], *outs, 0)
    end = grads_kernel(mixed, [attended_ref], *outs, end)
    end = grads_kernel(turned_ref[...], [query_ref, key_ref], *outs, end)
    gate = gate_ref[...]
    opened = sigmoid(gate)
    scanned = scanned_ref[...]
    wait_all(copies)
    incoming = mm(grad_mamba_ref[...], weight[...])
    incoming_ref[...] = incoming
    grad_gated = incoming * gain_ref[...] + 2.0 * scanned * (gate * opened) * square_ref[...]
    grad_ref[...] = narrow(grad_gated * scanned * opened * (1.0 + gate * (1.0 - opened)))
    grads_kernel(turned_ref[...], [grad_ref], *outs, end)


def gate_backward(starts, projected, scanned, arrays, pieces, column, columns):
    rows, width = scanned.shape
    model = pieces[0].shape[0] * len(pieces)
    count = len(pieces)
    still = lambda p: (0, 0)
    grad_mamba, *others = arrays
    shapes = [
        ((rows, width), jnp.float32),
        ((rows, width), jnp.bfloat16),
        ((model // 2, columns), jnp.bfloat16),
        ((model // 4, columns), jnp.bfloat16),
        ((model // 4, columns), jnp.bfloat16),
    ]
    return pl.pallas_call(
        lambda *refs: gate_kernel(count, column, *refs),
        grid=(1,),
        in_specs=[
            smem(),
            fixed(grad_mamba),
            block_spec((rows, width), still),
            fixed(scanned),
        ]
        + [fixed(array) for array in others]
        + [hbm()] * count,
        out_specs=[block_spec(shape, still) for shape, _ in shapes],
        out_shape=[jax.ShapeDtypeStruct(shape, kind) for shape, kind in shapes],
        scratch_shapes=[
            pltpu.VMEM((model, width), jnp.bfloat16),
            pltpu.SemaphoreType.DMA((count,)),
        ],
        compiler_params=params(),
        cost_estimate=pl.CostEstimate(flops=1, bytes_accessed=1, transcendentals=0),
        name="gate_backward",
    )(starts, grad_mamba, projected, scanned, *others, *pieces)


def swaps(size, bit):
    return [(i, i ^ bit) for i in range(size)]


def ring(size):
    return [(i, (i + 4) % size) for i in range(size)]


def tie(*values):
    return lax.optimization_barrier(values)


class Gathering:
    def __init__(self, shards, size):
        self.size = size
        self.held = {(group, 0): shard for group, shard in enumerate(shards)}
        self.lined, self.crossed, self.flying = {}, {}, {}

    def step(self, begun, awaited, main):
        def send(value, pairs):
            return lax.ppermute(value, "fsdp", pairs)

        for kind, group, k in begun:
            if kind == "z":
                value = send(self.held[group, k - 1], ring(self.size))
            elif kind == "r":
                value = send(self.held[group, 0], [(j, i) for i, j in ring(self.size)])
            elif kind == "x":
                value = send(self.held[group, k], swaps(self.size, 2))
            else:
                value = [
                    send(self.held[group, k], swaps(self.size, 1)),
                    send(self.lined[group, k], swaps(self.size, 1)),
                ]
                if (kind, group, k) not in awaited:
                    self.crossed[group, k] = value
                    continue
            self.flying[kind, group, k] = value
        values = main()
        self.held, landed, values = lax.optimization_barrier(
            (self.held, [self.flying.pop(key) for key in awaited], values)
        )
        for (kind, group, k), value in zip(awaited, landed):
            kept = {"x": self.lined, "c": self.crossed}.get(kind, self.held)
            kept[group, k] = value
        return values

    def pieces(self, group):
        return [
            piece
            for k in range(self.size // 4)
            for piece in (
                self.held[group, k],
                self.crossed[group, k][0],
                self.lined[group, k],
                self.crossed[group, k][1],
            )
        ]


def grads_kernel(turned, rights, far_ref, line_ref, own_ref, column):
    half = turned.shape[0] // 2
    quarter = half // 2
    for right in rights:
        width = right.shape[1]
        for at in range(0, width, 256):
            size = min(256, width - at)
            product = narrow(mm(turned, right[:, at : at + size]))
            span = slice(column + at, column + at + size)
            far_ref[:, span] = product[half:]
            line_ref[:, span] = product[quarter:half]
            own_ref[:, span] = product[:quarter]
        column += width
    return column


def last_kernel(turned_ref, *refs):
    grads_kernel(turned_ref[...], refs[:-3], *refs[-3:], 0)


def feed_grads_kernel(order_ref, cotangent_ref, input_ref, activated_ref, grad_ref, *outs):
    turned = narrow(contract_cols(order_ref[...], cotangent_ref[...]))
    column = grads_kernel(turned, [activated_ref], *outs, 0)
    turned = narrow(contract_cols(order_ref[...], input_ref[...]))
    grads_kernel(turned, [grad_ref], *outs, column)


def weight_grads(kernel, arrays, model, columns, name):
    return pl.pallas_call(
        kernel,
        in_specs=[vmem()] * len(arrays),
        out_specs=[vmem()] * 3,
        out_shape=[
            jax.ShapeDtypeStruct((rows, columns), jnp.bfloat16)
            for rows in (model // 2, model // 4, model // 4)
        ],
        compiler_params=params(),
        cost_estimate=pl.CostEstimate(flops=1, bytes_accessed=1, transcendentals=0),
        name=name,
    )(*arrays)


def send_core(far, size):
    return lax.ppermute(far, "fsdp", swaps(size, 1))


def send_line(line, size):
    return lax.ppermute(line, "fsdp", swaps(size, 2))


def send_block(parts, size, k):
    return lax.ppermute(parts[k], "fsdp", [(i, (i - 4 * k) % size) for i in range(size)])


def send_blocks(parts, size):
    return [send_block(parts, size, k) for k in range(1, size // 4)]


def send_ring(total, size):
    return lax.ppermute(total, "fsdp", ring(size))


def add_core(came, line, own):
    half = own.shape[0]
    return narrow(wide(line) + wide(came[half:])), narrow(wide(own) + wide(came[:half]))


def add_line(came, own, size):
    return narrow(wide(own) + wide(came)).reshape(size // 4, -1, own.shape[1])


def add_blocks(parts, came):
    total = wide(parts[0])
    for block in came:
        total = total + wide(block)
    return total


def packed_body(
    size,
    block_input,
    segment_ids,
    output_cotangent,
    input_gain,
    inner_weight,
    timestep_weight,
    state_weight,
    query_weight,
    keyvalue_matrix,
    conv_kernel,
    conv_offset,
    timestep_bias,
    decay_log,
    skip_scale,
    gated_gain,
    mamba_down,
    attention_down,
    middle_gain,
    gateup_weight,
    down_weight,
):
    rank = lax.axis_index("tp")
    at = lax.axis_index("fsdp")
    depth = size // 4
    rows = segment_ids.shape[0]
    own_rows = rows // 2
    shard, _, width = inner_weight.shape
    model = shard * size
    heads = timestep_weight.shape[1]
    state_width = state_weight.shape[1]
    query_width = query_weight.shape[1]
    keyvalue_width = keyvalue_matrix.shape[1]
    attended_width = attention_down.shape[0]
    hidden = gateup_weight.shape[2]
    ssm_width = gated_gain.shape[0]
    state_at = 2 * width
    steps_at = state_at + state_width

    def other(values):
        return lax.ppermute(values, "tp", swaps(2, 1))

    def joined(own, far):
        first = jnp.where(rank == 0, own, far)
        second = jnp.where(rank == 0, far, own)
        return jnp.concatenate([first, second], 0)

    def own_half(values):
        return lax.dynamic_slice_in_dim(values, rank * own_rows, own_rows, 0)

    def far_half(values):
        return lax.dynamic_slice_in_dim(values, (1 - rank) * own_rows, own_rows, 0)

    first_shard = jnp.concatenate(
        [
            inner_weight.reshape(shard, 2 * width),
            state_weight,
            jnp.pad(timestep_weight, ((0, 0), (0, 128 - heads))),
        ],
        1,
    )
    second_shard = jnp.concatenate(
        [query_weight, keyvalue_matrix, jnp.concatenate([mamba_down, attention_down], 0).T], 1
    )
    third_shard = jnp.concatenate([gateup_weight.reshape(shard, 2 * hidden), down_weight.T], 1)
    ring_at, x_at, core_at = at // 4, (at // 2) % 2, at % 2

    def block_of(distance, x_flip, core_flip):
        return ((ring_at - distance + depth) % depth) * 4 + (x_at ^ x_flip) * 2 + (
            core_at ^ core_flip
        )

    starts = jnp.stack(
        [block_of(k, i, j) for k in range(depth) for i in range(2) for j in range(2)]
    ).astype(jnp.int32)
    relative = jnp.arange(model, dtype=jnp.int32)
    piece_at = relative // shard
    absolute = (
        block_of(piece_at % depth, (piece_at // depth) % 2, piece_at // (2 * depth)) * shard
        + relative % shard
    )
    order = (absolute[:, None] == relative[None, :]).astype(jnp.bfloat16)

    labels = segment_ids.astype(jnp.float32)
    info = [jnp.zeros((rows, 1), jnp.float32)]
    for distance in range(1, 4):
        earlier = jnp.concatenate([jnp.full((distance,), -1.0), labels[:-distance]], 0)
        info.append((earlier == labels).astype(jnp.float32)[:, None])
    info = jnp.concatenate(info + [labels[:, None], jnp.zeros((rows, 123), jnp.float32)], 1)
    label_rows = jnp.broadcast_to(labels[None, :], (8, rows))
    repeat = width // heads
    local_skip = lax.dynamic_slice_in_dim(skip_scale, rank * heads, heads, 0)
    local = lambda array: lax.dynamic_slice_in_dim(array, rank * width, width, array.ndim - 1)
    local_gain = local(gated_gain)
    channel = jnp.concatenate(
        [
            local(conv_kernel),
            local(conv_offset)[None],
            jnp.repeat(local_skip, repeat)[None],
            local_gain[None],
            jnp.zeros((1, width), jnp.float32),
        ],
        0,
    )
    state_channel = jnp.concatenate(
        [
            conv_kernel[:, ssm_width:],
            conv_offset[None, ssm_width:],
            jnp.zeros((3, state_width), jnp.float32),
        ],
        0,
    )
    local_head = lambda array: lax.dynamic_slice_in_dim(array, rank * heads, heads, 0)
    head_rows = jnp.pad(
        jnp.stack([local_head(timestep_bias), -jnp.exp(local_head(decay_log))]),
        ((0, 6), (0, 128 - heads)),
    )
    quarter = HEAD_SIZE // 2
    frequency = jnp.exp(
        jnp.arange(quarter, dtype=jnp.float32) * (-2.0 * math.log(ROPE_BASE) / HEAD_SIZE)
    )
    angles = jnp.arange(rows, dtype=jnp.float32)[:, None] * frequency[None, :]
    cosine = jnp.concatenate([jnp.cos(angles)] * 4, 1)
    sinusoid = jnp.sin(angles)
    sinusoid = jnp.concatenate([-sinusoid, sinusoid, -sinusoid, sinusoid], 1)
    rank_array = rank.astype(jnp.int32)[None]
    mixer_widths = (width, state_at, steps_at)

    gathering = Gathering([first_shard, second_shard, third_shard], size)
    step = gathering.step
    empty = lambda: ()
    far_input = other(block_input)
    step([("z", 0, 1), ("x", 0, 0)], [("z", 0, 1)], empty)
    tables = step(
        [("z", 0, 2), ("x", 0, 1)],
        [("z", 0, 2), ("x", 0, 0)],
        lambda: (info, label_rows, channel, state_channel, head_rows),
    )
    info, label_rows, channel, state_channel, head_rows = tables
    group_input, cosine, sinusoid, order = step(
        [("z", 0, 3), ("x", 0, 2), ("c", 0, 0)],
        [("z", 0, 3), ("x", 0, 1)],
        lambda: (joined(block_input, far_input), cosine, sinusoid, order),
    )
    step(
        [("x", 0, 3), ("z", 1, 1), ("c", 0, 1)], [("z", 1, 1), ("x", 0, 2), ("x", 0, 3)], empty
    )
    projected, normed = step(
        [("c", 0, 2), ("c", 0, 3), ("x", 1, 0), ("z", 1, 2), ("x", 1, 1), ("r", 1, 3)],
        [("z", 1, 2), ("x", 1, 0), ("r", 1, 3), ("x", 1, 1)],
        lambda: project(starts, gathering.pieces(0), group_input, input_gain[None]),
    )

    def mix_forward():
        return mixer_forward(
            projected, mixer_widths, info, label_rows, channel, state_channel, head_rows
        )

    gated_low, scanned, square_lanes, dt, cum = step(
        [("x", 1, 2), ("x", 1, 3), ("z", 2, 1), ("x", 2, 0), ("c", 1, 0), ("c", 1, 1)],
        [("x", 1, 2), ("x", 1, 3), ("z", 2, 1)],
        mix_forward,
    )
    square_own = jnp.sum(square_lanes, 1)
    squares, far_cotangent = step(
        [("c", 1, 2), ("c", 1, 3)],
        [("c", 1, 2), ("c", 1, 3)],
        lambda: (square_own + other(square_own), other(output_cotangent)),
    )
    norm_factor = lax.rsqrt(squares / ssm_width + EPSILON)
    factor = wide(narrow(norm_factor))[:, None]

    def attend():
        return (
            attention_forward(
                rank_array,
                starts,
                normed,
                info,
                label_rows,
                cosine,
                sinusoid,
                gated_low,
                factor,
                gathering.pieces(1),
                query_width,
            ),
            far_cotangent,
        )

    attending, far_cotangent = step(
        [("x", 2, 1), ("z", 2, 2)], [("z", 2, 2), ("x", 2, 0)], attend
    )
    attended, turned, keys, values, logsum, mamba_own, mixed_one, mixed_two = attending
    mixed_first, cotangent = step(
        [("z", 2, 3), ("x", 2, 2), ("c", 2, 0)],
        [("z", 2, 3), ("x", 2, 1)],
        lambda: (
            other(mixed_one),
            joined(output_cotangent, far_cotangent),
        ),
    )
    mixed_second = step(
        [("x", 2, 3), ("c", 2, 1)],
        [("x", 2, 2), ("x", 2, 3)],
        lambda: other(mixed_two),
    )
    step([("c", 2, 2), ("c", 2, 3)], [], empty)
    middle, hidden_in, activated, grad_gateup, low_one, low_two, feedforward_low = feed_forward(
        starts,
        gathering.pieces(2),
        hidden,
        group_input,
        [mixed_one, mixed_two, mixed_first, mixed_second],
        middle_gain[None],
        cotangent,
    )

    hidden_first = other(low_one)
    feed_far, feed_line, feed_own = weight_grads(
        feed_grads_kernel,
        [order, cotangent, hidden_in, activated, grad_gateup],
        model,
        3 * hidden,
        "feed_grads",
    )
    hidden_first, feed_far, low_two, feedforward_low = tie(
        hidden_first, feed_far, low_two, feedforward_low
    )
    hidden_second = other(low_two)
    feed_came = send_core(feed_far, size)
    feed_came, feedforward_low = tie(feed_came, feedforward_low)
    cuts = [0, 2 * hidden, 3 * hidden]
    lines, owns = [], []
    for i, j in zip(cuts, cuts[1:]):
        line, own = add_core(feed_came[:, i:j], feed_line[:, i:j], feed_own[:, i:j])
        lines.append(line)
        owns.append(own)
    came = send_line(lines[0], size)
    normed_turned = narrow(contract_cols(order, normed))
    hidden_first, hidden_second, lines, owns, feedforward_low, normed_turned = tie(
        hidden_first, hidden_second, lines, owns, feedforward_low, normed_turned
    )

    grad_hidden = jnp.concatenate(
        [wide(low_one) + wide(hidden_first), wide(low_two) + wide(hidden_second)], 0
    )
    middle_rms = inverse_rms(middle)
    middle_normal = middle * middle_rms
    middle_gain_part = jnp.sum(grad_hidden * middle_normal, 0)
    middle_scaled = grad_hidden * middle_gain
    grad_middle = wide(cotangent) + middle_rms * (
        middle_scaled - middle_normal * jnp.mean(middle_scaled * middle_normal, -1, keepdims=True)
    )
    mix_low = narrow(grad_middle)
    mix = wide(mix_low)
    square_sum = jnp.sum(mix * wide(mamba_own), -1)
    square_sum = square_sum + other(square_sum)
    grad_mamba = narrow(factor * mix)
    second_pieces = gathering.pieces(1)
    mamba_at = query_width + keyvalue_width
    grad_query, grad_keyvalue = attention_backward(
        rank_array,
        starts,
        mix_low,
        turned,
        keys,
        values,
        logsum,
        info,
        label_rows,
        cosine,
        sinusoid,
        second_pieces,
        mamba_at + width,
    )
    came_first, square_sum, grad_query, grad_mamba, lines, owns = tie(
        came, square_sum, grad_query, grad_mamba, lines, owns
    )
    came = send_line(lines[1], size)
    first_parts = add_line(came_first, owns[0], size)
    first_came = send_blocks(first_parts, size)
    square_column = wide(
        narrow(square_sum * -0.5 * norm_factor * norm_factor * norm_factor / ssm_width)
    )[:, None]
    second_width = width + attended_width + query_width + keyvalue_width
    grad_gated_low, grad_gate, second_far, second_line, second_own = gate_backward(
        starts,
        projected,
        scanned,
        [
            grad_mamba,
            local_gain[None],
            square_column,
            normed_turned,
            order,
            mix_low,
            factor.reshape(1, rows),
            gated_low,
            attended,
            grad_query,
            grad_keyvalue,
        ],
        second_pieces,
        mamba_at,
        second_width + width,
    )
    came, second_far, feedforward_low = tie(came, second_far, feedforward_low)

    second_came = send_core(second_far, size)
    feed_parts = add_line(came, owns[1], size)
    second_came, grad_gated_low, feed_parts = tie(second_came, grad_gated_low, feed_parts)
    second_line, second_own = add_core(second_came, second_line, second_own)
    second_line, second_own, grad_gated_low = tie(second_line, second_own, grad_gated_low)
    second_came = send_line(second_line, size)
    feed_came = send_blocks(feed_parts, size)
    feedforward_far = other(far_half(feedforward_low))
    lanes = jnp.arange(128, dtype=jnp.int32)[None, :]
    info = jnp.where(lanes == 5, square_column, info)
    grad_value, grad_state, grad_steps, channel_grad, state_grad, head_grad = mixer_backward(
        projected,
        mixer_widths,
        info,
        label_rows,
        channel,
        state_channel,
        head_rows,
        scanned,
        grad_gated_low,
        dt,
        cum,
    )
    grad_value, first_came, feedforward_far, second_came = tie(
        grad_value, first_came, feedforward_far, second_came
    )

    last_far, last_line, last_own = weight_grads(
        last_kernel,
        [normed_turned, grad_value, grad_state, grad_steps],
        model,
        width + state_width + 128,
        "last_grads",
    )
    last_far, second_came = tie(last_far, second_came)
    last_came = send_core(last_far, size)
    second_parts = add_line(second_came, second_own, size)
    last_came, grad_value, second_parts = tie(last_came, grad_value, second_parts)
    last_line, last_own = add_core(last_came, last_line, last_own)
    last_line, last_own, grad_value = tie(last_line, last_own, grad_value)
    last_came = send_line(last_line, size)
    second_came = send_ring(second_parts[1], size)
    normed_low = back_project(
        starts,
        gathering.pieces(0),
        second_pieces,
        [grad_gate, grad_value, grad_state, grad_steps, grad_query, grad_keyvalue],
    )
    normed_low, last_came, feed_came, feedforward_far, second_came = tie(
        normed_low, last_came, feed_came, feedforward_far, second_came
    )
    second_total = narrow(wide(second_parts[2]) + wide(second_came))
    second_came = send_ring(second_total, size)
    last_parts = add_line(last_came, last_own, size)
    last_sent = send_block(last_parts, size, 1)
    normed_far = other(far_half(normed_low))
    feed_total = add_blocks(feed_parts, feed_came)
    first_total = add_blocks(first_parts, first_came)
    spread = lambda part, total, start: lax.dynamic_update_slice_in_dim(
        jnp.zeros(part.shape[:-1] + (total,), jnp.float32), part, start, part.ndim - 1
    )
    block_output = (
        own_half(middle)
        + wide(own_half(feedforward_low))
        + wide(feedforward_far)
    )
    residual = wide(group_input)
    first_rms = inverse_rms(residual)
    first_normal = residual * first_rms
    input_gain_part = jnp.sum(wide(normed_low) * first_normal, 0)
    channel_parts = jnp.concatenate(
        [spread(channel_grad[:5], ssm_width, rank * width), state_grad[:5]], 1
    )
    skip_grad = jnp.sum(channel_grad[5].reshape(heads, repeat), 1)
    head_parts = spread(
        jnp.concatenate([head_grad[:2, :heads], skip_grad[None]], 0),
        timestep_bias.shape[0],
        rank * heads,
    )
    gain_parts = spread(channel_grad[6], ssm_width, rank * width)
    leader = (rank == 0).astype(jnp.float32)
    parts = [input_gain_part, middle_gain_part * leader, gain_parts, channel_parts, head_parts]
    flat = jnp.concatenate([part.reshape(-1) for part in parts])
    flat = jnp.pad(flat, (0, -flat.shape[0] % 1024)).reshape(-1, 128)

    flat_far = lax.ppermute(flat, "fsdp", swaps(size, 1))
    last_sent, flat_far, second_came = tie(last_sent, flat_far, second_came)
    second_total = narrow(wide(second_parts[3]) + wide(second_came))
    second_came = send_ring(second_total, size)
    last_total = wide(last_parts[0]) + wide(last_sent)
    last_sent = send_block(last_parts, size, 2)
    flat = flat + flat_far
    flat_far = lax.ppermute(flat, "fsdp", swaps(size, 2))
    last_sent, flat_far, second_came = tie(last_sent, flat_far, second_came)
    last_total = last_total + wide(last_sent)
    last_sent = send_block(last_parts, size, 3)
    flat = flat + flat_far
    lined = [
        lax.ppermute(flat, "fsdp", [(i, (i + 4 * k) % size) for i in range(size)])
        for k in range(1, depth)
    ]
    last_sent, *lined = tie(last_sent, *lined)
    last_total = last_total + wide(last_sent)
    placed = jnp.stack([flat] + lined)
    flat = sum(placed[(ring_at - k + depth) % depth] for k in range(depth))
    normed_far, flat, feed_total, first_total = tie(normed_far, flat, feed_total, first_total)
    second_total = wide(second_parts[0]) + wide(second_came)
    flat = (flat + other(flat)).reshape(-1)
    shared_at = width + attended_width + query_width
    shared = jnp.concatenate(
        [last_total[:, width : width + state_width], second_total[:, shared_at : shared_at + keyvalue_width]],
        1,
    )
    shared = shared + other(shared)
    normed_grad = wide(own_half(normed_low)) + wide(normed_far)
    own_normal = own_half(first_normal)
    first_scaled = normed_grad * input_gain
    input_grad = own_half(grad_middle) + own_half(first_rms) * (
        first_scaled - own_normal * jnp.mean(first_scaled * own_normal, -1, keepdims=True)
    )

    summed = []
    for part in parts:
        summed.append(flat[: part.size].reshape(part.shape))
        flat = flat[part.size :]
    inner_grad = jnp.stack(
        [second_total[:, second_width:], last_total[:, :width]], 1
    )
    return (
        block_output,
        input_grad,
        summed[0],
        inner_grad,
        last_total[:, width + state_width : width + state_width + heads],
        shared[:, :state_width],
        second_total[:, width + attended_width : shared_at],
        shared[:, state_width:],
        summed[3][:4],
        summed[3][4],
        summed[4][0],
        summed[4][1],
        summed[4][2],
        summed[2],
        second_total[:, :width].T,
        second_total[:, width : width + attended_width].T,
        summed[1],
        jnp.concatenate([first_total[:, hidden:], feed_total], 1).reshape(shard, 2, hidden),
        first_total[:, :hidden].T,
    )


def solution(mesh):
    fsdp, tp = mesh.shape["fsdp"], mesh.shape["tp"]

    def body(*operands):
        rows = operands[1].shape[0]
        if tp == 2 and fsdp == 16 and rows == 2 * BLOCK:
            return packed_body(fsdp, *operands)
        return general_body(*operands)

    return jax.shard_map(
        body,
        mesh=mesh,
        in_specs=(
            P(("fsdp", "tp"), None),
            P("fsdp"),
            P(("fsdp", "tp"), None),
            P(),
            P("fsdp", None, "tp"),
            P("fsdp", "tp"),
            P("fsdp", None),
            P("fsdp", "tp"),
            P("fsdp", None),
            P(),
            P(),
            P(),
            P(),
            P(),
            P(),
            P("tp", "fsdp"),
            P("tp", "fsdp"),
            P(),
            P("fsdp", None, "tp"),
            P("tp", "fsdp"),
        ),
        out_specs=(
            P(("fsdp", "tp"), None),
            P(("fsdp", "tp"), None),
            P(),
            P("fsdp", None, "tp"),
            P("fsdp", "tp"),
            P("fsdp", None),
            P("fsdp", "tp"),
            P("fsdp", None),
            P(),
            P(),
            P(),
            P(),
            P(),
            P(),
            P("tp", "fsdp"),
            P("tp", "fsdp"),
            P(),
            P("fsdp", None, "tp"),
            P("tp", "fsdp"),
        ),
        check_vma=False,
    )
```
